32 devices in a mesh: wide: 8 (over y, x, core), narrow: 4 (over z).
Axes of the slice: x: 2, y: 2, z: 4, core: 2. Of those that a mesh axis runs over, the one named last changes fastest.
Arguments:
- inputs: bfloat16 [10240, 768], P(('wide', 'narrow')), may hold values from -6 to 6
- pass_ids: int32 [8, 1280], P('wide'), may hold values from 0 to 4, as said below
- front_gain: bfloat16 [768], replicated, may hold values from 0.25 to 1.75
- front_shift: bfloat16 [768], replicated, may hold values from -3 to 3
- triple_weight: bfloat16 [3, 768, 768], P(None, None, 'narrow'), may hold values from -0.21875 to 0.21875
- triple_bias: bfloat16 [2, 768], P(None, 'narrow'), may hold values from -3 to 3
- mixer_weight: bfloat16 [768, 768], replicated, may hold values from -0.875 to 0.875
- mixer_bias: bfloat16 [768], replicated, may hold values from -3 to 3
- back_gain: bfloat16 [768], replicated, may hold values from 0.25 to 1.75
- back_shift: bfloat16 [768], replicated, may hold values from -3 to 3
- expand_weight: bfloat16 [768, 3072], replicated, may hold values from -0.21875 to 0.21875
- expand_bias: bfloat16 [3072], replicated, may hold values from -3 to 3
- reduce_weight: bfloat16 [3072, 768], replicated, may hold values from -0.109375 to 0.109375
- reduce_bias: bfloat16 [768], replicated, may hold values from -3 to 3
- pass_table: bfloat16 [5, 768], replicated, may hold values from -3 to 3
- cotangent: bfloat16 [10240, 768], P(('wide', 'narrow')), may hold values from -15 to 15
Outputs:
- layer_out: bfloat16 [10240, 768], P(('wide', 'narrow'))
- grad_inputs: bfloat16 [10240, 768], P(('wide', 'narrow'))
- grad_front_gain: float32 [768], replicated
- grad_front_shift: float32 [768], replicated
- grad_triple_weight: float32 [3, 768, 768], P(None, None, 'narrow')
- grad_triple_bias: float32 [2, 768], P(None, 'narrow')
- grad_mixer_weight: float32 [768, 768], P('wide', 'narrow')
- grad_mixer_bias: float32 [768], replicated
- grad_back_gain: float32 [768], replicated
- grad_back_shift: float32 [768], replicated
- grad_expand_weight: float32 [768, 3072], P('wide', 'narrow')
- grad_expand_bias: float32 [3072], replicated
- grad_reduce_weight: float32 [3072, 768], P('wide', 'narrow')
- grad_reduce_bias: float32 [768], replicated
- grad_pass_table: float32 [5, 768], replicated
The draws below stay inside these ranges and needn't reach their ends.
Inputs may be any that keep to these rules, and one draw needn't show every extreme that they name: `pass_ids`: in each sequence the first 5 rows are passes 0 to 4 of its first token; every later row has pass 0 or one more than the row before it.
All inputs are finite; a program needn't handle non-finite values.
Results may differ from the reference program's by a relative error of at most 0.013.
Values may be sent and summed in bfloat16 or wider, within the bound.
No kernel may reach another device: no remote copies, remote signals or barrier semaphores. Data moves between devices by JAX's collectives and lax.ppermute only.
A program may use at most 128 MiB of HBM per device.

```python
import jax
import jax.numpy as jnp
from jax import lax

D = 768
HEADS = 12
HEAD_DIM = 64
FF = 3072
PASSES = 5
ROWS_SEQ = 1280
SEQS = 8
ROWS = 10240


def draw_pass_ids(key, part):
    key = jax.random.fold_in(key, 11)
    picks = jax.random.randint(key, (ROWS_SEQ, SEQS), 0, 5)
    starts = picks < 2
    places = jnp.arange(ROWS_SEQ, dtype=jnp.int32)[:, None]
    starts = jnp.where(places < PASSES, places == 0, starts)

    def advance(previous, start_now):
        following = jnp.where(start_now | (previous >= PASSES - 1), 0, previous + 1).astype(jnp.int32)
        return (following, following)
    _, passes = lax.scan(advance, jnp.zeros((SEQS,), jnp.int32), starts)
    return passes.T.astype(jnp.int32)


def draw_cotangent(key, part):
    key = jax.random.fold_in(key, 23)
    first, second = jax.random.split(key, 2)
    rising = 3.0 ** (jnp.arange(ROWS, dtype=jnp.float32) / ROWS)
    row_scale = jnp.exp(jax.random.uniform(second, (ROWS, 1), minval=-0.69, maxval=0.69))
    base = jax.random.normal(first, (ROWS, D))
    base = jnp.clip(base, -5.0, 5.0)
    return (0.45 * base * rising[:, None] * row_scale).astype(jnp.float32).astype(jnp.bfloat16)


def block_scale(stream_key, shape, pieces, smallest, top_value):
    gain, own = 1.0, jax.random.fold_in(stream_key, 6)
    for dim, parts in pieces:
        heights = jnp.exp(jax.random.uniform(jax.random.fold_in(own, dim), (parts,), jnp.float32, smallest / len(pieces), top_value / len(pieces)))
        gain = gain * jnp.repeat(heights, shape[dim] // parts).reshape([-1 if axis == dim else 1 for axis in range(len(shape))])
    return gain


def gaussian(rng, dims, width, reach, pieces=(), held_as=jnp.bfloat16):
    loudness = block_scale(rng, dims, pieces, -0.22, 0.18) if pieces else 1.0
    entries = jax.random.normal(rng, dims, jnp.float32) * width * loudness
    return jnp.minimum(jnp.maximum(entries, -reach), reach).astype(held_as)


def setup_inputs(seed: int = 0) -> dict:
    key_of = jax.random.split(jax.random.key(seed), 17)
    return {
        "inputs": gaussian(key_of[0], (ROWS, D), 1.0, 6.0, ((0, 32),)),
        "pass_ids": draw_pass_ids(jax.random.fold_in(key_of[16], 71), 0),
        "front_gain": jnp.clip(1.0 + 0.15 * jax.random.normal(key_of[2], (D,), jnp.float32), 0.25, 1.75).astype(jnp.bfloat16),
        "front_shift": gaussian(key_of[3], (D,), 0.3, 3.0),
        "triple_weight": gaussian(key_of[4], (3, D, D), D ** -0.5, 0.21875, ((2, 4),)),
        "triple_bias": gaussian(key_of[5], (2, D), 0.5, 3.0, ((1, 4),)),
        "mixer_weight": gaussian(key_of[6], (D, D), (D // 16) ** -0.5, 0.875),
        "mixer_bias": gaussian(key_of[7], (D,), 0.3, 3.0),
        "back_gain": jnp.clip(1.0 + 0.15 * jax.random.normal(key_of[8], (D,), jnp.float32), 0.25, 1.75).astype(jnp.bfloat16),
        "back_shift": gaussian(key_of[9], (D,), 0.3, 3.0),
        "expand_weight": gaussian(key_of[10], (D, FF), D ** -0.5, 0.21875),
        "expand_bias": gaussian(key_of[11], (FF,), 0.5, 3.0),
        "reduce_weight": gaussian(key_of[12], (FF, D), FF ** -0.5, 0.109375),
        "reduce_bias": gaussian(key_of[13], (D,), 0.3, 3.0),
        "pass_table": gaussian(key_of[14], (PASSES, D), 0.5, 3.0),
        "cotangent": draw_cotangent(jax.random.fold_in(key_of[16], 71), 0),
    }


@jax.custom_vjp
def low(v):
    return lax.optimization_barrier(v.astype(jnp.bfloat16)).astype(jnp.float32)

@jax.custom_vjp
def low_back(v):
    return v

def low_keep(v):
    return (low(v), None)

def low_pass(kept, grad):
    return (grad,)

def back_keep(v):
    return (v, None)

def back_low(kept, grad):
    return (low(grad),)
low.defvjp(low_keep, low_pass)
low_back.defvjp(back_keep, back_low)
epsilon = 1e-05

def matmul(left, right):
    return jnp.dot(left, right, precision=lax.Precision.HIGHEST, preferred_element_type=jnp.float32)

def layer_norm(values, weight_gain, weight_shift):
    row_mean = lax.optimization_barrier(jnp.mean(values, axis=-1, keepdims=True))
    centred = values - row_mean
    inv_scale = lax.rsqrt(lax.optimization_barrier(jnp.mean(centred * centred, axis=-1, keepdims=True)) + epsilon)
    return centred * inv_scale * weight_gain + weight_shift

def visible(seq_ids):
    positions = (jnp.cumsum((seq_ids == 0).astype(jnp.int32)) - 1).astype(jnp.int32)
    return (positions[None, :] <= positions[:, None]) & (seq_ids[None, :] <= seq_ids[:, None])

def attend(queries, key_rows, value_rows, seq_ids):
    row_count = queries.shape[0]
    query_heads = queries.reshape(row_count, HEADS, HEAD_DIM)
    key_heads = key_rows.reshape(row_count, HEADS, HEAD_DIM)
    value_heads = value_rows.reshape(row_count, HEADS, HEAD_DIM)
    scores = jnp.einsum('qhe,khe->hqk', query_heads, key_heads, precision=lax.Precision.HIGHEST) * HEAD_DIM ** (-0.5)
    scores = low_back(scores)
    scores = jnp.where(visible(seq_ids)[None], scores, -1e+30)
    row_top = lax.optimization_barrier(jnp.max(scores, axis=-1, keepdims=True))
    exp_scores = jnp.exp(scores - row_top)
    probs = low(exp_scores / lax.optimization_barrier(jnp.sum(exp_scores, axis=-1, keepdims=True)))
    mixed = jnp.einsum('hqk,khe->qhe', probs, value_heads, precision=lax.Precision.HIGHEST)
    return mixed.reshape(row_count, HEADS * HEAD_DIM)

def forward(seq_rows, front_gain, front_shift, triple_weight, triple_bias, mixer_weight, mixer_bias, back_gain, back_shift, expand_weight, expand_bias, reduce_weight, reduce_bias, pass_table, seq_ids):
    normed = low(layer_norm(seq_rows, front_gain, front_shift))
    queries = low(low_back(matmul(normed, triple_weight[0]) + triple_bias[0]))
    key_rows = low(low_back(matmul(normed, triple_weight[1])))
    value_rows = low(low_back(matmul(normed, triple_weight[2]) + triple_bias[1]))
    mixed_rows = low(low_back(attend(queries, key_rows, value_rows, seq_ids)))
    branch = low_back(matmul(mixed_rows, mixer_weight) + mixer_bias)
    middle = seq_rows + branch
    normed_two = low(layer_norm(middle, back_gain, back_shift))
    hidden = low_back(matmul(normed_two, expand_weight) + expand_bias)
    active = low(jax.nn.gelu(hidden))
    second = low_back(matmul(active, reduce_weight) + reduce_bias)
    onehot = (seq_ids[:, None] == jnp.arange(PASSES, dtype=jnp.int32)[None, :]).astype(jnp.float32)
    return middle + second + matmul(onehot, pass_table)

def reference(inputs, pass_ids, front_gain, front_shift, triple_weight, triple_bias, mixer_weight, mixer_bias, back_gain, back_shift, expand_weight, expand_bias, reduce_weight, reduce_bias, pass_table, cotangent):
    params = tuple((w.astype(jnp.float32) for w in (front_gain, front_shift, triple_weight, triple_bias, mixer_weight, mixer_bias, back_gain, back_shift, expand_weight, expand_bias, reduce_weight, reduce_bias, pass_table)))
    rows_in = inputs.astype(jnp.float32).reshape(SEQS, ROWS_SEQ, D)
    grads_in = cotangent.astype(jnp.float32).reshape(SEQS, ROWS_SEQ, D)

    def per_sequence(running, arrays):
        seq_rows, seq_ids, seq_grads = arrays

        def forward_one(rows_here, *weights):
            return forward(rows_here, *weights, seq_ids)
        result, pullback = jax.vjp(forward_one, seq_rows, *params)
        grads = pullback(seq_grads)
        running = tuple((acc + new for acc, new in zip(running, grads[1:])))
        return (running, (result.astype(jnp.bfloat16), grads[0].astype(jnp.bfloat16)))
    zero_grads = tuple((jnp.zeros_like(w) for w in params))
    totals, (outs, back_rows) = lax.scan(per_sequence, zero_grads, (rows_in, pass_ids, grads_in))
    return (outs.reshape(ROWS, D), back_rows.reshape(ROWS, D), totals[0], totals[1], totals[2], totals[3], totals[4], totals[5], totals[6], totals[7], totals[8], totals[9], totals[10], totals[11], totals[12])
```

```python
import functools
import math

import jax
import jax.numpy as jnp
from jax import lax
from jax.experimental import pallas as pl
from jax.experimental.pallas import tpu as pltpu
from jax.sharding import PartitionSpec as P

HEAD_DIM = 64
EPSILON = 1e-05
BLOCK = 256
HIDDEN = -1e30
F32 = jnp.float32
BF16 = jnp.bfloat16
VMEM_LIMIT = 60 * 1024 * 1024
NN = (((1,), (0,)), ((), ()))
NT = (((1,), (1,)), ((), ()))
TN = (((0,), (0,)), ((), ()))
GELU_A = math.sqrt(2.0 / math.pi)
GELU_B = 0.044715


def dot(left, right, dims=NN):
    return lax.dot_general(left, right, dims, preferred_element_type=F32)


def whole():
    return pl.BlockSpec(memory_space=pltpu.VMEM)


def params(**more):
    return pltpu.CompilerParams(vmem_limit_bytes=VMEM_LIMIT, **more)


def unit_rows(values):
    centred = values - jnp.mean(values, axis=-1, keepdims=True)
    scale = lax.rsqrt(jnp.mean(centred * centred, axis=-1, keepdims=True) + EPSILON)
    return centred * scale, scale


def norm_pullback(grad_out, unit, scale, gain):
    grad_unit = grad_out * gain
    inner = (
        grad_unit
        - jnp.mean(grad_unit, axis=-1, keepdims=True)
        - unit * jnp.mean(grad_unit * unit, axis=-1, keepdims=True)
    )
    return inner * scale


def keep_head(block, head, axis):
    place = lax.broadcasted_iota(jnp.int32, block.shape, axis) // HEAD_DIM
    return jnp.where(place == head, block, jnp.zeros_like(block))


def visibility(ids_col_ref, ids_row_ref, start, keys):
    seen = ids_col_ref[0:keys, :] <= ids_row_ref[:, start : start + BLOCK]
    key_place = lax.broadcasted_iota(jnp.int32, (keys, BLOCK), 0)
    query_place = lax.broadcasted_iota(jnp.int32, (keys, BLOCK), 1) + start
    return jnp.where(seen & (key_place <= query_place), 0.0, HIDDEN).astype(F32)


def attend_forward_kernel(
    x_ref, ids_row_ref, ids_col_ref, gain_ref, shift_ref, weight_ref, bias_ref,
    mixed_ref, mixed_t_ref, lse_ref, normed_ref, q_ref, k_ref, v_ref, q_t_ref, k_t_ref,
    v_t_ref, bias_t_ref,
):
    rows = x_ref.shape[0]
    heads = weight_ref.shape[2] // HEAD_DIM
    gain = gain_ref[...].astype(F32)
    shift = shift_ref[...].astype(F32)

    def project(step, carry):
        here = pl.ds(pl.multiple_of(step * BLOCK, BLOCK), BLOCK)
        unit, _ = unit_rows(x_ref[here, :].astype(F32))
        normed = (unit * gain + shift).astype(BF16)
        normed_ref[here, :] = normed
        q = (dot(normed, weight_ref[0]) + bias_ref[0:1, :].astype(F32)).astype(BF16)
        q = q * jnp.asarray(HEAD_DIM**-0.5, BF16)
        k = dot(normed, weight_ref[1]).astype(BF16)
        v = (dot(normed, weight_ref[2]) + bias_ref[1:2, :].astype(F32)).astype(BF16)
        q_ref[here, :] = q
        k_ref[here, :] = k
        v_ref[here, :] = v
        q_t_ref[:, here] = q.T
        k_t_ref[:, here] = k.T
        v_t_ref[:, here] = v.T
        return carry

    lax.fori_loop(0, rows // BLOCK, project, 0)

    for start in range(0, rows, BLOCK):
        keys = start + BLOCK
        bias_t_ref[0:keys, :] = visibility(ids_col_ref, ids_row_ref, start, keys)
        for head in range(heads):
            here = slice(head * HEAD_DIM, (head + 1) * HEAD_DIM)
            q_t = keep_head(q_t_ref[:, start : start + BLOCK], head, 0)
            scores = dot(k_ref[0:keys, :], q_t) + bias_t_ref[0:keys, :]
            top = jnp.max(scores, axis=0, keepdims=True)
            weights = jnp.exp(scores - top)
            total = jnp.sum(weights, axis=0, keepdims=True)
            mixed_t = dot(v_t_ref[here, 0:keys], weights.astype(BF16)) / total
            mixed_t_ref[here, start : start + BLOCK] = mixed_t
            lse_ref[head : head + 1, start : start + BLOCK] = top + jnp.log(total)
        mixed_ref[start : start + BLOCK, :] = mixed_t_ref[:, start : start + BLOCK].T.astype(BF16)


def attend_forward(x_all, ids, gain, shift, weight, bias):
    rows, width = x_all.shape
    part = weight.shape[2]
    heads = part // HEAD_DIM
    shape = jax.ShapeDtypeStruct
    return pl.pallas_call(
        attend_forward_kernel,
        out_shape=(
            shape((rows, part), BF16),
            shape((part, rows), F32),
            shape((heads, rows), F32),
            shape((rows, width), BF16),
            shape((rows, part), BF16),
            shape((rows, part), BF16),
            shape((rows, part), BF16),
            shape((part, rows), BF16),
            shape((part, rows), BF16),
        ),
        in_specs=[whole()] * 7,
        out_specs=(whole(),) * 9,
        scratch_shapes=[pltpu.VMEM((part, rows), BF16), pltpu.VMEM((rows, BLOCK), F32)],
        compiler_params=params(),
        name="attend_forward",
    )(x_all, ids.reshape(1, rows), ids.reshape(rows, 1), gain, shift, weight, bias)


def attend_backward_kernel(
    grad_ref, q_ref, k_ref, v_ref, q_t_ref, k_t_ref, mixed_t_ref, lse_ref,
    ids_row_ref, ids_col_ref, weight_ref,
    grad_triple_ref, grad_normed_ref,
    grad_t_ref, delta_ref, grad_q_t_ref, grad_k_ref, grad_v_ref, bias_t_ref,
):
    rows, part = q_ref.shape
    heads = part // HEAD_DIM
    for start in range(0, rows, BLOCK):
        cols = slice(start, start + BLOCK)
        grad_t = grad_ref[cols, :].T
        grad_t_ref[:, cols] = grad_t
        product = grad_t.astype(F32) * mixed_t_ref[:, cols]
        for head in range(heads):
            delta_ref[head : head + 1, cols] = jnp.sum(
                product[head * HEAD_DIM : (head + 1) * HEAD_DIM, :], axis=0, keepdims=True
            )
    grad_k_ref[...] = jnp.zeros_like(grad_k_ref)
    grad_v_ref[...] = jnp.zeros_like(grad_v_ref)
    for start in range(0, rows, BLOCK):
        keys = start + BLOCK
        cols = slice(start, start + BLOCK)
        bias_t_ref[0:keys, :] = visibility(ids_col_ref, ids_row_ref, start, keys)
        for head in range(heads):
            here = slice(head * HEAD_DIM, (head + 1) * HEAD_DIM)
            scores = dot(k_ref[0:keys, :], keep_head(q_t_ref[:, cols], head, 0))
            probs = jnp.exp(scores + bias_t_ref[0:keys, :] - lse_ref[head : head + 1, cols])
            grad_probs = dot(v_ref[0:keys, :], keep_head(grad_t_ref[:, cols], head, 0))
            grad_scores = (probs * (grad_probs - delta_ref[head : head + 1, cols])).astype(BF16)
            grad_v_ref[0:keys, :] += dot(probs.astype(BF16), keep_head(grad_ref[cols, :], head, 1))
            grad_k_ref[0:keys, :] += dot(grad_scores, keep_head(q_ref[cols, :], head, 1))
            grad_q_t_ref[here, cols] = dot(k_t_ref[here, 0:keys], grad_scores)
    factor = HEAD_DIM**-0.5
    for start in range(0, rows, BLOCK):
        cols = slice(start, start + BLOCK)
        grad_q = (grad_q_t_ref[:, cols].T * factor).astype(BF16)
        grad_k = grad_k_ref[cols, :].astype(BF16)
        grad_v = grad_v_ref[cols, :].astype(BF16)
        grad_triple_ref[0, cols, :] = grad_q
        grad_triple_ref[1, cols, :] = grad_k
        grad_triple_ref[2, cols, :] = grad_v
        grad_normed_ref[cols, :] = (
            dot(grad_q, weight_ref[0], NT)
            + dot(grad_k, weight_ref[1], NT)
            + dot(grad_v, weight_ref[2], NT)
        ).astype(BF16)


def attend_backward(grad, q, k, v, q_t, k_t, mixed_t, lse, ids, weight):
    rows, part = q.shape
    heads = part // HEAD_DIM
    shape = jax.ShapeDtypeStruct
    return pl.pallas_call(
        attend_backward_kernel,
        out_shape=(shape((3, rows, part), BF16), shape((rows, weight.shape[1]), BF16)),
        in_specs=[whole()] * 11,
        out_specs=(whole(),) * 2,
        scratch_shapes=[
            pltpu.VMEM((part, rows), BF16),
            pltpu.VMEM((heads, rows), F32),
            pltpu.VMEM((part, rows), F32),
            pltpu.VMEM((rows, part), F32),
            pltpu.VMEM((rows, part), F32),
            pltpu.VMEM((rows, BLOCK), F32),
        ],
        compiler_params=params(),
        name="attend_backward",
    )(grad, q, k, v, q_t, k_t, mixed_t, lse, ids.reshape(1, rows), ids.reshape(rows, 1), weight)


def middle_kernel(
    mixed_ref, x_ref, cot_ref, ids_ref, mixer_ref, mixer_bias_ref, gain_ref, shift_ref,
    expand_ref, expand_bias_ref, reduce_ref, reduce_bias_ref, table_ref,
    out_ref, active_ref, grad_hidden_ref, normed_ref, grad_middle_ref, grad_low_ref,
    grad_mixed_ref, sums_ref,
    unit_ref, scale_ref, total_ref, grad_normed_ref,
):
    step = pl.program_id(0)
    last = pl.num_programs(0) - 1
    groups, rows, part = mixed_ref.shape
    passes = table_ref.shape[0]

    @pl.when(step == 0)
    def _():
        branch = jnp.zeros((rows, x_ref.shape[1]), F32)
        for group in range(groups):
            branch += dot(mixed_ref[group], mixer_ref[group * part : (group + 1) * part, :])
        middle = x_ref[...].astype(F32) + (branch + mixer_bias_ref[...].astype(F32))
        unit, scale = unit_rows(middle)
        normed_ref[...] = (unit * gain_ref[...].astype(F32) + shift_ref[...].astype(F32)).astype(BF16)
        unit_ref[...] = unit
        scale_ref[...] = jnp.broadcast_to(scale, scale_ref.shape)
        total_ref[...] = middle + reduce_bias_ref[...].astype(F32)
        grad_normed_ref[...] = jnp.zeros_like(grad_normed_ref)
        sums_ref[...] = jnp.zeros_like(sums_ref)

    expand = expand_ref[...]
    reduce = reduce_ref[...]
    hidden = dot(normed_ref[...], expand) + expand_bias_ref[...].astype(F32)
    square = hidden * hidden
    bend = jnp.tanh(GELU_A * hidden * (1.0 + GELU_B * square))
    half = 0.5 * (1.0 + bend)
    active = (hidden * half).astype(BF16)
    active_ref[...] = active
    total_ref[...] += dot(active, reduce)
    slope = half + (0.5 * GELU_A) * hidden * (1.0 - bend * bend) * (1.0 + (3.0 * GELU_B) * square)
    grad_hidden = (dot(cot_ref[...], reduce, NT) * slope).astype(BF16)
    grad_hidden_ref[...] = grad_hidden
    sums_ref[pl.ds(9 + step, 1), :] = jnp.sum(grad_hidden.astype(F32), axis=0, keepdims=True)
    grad_normed_ref[...] += dot(grad_hidden, expand, NT)

    @pl.when(step == last)
    def _():
        cot = cot_ref[...].astype(F32)
        embedded = jnp.zeros_like(cot)
        for index in range(passes):
            chosen = ids_ref[...] == index
            embedded += jnp.where(chosen, table_ref[index : index + 1, :].astype(F32), 0.0)
            sums_ref[index : index + 1, :] = jnp.sum(
                jnp.where(chosen, cot, 0.0), axis=0, keepdims=True
            )
        out_ref[...] = (total_ref[...] + embedded).astype(BF16)
        unit = unit_ref[...]
        grad_normed = grad_normed_ref[...]
        back = norm_pullback(grad_normed, unit, scale_ref[:, 0:1], gain_ref[...].astype(F32))
        grad_middle = cot + back
        grad_middle_ref[...] = grad_middle
        grad_low = grad_middle.astype(BF16)
        grad_low_ref[...] = grad_low
        sums_ref[5:6, :] = jnp.sum(cot, axis=0, keepdims=True)
        sums_ref[6:7, :] = jnp.sum(grad_low.astype(F32), axis=0, keepdims=True)
        sums_ref[7:8, :] = jnp.sum(grad_normed * unit, axis=0, keepdims=True)
        sums_ref[8:9, :] = jnp.sum(grad_normed, axis=0, keepdims=True)
        for group in range(groups):
            grad_mixed_ref[group] = dot(
                grad_low, mixer_ref[group * part : (group + 1) * part, :], NT
            ).astype(BF16)


def middle_part(mixed, x, cot, ids, mixer, mixer_bias, gain, shift, expand, expand_bias, reduce, reduce_bias, table):
    groups, rows, part = mixed.shape
    width, hidden = expand.shape
    chunk = width
    steps = hidden // chunk
    shape = jax.ShapeDtypeStruct

    def fixed(array):
        return pl.BlockSpec(array.shape, lambda i, n=array.ndim: (0,) * n)

    def fixed_out(dims):
        return pl.BlockSpec(dims, lambda i, n=len(dims): (0,) * n)

    return pl.pallas_call(
        middle_kernel,
        grid=(steps,),
        out_shape=(
            shape((rows, width), BF16),
            shape((rows, hidden), BF16),
            shape((rows, hidden), BF16),
            shape((rows, width), BF16),
            shape((rows, width), F32),
            shape((rows, width), BF16),
            shape((groups, rows, part), BF16),
            shape((16, width), F32),
        ),
        in_specs=[
            fixed(mixed), fixed(x), fixed(cot), fixed(ids), fixed(mixer), fixed(mixer_bias), fixed(gain), fixed(shift),
            pl.BlockSpec((width, chunk), lambda i: (0, i)),
            pl.BlockSpec((1, chunk), lambda i: (0, i)),
            pl.BlockSpec((chunk, width), lambda i: (i, 0)),
            fixed(reduce_bias), fixed(table),
        ],
        out_specs=(
            fixed_out((rows, width)),
            pl.BlockSpec((rows, chunk), lambda i: (0, i)),
            pl.BlockSpec((rows, chunk), lambda i: (0, i)),
            fixed_out((rows, width)),
            fixed_out((rows, width)),
            fixed_out((rows, width)),
            fixed_out((groups, rows, part)),
            fixed_out((16, width)),
        ),
        scratch_shapes=[
            pltpu.VMEM((rows, width), F32),
            pltpu.VMEM((rows, 128), F32),
            pltpu.VMEM((rows, width), F32),
            pltpu.VMEM((rows, width), F32),
        ],
        compiler_params=params(dimension_semantics=("arbitrary",)),
        name="middle_part",
    )(mixed, x, cot, ids, mixer, mixer_bias, gain, shift, expand, expand_bias, reduce, reduce_bias, table)


def weight_grads_kernel(mixed_ref, grad_low_ref, normed_ref, cot_ref, active_ref, grad_hidden_ref, mixer_ref, expand_ref, reduce_ref):
    step = pl.program_id(0)
    groups, rows, part = mixed_ref.shape

    @pl.when(step == 0)
    def _():
        for group in range(groups):
            mixer_ref[group * part : (group + 1) * part, :] = dot(
                mixed_ref[group], grad_low_ref[...], TN
            ).astype(BF16)

    expand_ref[...] = dot(normed_ref[...], grad_hidden_ref[...], TN).astype(BF16)
    reduce_ref[...] = dot(active_ref[...], cot_ref[...], TN).astype(BF16)


def weight_grads(mixed, grad_low, normed, cot, active, grad_hidden):
    groups, rows, part = mixed.shape
    width = normed.shape[1]
    hidden = active.shape[1]
    chunk = width
    shape = jax.ShapeDtypeStruct

    def fixed(array):
        return pl.BlockSpec(array.shape, lambda i, n=array.ndim: (0,) * n)

    return pl.pallas_call(
        weight_grads_kernel,
        grid=(hidden // chunk,),
        out_shape=(shape((width, width), BF16), shape((width, hidden), BF16), shape((hidden, width), BF16)),
        in_specs=[
            fixed(mixed), fixed(grad_low), fixed(normed), fixed(cot),
            pl.BlockSpec((rows, chunk), lambda i: (0, i)),
            pl.BlockSpec((rows, chunk), lambda i: (0, i)),
        ],
        out_specs=(
            pl.BlockSpec((width, width), lambda i: (0, 0)),
            pl.BlockSpec((width, chunk), lambda i: (0, i)),
            pl.BlockSpec((chunk, width), lambda i: (i, 0)),
        ),
        compiler_params=params(dimension_semantics=("arbitrary",)),
        name="weight_grads",
    )(mixed, grad_low, normed, cot, active, grad_hidden)


def triple_grads_kernel(x_ref, normed_ref, grad_triple_ref, grad_normed_ref, weight_ref, bias_ref, sums_ref):
    unit, _ = unit_rows(x_ref[...].astype(F32))
    grad_normed = grad_normed_ref[...].astype(F32)
    sums_ref[0:1, :] = jnp.sum(grad_normed * unit, axis=0, keepdims=True)
    sums_ref[1:2, :] = jnp.sum(grad_normed, axis=0, keepdims=True)
    for index in range(3):
        weight_ref[index] = dot(normed_ref[...], grad_triple_ref[index], TN).astype(BF16)
    bias_ref[0:1, :] = jnp.sum(grad_triple_ref[0].astype(F32), axis=0, keepdims=True)
    bias_ref[1:2, :] = jnp.sum(grad_triple_ref[2].astype(F32), axis=0, keepdims=True)


def triple_grads(x_all, normed, grad_triple, grad_normed):
    rows, width = x_all.shape
    part = grad_triple.shape[2]
    shape = jax.ShapeDtypeStruct
    return pl.pallas_call(
        triple_grads_kernel,
        out_shape=(shape((3, width, part), BF16), shape((2, part), F32), shape((2, width), F32)),
        in_specs=[whole()] * 4,
        out_specs=(whole(),) * 3,
        compiler_params=params(),
        name="triple_grads",
    )(x_all, normed, grad_triple, grad_normed)


def front_kernel(x_ref, grad_normed_ref, grad_middle_ref, gain_ref, out_ref):
    unit, scale = unit_rows(x_ref[...].astype(F32))
    back = norm_pullback(grad_normed_ref[...].astype(F32), unit, scale, gain_ref[...].astype(F32))
    out_ref[...] = (grad_middle_ref[...] + back).astype(BF16)


def front_part(x, grad_normed, grad_middle, gain):
    return pl.pallas_call(
        front_kernel,
        out_shape=jax.ShapeDtypeStruct(x.shape, BF16),
        in_specs=[whole()] * 4,
        out_specs=whole(),
        compiler_params=params(),
        name="front_part",
    )(x, grad_normed, grad_middle, gain)


def body(
    inputs,
    pass_ids,
    front_gain,
    front_shift,
    triple_weight,
    triple_bias,
    mixer_weight,
    mixer_bias,
    back_gain,
    back_shift,
    expand_weight,
    expand_bias,
    reduce_weight,
    reduce_bias,
    pass_table,
    cotangent,
):
    local_rows, width = inputs.shape
    seq_rows = pass_ids.shape[1]
    part = triple_weight.shape[2]
    groups = seq_rows // local_rows
    ids = pass_ids.reshape(seq_rows)
    own_ids = lax.dynamic_slice_in_dim(ids, lax.axis_index("narrow") * local_rows, local_rows)

    def row(vector):
        return vector.reshape(1, -1)

    x_all = lax.all_gather(inputs, "narrow", axis=0, tiled=True)
    mixed, mixed_t, lse, normed, q, k, v, q_t, k_t = attend_forward(
        x_all, ids, row(front_gain), row(front_shift), triple_weight, triple_bias
    )
    mixed_rows = lax.all_to_all(
        mixed.reshape(groups, local_rows, part), "narrow", split_axis=0, concat_axis=0, tiled=True
    )
    layer_out, active, grad_hidden, normed_two, grad_middle, grad_low, grad_mixed, sums = middle_part(
        mixed_rows, inputs, cotangent, own_ids.reshape(local_rows, 1), mixer_weight, row(mixer_bias),
        row(back_gain), row(back_shift), expand_weight, row(expand_bias), reduce_weight, row(reduce_bias), pass_table,
    )
    grad_heads = lax.all_to_all(grad_mixed, "narrow", split_axis=0, concat_axis=0, tiled=True)
    grad_mixer, grad_expand, grad_reduce = weight_grads(
        mixed_rows, grad_low, normed_two, cotangent, active, grad_hidden
    )
    grad_triple_rows, grad_normed_part = attend_backward(
        grad_heads.reshape(seq_rows, part), q, k, v, q_t, k_t, mixed_t, lse, ids, triple_weight
    )
    grad_normed = lax.psum_scatter(grad_normed_part, "narrow", scatter_dimension=0, tiled=True)
    term_weight, term_bias, front_sums = triple_grads(x_all, normed, grad_triple_rows, grad_normed_part)
    grad_inputs = front_part(inputs, grad_normed, grad_middle, row(front_gain))
    grad_triple = lax.psum(term_weight, "wide").astype(F32)

    def scatter(array):
        array = lax.psum_scatter(array, "wide", scatter_dimension=0, tiled=True)
        return lax.psum_scatter(array, "narrow", scatter_dimension=1, tiled=True).astype(F32)

    total_mixer, total_expand, total_reduce = scatter(grad_mixer), scatter(grad_expand), scatter(grad_reduce)
    grad_triple_bias = lax.psum(term_bias, "wide")
    sums, front_sums = lax.psum((sums, front_sums), ("wide", "narrow"))
    passes = pass_table.shape[0]
    return (
        layer_out,
        grad_inputs,
        front_sums[0],
        front_sums[1],
        grad_triple,
        grad_triple_bias,
        total_mixer,
        sums[6],
        sums[7],
        sums[8],
        total_expand,
        sums[9:13].reshape(-1),
        total_reduce,
        sums[5],
        sums[0:passes],
    )


def solution(mesh):
    rows = P(("wide", "narrow"), None)
    block = P("wide", "narrow")
    return jax.shard_map(
        body,
        mesh=mesh,
        in_specs=(
            rows, P("wide", None), P(), P(), P(None, None, "narrow"), P(None, "narrow"),
            P(), P(), P(), P(), P(), P(), P(), P(), P(), rows,
        ),
        out_specs=(
            rows, rows, P(), P(), P(None, None, "narrow"), P(None, "narrow"), block,
            P(), P(), P(), block, P(), block, P(), P(),
        ),
        check_vma=False,
    )
```

```python
import math

import jax
import jax.numpy as jnp
from jax import lax
from jax.experimental import pallas as pl
from jax.experimental.pallas import tpu as pltpu
from jax.sharding import PartitionSpec as P


HEAD_DIM = 64
EPSILON = 1e-05
BLOCK = 256
HIDDEN = -1e30
F32 = jnp.float32
BF16 = jnp.bfloat16
VMEM_LIMIT = 60 * 1024 * 1024
AXES = ("wide", "narrow")
NN = (((1,), (0,)), ((), ()))
NT = (((1,), (1,)), ((), ()))
TN = (((0,), (0,)), ((), ()))
GELU_A = math.sqrt(2.0 / math.pi)
GELU_B = 0.044715
shape = jax.ShapeDtypeStruct


def dot(left, right, dims=NN):
    return lax.dot_general(left, right, dims, preferred_element_type=F32)


def whole():
    return pl.BlockSpec(memory_space=pltpu.VMEM)


def scalars():
    return pl.BlockSpec(memory_space=pltpu.SMEM)


def call(kernel, outs, *arrays, scratch=(), flops=0, name=None):
    size = sum(a.size * a.dtype.itemsize for a in (*arrays, *outs))
    return pl.pallas_call(
        kernel,
        out_shape=tuple(outs),
        in_specs=[scalars()] + [whole()] * (len(arrays) - 1),
        out_specs=(whole(),) * len(outs),
        scratch_shapes=list(scratch),
        compiler_params=pltpu.CompilerParams(vmem_limit_bytes=VMEM_LIMIT),
        cost_estimate=pl.CostEstimate(flops=flops, bytes_accessed=size, transcendentals=0),
        name=name,
    )(*arrays)


def unit_rows(values):
    centred = values - jnp.mean(values, axis=-1, keepdims=True)
    scale = lax.rsqrt(jnp.mean(centred * centred, axis=-1, keepdims=True) + EPSILON)
    return centred * scale, scale


def norm_pullback(grad_out, unit, scale, gain):
    grad_unit = grad_out * gain
    inner = (
        grad_unit
        - jnp.mean(grad_unit, axis=-1, keepdims=True)
        - unit * jnp.mean(grad_unit * unit, axis=-1, keepdims=True)
    )
    return inner * scale


def column_sum(values):
    return jnp.sum(values, axis=0, keepdims=True)


def keep_head(block, head, axis):
    place = lax.broadcasted_iota(jnp.int32, block.shape, axis) // HEAD_DIM
    return jnp.where(place == head, block, jnp.zeros_like(block))


def rows_at(index, count):
    return pl.ds(pl.multiple_of(index * count, math.gcd(count, 64)), count)


def visibility(ids_col_ref, ids_row_ref, start, keys):
    seen = ids_col_ref[0:keys, :] <= ids_row_ref[:, start : start + BLOCK]
    key_place = lax.broadcasted_iota(jnp.int32, (keys, BLOCK), 0)
    query_place = lax.broadcasted_iota(jnp.int32, (keys, BLOCK), 1) + start
    return jnp.where(seen & (key_place <= query_place), 0.0, HIDDEN).astype(F32)


def attend_forward_kernel(
    place_ref, x0_ref, x1_ref, x2_ref, x3_ref, ids_row_ref, ids_col_ref, gain_ref, shift_ref, packed_ref,
    m0_ref, m1_ref, m2_ref, m3_ref, mixed_t_ref, lse_ref, normed_ref, q_ref, k_ref, v_ref, q_t_ref, k_t_ref,
    weight_ref,
    v_t_ref, bias_t_ref, mixed_ref,
):
    me = place_ref[0]
    rows, part = q_ref.shape
    local = x0_ref.shape[0]
    width = x0_ref.shape[1]
    half = packed_ref.shape[0]
    heads = part // HEAD_DIM
    gain = gain_ref[...].astype(F32)
    shift = shift_ref[...].astype(F32)
    weight_ref[0] = packed_ref[0:width, 0:part]
    weight_ref[1, 0 : half - width, :] = packed_ref[width:half, 0:part]
    weight_ref[1, half - width : width, :] = packed_ref[0 : 2 * width - half, part : 2 * part]
    weight_ref[2] = packed_ref[2 * width - half : 3 * width - half, part : 2 * part]
    bias = packed_ref[3 * width - half : 3 * width - half + 2, part : 2 * part].astype(F32)
    for slot, x_ref in enumerate((x0_ref, x1_ref, x2_ref, x3_ref)):
        here = rows_at(me ^ slot, local)
        unit, _ = unit_rows(x_ref[...].astype(F32))
        normed = (unit * gain + shift).astype(BF16)
        normed_ref[here, :] = normed
        q = (dot(normed, weight_ref[0]) + bias[0:1, :]).astype(BF16)
        q_ref[here, :] = q * jnp.asarray(HEAD_DIM**-0.5, BF16)
        k_ref[here, :] = dot(normed, weight_ref[1]).astype(BF16)
        v_ref[here, :] = (dot(normed, weight_ref[2]) + bias[1:2, :]).astype(BF16)

    for start in range(0, rows, BLOCK):
        cols = slice(start, start + BLOCK)
        q_t_ref[:, cols] = q_ref[cols, :].T
        k_t_ref[:, cols] = k_ref[cols, :].T
        v_t_ref[:, cols] = v_ref[cols, :].T

    for start in range(0, rows, BLOCK):
        keys = start + BLOCK
        cols = slice(start, keys)
        bias_t_ref[0:keys, :] = visibility(ids_col_ref, ids_row_ref, start, keys)
        for head in range(heads):
            here = slice(head * HEAD_DIM, (head + 1) * HEAD_DIM)
            scores = dot(k_ref[0:keys, :], keep_head(q_t_ref[:, cols], head, 0)) + bias_t_ref[0:keys, :]
            top = jnp.max(scores, axis=0, keepdims=True)
            weights = jnp.exp(scores - top)
            total = jnp.sum(weights, axis=0, keepdims=True)
            mixed_t_ref[here, cols] = dot(v_t_ref[here, 0:keys], weights.astype(BF16)) / total
            lse_ref[head : head + 1, cols] = top + jnp.log(total)
        mixed_ref[cols, :] = mixed_t_ref[:, cols].T.astype(BF16)
    for slot, out_ref in enumerate((m0_ref, m1_ref, m2_ref, m3_ref)):
        pack_rows(out_ref, mixed_ref, me ^ slot)


def pack_rows(out_ref, rows_ref, index):
    half, part = out_ref.shape[0], out_ref.shape[1] // 2
    out_ref[:, 0:part] = rows_ref[rows_at(2 * index, half), :]
    out_ref[:, part : 2 * part] = rows_ref[rows_at(2 * index + 1, half), :]


def unpack_rows(rows_ref, packed_ref, index):
    half, part = packed_ref.shape[0], packed_ref.shape[1] // 2
    rows_ref[rows_at(2 * index, half), :] = packed_ref[:, 0:part]
    rows_ref[rows_at(2 * index + 1, half), :] = packed_ref[:, part : 2 * part]


def attend_forward(place, shards, ids, gain, shift, packed):
    local, width = shards[0].shape
    rows = ids.shape[0]
    part = packed.shape[1] // 2
    heads = part // HEAD_DIM
    return call(
        attend_forward_kernel,
        [shape((local // 2, 2 * part), BF16)] * 4
        + [
            shape((part, rows), F32),
            shape((heads, rows), F32),
            shape((rows, width), BF16),
            shape((rows, part), BF16),
            shape((rows, part), BF16),
            shape((rows, part), BF16),
            shape((part, rows), BF16),
            shape((part, rows), BF16),
            shape((3, width, part), BF16),
        ],
        place, *shards, ids.reshape(1, rows), ids.reshape(rows, 1), gain, shift, packed,
        scratch=[pltpu.VMEM((part, rows), BF16), pltpu.VMEM((rows, BLOCK), F32), pltpu.VMEM((rows, part), BF16)],
        flops=6 * rows * width * part + 2 * rows * rows * part,
        name="attend_forward",
    )


def attend_backward_kernel(
    place_ref, g0_ref, g1_ref, g2_ref, g3_ref, q_ref, k_ref, v_ref, q_t_ref, k_t_ref, mixed_t_ref, lse_ref,
    ids_row_ref, ids_col_ref, weight_ref,
    n0_ref, n1_ref, n2_ref, n3_ref, grad_triple_ref,
    grad_ref, grad_t_ref, delta_ref, grad_q_t_ref, grad_k_ref, grad_v_ref, bias_t_ref,
):
    me = place_ref[0]
    rows, part = q_ref.shape
    local = n0_ref.shape[0]
    heads = part // HEAD_DIM
    for slot, packed_ref in enumerate((g0_ref, g1_ref, g2_ref, g3_ref)):
        unpack_rows(grad_ref, packed_ref, me ^ slot)
    for start in range(0, rows, BLOCK):
        cols = slice(start, start + BLOCK)
        grad_t = grad_ref[cols, :].T
        grad_t_ref[:, cols] = grad_t
        product = grad_t.astype(F32) * mixed_t_ref[:, cols]
        for head in range(heads):
            delta_ref[head : head + 1, cols] = column_sum(product[head * HEAD_DIM : (head + 1) * HEAD_DIM, :])
    grad_k_ref[...] = jnp.zeros_like(grad_k_ref)
    grad_v_ref[...] = jnp.zeros_like(grad_v_ref)
    for start in range(0, rows, BLOCK):
        keys = start + BLOCK
        cols = slice(start, keys)
        bias_t_ref[0:keys, :] = visibility(ids_col_ref, ids_row_ref, start, keys)
        for head in range(heads):
            here = slice(head * HEAD_DIM, (head + 1) * HEAD_DIM)
            scores = dot(k_ref[0:keys, :], keep_head(q_t_ref[:, cols], head, 0))
            probs = jnp.exp(scores + bias_t_ref[0:keys, :] - lse_ref[head : head + 1, cols])
            grad_probs = dot(v_ref[0:keys, :], keep_head(grad_t_ref[:, cols], head, 0))
            grad_scores = (probs * (grad_probs - delta_ref[head : head + 1, cols])).astype(BF16)
            grad_v_ref[0:keys, :] += dot(probs.astype(BF16), keep_head(grad_ref[cols, :], head, 1))
            grad_k_ref[0:keys, :] += dot(grad_scores, keep_head(q_ref[cols, :], head, 1))
            grad_q_t_ref[here, cols] = dot(k_t_ref[here, 0:keys], grad_scores)
    factor = HEAD_DIM**-0.5
    for start in range(0, rows, BLOCK):
        cols = slice(start, start + BLOCK)
        grad_triple_ref[0, cols, :] = (grad_q_t_ref[:, cols].T * factor).astype(BF16)
    grad_triple_ref[1] = grad_k_ref[...].astype(BF16)
    grad_triple_ref[2] = grad_v_ref[...].astype(BF16)
    for slot, out_ref in enumerate((n0_ref, n1_ref, n2_ref, n3_ref)):
        here = rows_at(me ^ slot, local)
        out_ref[...] = (
            dot(grad_triple_ref[0, here, :], weight_ref[0], NT)
            + dot(grad_triple_ref[1, here, :], weight_ref[1], NT)
            + dot(grad_triple_ref[2, here, :], weight_ref[2], NT)
        ).astype(BF16)


def attend_backward(place, grads, q, k, v, q_t, k_t, mixed_t, lse, ids, weight):
    rows, part = q.shape
    width = weight.shape[1]
    heads = part // HEAD_DIM
    return call(
        attend_backward_kernel,
        [shape((rows // 4, width), BF16)] * 4 + [shape((3, rows, part), BF16)],
        place, *grads, q, k, v, q_t, k_t, mixed_t, lse, ids.reshape(1, rows), ids.reshape(rows, 1), weight,
        scratch=[
            pltpu.VMEM((rows, part), BF16),
            pltpu.VMEM((part, rows), BF16),
            pltpu.VMEM((heads, rows), F32),
            pltpu.VMEM((part, rows), F32),
            pltpu.VMEM((rows, part), F32),
            pltpu.VMEM((rows, part), F32),
            pltpu.VMEM((rows, BLOCK), F32),
        ],
        flops=6 * rows * width * part + 5 * rows * rows * part,
        name="attend_backward",
    )


def mixer_kernel(
    place_ref, m0_ref, m1_ref, m2_ref, m3_ref, x_ref, mixer_ref, bias_ref, gain_ref, shift_ref,
    normed_ref, unit_ref, scale_ref, middle_ref, mixed_ref,
):
    me = place_ref[0]
    half, double = m0_ref.shape
    part = double // 2
    middle = x_ref[...].astype(F32) + bias_ref[...].astype(F32)
    for slot, packed_ref in enumerate((m0_ref, m1_ref, m2_ref, m3_ref)):
        cols = slice(slot * part, (slot + 1) * part)
        mixed_ref[0:half, cols] = packed_ref[:, 0:part]
        mixed_ref[half : 2 * half, cols] = packed_ref[:, part:double]
        middle += dot(mixed_ref[:, cols], mixer_ref[rows_at(me ^ slot, part), :])
    middle_ref[...] = middle
    unit, scale = unit_rows(middle)
    unit_ref[...] = unit
    scale_ref[...] = jnp.broadcast_to(scale, scale_ref.shape)
    normed_ref[...] = (unit * gain_ref[...].astype(F32) + shift_ref[...].astype(F32)).astype(BF16)


def mixer_part(place, packed, x, mixer, bias, gain, shift):
    rows, width = x.shape
    return call(
        mixer_kernel,
        [
            shape((rows, width), BF16), shape((rows, width), F32), shape((rows, 128), F32),
            shape((rows, width), F32), shape((rows, width), BF16),
        ],
        place, *packed, x, mixer, bias, gain, shift,
        flops=2 * rows * width * width,
        name="mixer_part",
    )


def feed_kernel(
    place_ref, normed_own_ref, normed_other_ref, cot_own_ref, cot_other_ref,
    expand_a_ref, expand_b_ref, bias_a_ref, bias_b_ref, reduce_a_ref, reduce_b_ref,
    second_own_ref, second_other_ref, grad_own_ref, grad_other_ref, active_ref, grad_hidden_ref, bias_sum_ref,
    normed_ref, cot_ref, second_ref, grad_ref, expand_ref, reduce_ref,
):
    step = pl.program_id(0)
    side = place_ref[1]
    rows = normed_own_ref.shape[0]
    chunk = expand_a_ref.shape[1]

    @pl.when(step == 0)
    def _():
        normed_ref[0:rows, :] = normed_own_ref[...]
        normed_ref[rows : 2 * rows, :] = normed_other_ref[...]
        cot_ref[0:rows, :] = cot_own_ref[...]
        cot_ref[rows : 2 * rows, :] = cot_other_ref[...]
        second_ref[...] = jnp.zeros_like(second_ref)
        grad_ref[...] = jnp.zeros_like(grad_ref)

    expand_ref[:, 0:chunk] = expand_a_ref[...]
    expand_ref[:, chunk : 2 * chunk] = expand_b_ref[...]
    reduce_ref[0:chunk, :] = reduce_a_ref[...]
    reduce_ref[chunk : 2 * chunk, :] = reduce_b_ref[...]
    bias = jnp.concatenate([bias_a_ref[...], bias_b_ref[...]], axis=1).astype(F32)
    lane = lax.broadcasted_iota(jnp.int32, (1, 2 * chunk), 1) // chunk
    sums = jnp.zeros((1, 2 * chunk), F32)
    for part in range(2):
        here = slice(part * rows, (part + 1) * rows)
        hidden = dot(normed_ref[here, :], expand_ref[...]) + bias
        square = hidden * hidden
        bend = jnp.tanh(GELU_A * hidden * (1.0 + GELU_B * square))
        half = 0.5 * (1.0 + bend)
        active = (hidden * half).astype(BF16)
        active_ref[here, :] = active
        second_ref[here, :] += dot(active, reduce_ref[...])
        slope = half + (0.5 * GELU_A) * hidden * (1.0 - bend * bend) * (1.0 + (3.0 * GELU_B) * square)
        grad_hidden = (dot(cot_ref[here, :], reduce_ref[...], NT) * slope).astype(BF16)
        grad_hidden_ref[here, :] = grad_hidden
        sums += column_sum(grad_hidden.astype(F32))
        grad_ref[here, :] += dot(grad_hidden, expand_ref[...], NT)
    for index in range(2):
        piece = sums[:, index * chunk : (index + 1) * chunk]
        bias_sum_ref[pl.ds(2 * step + index, 1), :] = jnp.where(
            lane == side, jnp.concatenate([piece, piece], axis=1), 0.0
        )

    @pl.when(step == pl.num_programs(0) - 1)
    def _():
        second_own_ref[...] = second_ref[0:rows, :]
        second_other_ref[...] = second_ref[rows : 2 * rows, :].astype(BF16)
        grad_own_ref[...] = grad_ref[0:rows, :]
        grad_other_ref[...] = grad_ref[rows : 2 * rows, :].astype(BF16)


def feed_part(place, normed_own, normed_other, cot_own, cot_other, expand, bias, reduce):
    rows, width = normed_own.shape
    hidden = expand.shape[1]
    chunk = hidden // 8
    steps = 2

    def fixed(dims):
        return pl.BlockSpec(dims, lambda i, place, n=len(dims): (0,) * n)

    def columns(height, offset):
        return pl.BlockSpec((height, chunk), lambda i, place: (0, 2 * (2 * i + offset) + place[1]))

    def block_rows(offset):
        return pl.BlockSpec((chunk, width), lambda i, place: (2 * (2 * i + offset) + place[1], 0))

    own = fixed((rows, width))
    wide_block = pl.BlockSpec((2 * rows, 2 * chunk), lambda i, place: (0, i))
    return pl.pallas_call(
        feed_kernel,
        grid_spec=pltpu.PrefetchScalarGridSpec(
            num_scalar_prefetch=1,
            grid=(steps,),
            in_specs=[
                own, own, own, own,
                columns(width, 0), columns(width, 1), columns(1, 0), columns(1, 1), block_rows(0), block_rows(1),
            ],
            out_specs=(own, own, own, own, wide_block, wide_block, fixed((4, 2 * chunk))),
            scratch_shapes=[
                pltpu.VMEM((2 * rows, width), BF16),
                pltpu.VMEM((2 * rows, width), BF16),
                pltpu.VMEM((2 * rows, width), F32),
                pltpu.VMEM((2 * rows, width), F32),
                pltpu.VMEM((width, 2 * chunk), BF16),
                pltpu.VMEM((2 * chunk, width), BF16),
            ],
        ),
        out_shape=(
            shape((rows, width), F32),
            shape((rows, width), BF16),
            shape((rows, width), F32),
            shape((rows, width), BF16),
            shape((2 * rows, hidden // 2), BF16),
            shape((2 * rows, hidden // 2), BF16),
            shape((4, 2 * chunk), F32),
        ),
        compiler_params=pltpu.CompilerParams(vmem_limit_bytes=VMEM_LIMIT, dimension_semantics=("arbitrary",)),
        cost_estimate=pl.CostEstimate(flops=8 * rows * width * hidden, bytes_accessed=4 * width * hidden, transcendentals=0),
        name="feed_part",
    )(place, normed_own, normed_other, cot_own, cot_other, expand, expand, bias, bias, reduce, reduce)


def joint_kernel(
    place_ref, second_own_ref, second_recv_ref, grad_own_ref, grad_recv_ref, middle_ref, unit_ref, scale_ref,
    cot_ref, ids_ref, mixer_ref, gain_ref, reduce_bias_ref, table_ref, bias_sum_ref,
    out_ref, grad_middle_ref, grad_low_ref, g0_ref, g1_ref, g2_ref, g3_ref, sums_ref,
):
    me = place_ref[0]
    half, double = g0_ref.shape
    part = double // 2
    cot = cot_ref[...].astype(F32)
    unit = unit_ref[...]
    grad_normed = grad_own_ref[...] + grad_recv_ref[...].astype(F32)
    back = norm_pullback(grad_normed, unit, scale_ref[:, 0:1], gain_ref[...].astype(F32))
    grad_middle = cot + back
    grad_middle_ref[...] = grad_middle
    grad_low = grad_middle.astype(BF16)
    grad_low_ref[...] = grad_low
    for slot, packed_ref in enumerate((g0_ref, g1_ref, g2_ref, g3_ref)):
        grad = dot(grad_low, mixer_ref[rows_at(me ^ slot, part), :], NT).astype(BF16)
        packed_ref[:, 0:part] = grad[0:half, :]
        packed_ref[:, part:double] = grad[half : 2 * half, :]
    sums_ref[...] = jnp.zeros_like(sums_ref)
    embedded = jnp.zeros_like(cot)
    for index in range(table_ref.shape[0]):
        chosen = ids_ref[...] == index
        embedded += jnp.where(chosen, table_ref[index : index + 1, :].astype(F32), 0.0)
        sums_ref[index : index + 1, :] = column_sum(jnp.where(chosen, cot, 0.0))
    second = second_own_ref[...] + second_recv_ref[...].astype(F32) + reduce_bias_ref[...].astype(F32)
    out_ref[...] = (middle_ref[...] + second + embedded).astype(BF16)
    sums_ref[5:6, :] = column_sum(cot)
    sums_ref[6:7, :] = column_sum(grad_low.astype(F32))
    sums_ref[7:8, :] = column_sum(grad_normed * unit)
    sums_ref[8:9, :] = column_sum(grad_normed)
    sums_ref[9:13, :] = bias_sum_ref[...]


def joint_part(place, *arrays):
    rows, width = arrays[0].shape
    part = width // 4
    return call(
        joint_kernel,
        [shape((rows, width), BF16), shape((rows, width), F32), shape((rows, width), BF16)]
        + [shape((rows // 2, 2 * part), BF16)] * 4
        + [shape((16, width), F32)],
        place, *arrays,
        flops=2 * rows * width * width,
        name="joint_part",
    )


def mixer_grads_kernel(place_ref, mixed_ref, grad_low_ref, send_ref, keep_ref, total_ref):
    me, side = place_ref[0], place_ref[1]
    block = send_ref.shape[1]
    total_ref[...] = dot(mixed_ref[...], grad_low_ref[...], TN).astype(BF16)
    for slot in range(4):
        keep_ref[me ^ slot] = total_ref[rows_at(2 * slot + side, block), :]
        send_ref[me ^ slot] = total_ref[rows_at(2 * slot + (1 - side), block), :]


def mixer_grads(place, mixed, grad_low):
    rows, width = mixed.shape
    out = shape((4, width // 8, width), BF16)
    return call(
        mixer_grads_kernel, [out, out], place, mixed, grad_low,
        scratch=[pltpu.VMEM((width, width), BF16)],
        flops=2 * rows * width * width,
        name="mixer_grads",
    )


def weight_grads_kernel(
    place_ref, normed_own_ref, normed_other_ref, cot_own_ref, cot_other_ref, active_ref, grad_hidden_ref,
    mixer_keep_ref, mixer_recv_ref,
    send_ref, keep_ref,
    normed_t_ref, cot_t_ref, stage_ref, sems,
):
    quarter, me_n = place_ref[2], place_ref[3]
    side = place_ref[1]
    rows, width = normed_own_ref.shape
    chunk = active_ref.shape[1] // 4
    high = width // 4
    normed_t_ref[:, 0:rows] = normed_own_ref[...].T
    normed_t_ref[:, rows : 2 * rows] = normed_other_ref[...].T
    cot_t_ref[:, 0:rows] = cot_own_ref[...].T
    cot_t_ref[:, rows : 2 * rows] = cot_other_ref[...].T

    def slot_of(index):
        apart = index ^ quarter
        y, x = apart >> 1, apart & 1
        return jnp.where(side == 0, 2 * x + y, apart)

    def order_of(index):
        apart = index ^ me_n
        return ((apart & 1) << 1) | (apart >> 1)

    for index in range(4):
        cols = slice(index * chunk, (index + 1) * chunk)
        expand = dot(normed_t_ref[...], grad_hidden_ref[:, cols]).astype(BF16)
        for other in range(4):
            stage_ref[slot_of(other), order_of(index), 0:high, :] = expand[other * high : (other + 1) * high, :]
        reduce = dot(cot_t_ref[...], active_ref[:, cols]).astype(BF16)
        for other in range(4):
            stage_ref[slot_of(index), order_of(other), high : 2 * high, :] = reduce[other * high : (other + 1) * high, :]
        mixer = (mixer_keep_ref[index].astype(F32) + mixer_recv_ref[index].astype(F32)).astype(BF16)
        block = mixer.shape[0] // 2
        for other in range(4):
            piece = mixer[:, other * high : (other + 1) * high]
            stage_ref[slot_of(index), order_of(other), 2 * high :, :] = jnp.concatenate(
                [piece[0:block, :], piece[block : 2 * block, :]], axis=1
            )
    out_send = pltpu.make_async_copy(stage_ref.at[2:4], send_ref, sems.at[0])
    out_keep = pltpu.make_async_copy(stage_ref.at[0:2], keep_ref, sems.at[1])
    out_send.start()
    out_keep.start()
    out_send.wait()
    out_keep.wait()


def weight_grads(place, normed_own, normed_other, cot_own, cot_other, active, grad_hidden, mixer_keep, mixer_recv):
    rows, width = normed_own.shape
    chunk = active.shape[1] // 4
    block = (4, 2 * (width // 4) + width // 16, chunk)
    out = shape((2, *block), BF16)
    return pl.pallas_call(
        weight_grads_kernel,
        out_shape=(out, out),
        in_specs=[scalars()] + [whole()] * 8,
        out_specs=(pl.BlockSpec(memory_space=pl.ANY),) * 2,
        scratch_shapes=[
            pltpu.VMEM((width, 2 * rows), BF16),
            pltpu.VMEM((width, 2 * rows), BF16),
            pltpu.VMEM((4, *block), BF16),
            pltpu.SemaphoreType.DMA((2,)),
        ],
        compiler_params=pltpu.CompilerParams(vmem_limit_bytes=VMEM_LIMIT),
        cost_estimate=pl.CostEstimate(flops=16 * rows * width * chunk * 2, bytes_accessed=20_000_000, transcendentals=0),
        name="weight_grads",
    )(place, normed_own, normed_other, cot_own, cot_other, active, grad_hidden, mixer_keep, mixer_recv)


def triple_grads_kernel(
    place_ref, x0_ref, x1_ref, x2_ref, x3_ref, n0_ref, n1_ref, n2_ref, n3_ref, normed_ref, grad_triple_ref, sums_in_ref,
    send_ref, keep_ref, sums_ref,
    packed_ref,
):
    mine = place_ref[4]
    rows, width = normed_ref.shape
    part = grad_triple_ref.shape[2]
    half = packed_ref.shape[0]
    gain_sum = jnp.zeros((1, width), F32)
    shift_sum = jnp.zeros((1, width), F32)
    for x_ref, n_ref in ((x0_ref, n0_ref), (x1_ref, n1_ref), (x2_ref, n2_ref), (x3_ref, n3_ref)):
        unit, _ = unit_rows(x_ref[...].astype(F32))
        grad = n_ref[...].astype(F32)
        gain_sum += column_sum(grad * unit)
        shift_sum += column_sum(grad)
    sums_ref[0:16, :] = sums_in_ref[...]
    sums_ref[16:24, :] = jnp.zeros((8, width), F32)
    sums_ref[16:17, :] = gain_sum
    sums_ref[17:18, :] = shift_sum
    normed = normed_ref[...]
    first, second, third = (dot(normed, grad_triple_ref[i], TN).astype(BF16) for i in range(3))
    packed_ref[0:width, 0:part] = first
    packed_ref[width:half, 0:part] = second[0 : half - width, :]
    packed_ref[0 : 2 * width - half, part : 2 * part] = second[half - width : width, :]
    packed_ref[2 * width - half : 3 * width - half, part : 2 * part] = third
    rest = half - (3 * width - half)
    place = lax.broadcasted_iota(jnp.int32, (rest, part), 0)
    bias = jnp.where(
        place == 0,
        column_sum(grad_triple_ref[0].astype(F32)),
        jnp.where(place == 1, column_sum(grad_triple_ref[2].astype(F32)), 0.0),
    )
    packed_ref[3 * width - half : half, part : 2 * part] = bias.astype(BF16)
    piece = half // 4
    for slot in range(4):
        target = keep_ref if slot < 2 else send_ref
        target[slot % 2] = packed_ref[rows_at(mine ^ slot, piece), :]


def triple_grads(place, shards, grads, normed, grad_triple, sums):
    rows, width = normed.shape
    part = grad_triple.shape[2]
    half = packed_rows(width)
    out = shape((2, half // 4, 2 * part), BF16)
    return call(
        triple_grads_kernel,
        [out, out, shape((24, width), F32)],
        place, *shards, *grads, normed, grad_triple, sums,
        scratch=[pltpu.VMEM((half, 2 * part), BF16)],
        flops=6 * rows * width * part,
        name="triple_grads",
    )


def packed_rows(width):
    return -(-(3 * width // 2 + 64) // 128) * 128


def front_kernel(place_ref, x_ref, own_ref, core_ref, pair_ref, grad_middle_ref, gain_ref, out_ref):
    unit, scale = unit_rows(x_ref[...].astype(F32))
    grad = own_ref[...].astype(F32) + core_ref[...].astype(F32) + pair_ref[...].astype(F32)
    back = norm_pullback(grad, unit, scale, gain_ref[...].astype(F32))
    out_ref[...] = (grad_middle_ref[...] + back).astype(BF16)


def front_part(place, x, *arrays):
    return call(front_kernel, [shape(x.shape, BF16)], place, x, *arrays, name="front_part")[0]


def unpack_triple_kernel(place_ref, own_ref, recv_ref, weight_ref, bias_ref, packed_ref):
    stay, mine = place_ref[5], place_ref[6]
    width, part = weight_ref.shape[1:]
    half = packed_ref.shape[0]
    piece = half // 4

    @pl.when(stay == 1)
    def _():
        for slot in range(4):
            packed_ref[rows_at(mine ^ slot, piece), :] = own_ref[slot]

    @pl.when(stay == 0)
    def _():
        for slot in range(4):
            packed_ref[rows_at(mine ^ slot, piece), :] = recv_ref[slot]

    weight_ref[0] = packed_ref[0:width, 0:part].astype(F32)
    weight_ref[1, 0 : half - width, :] = packed_ref[width:half, 0:part].astype(F32)
    weight_ref[1, half - width : width, :] = packed_ref[0 : 2 * width - half, part : 2 * part].astype(F32)
    weight_ref[2] = packed_ref[2 * width - half : 3 * width - half, part : 2 * part].astype(F32)
    bias_ref[...] = packed_ref[3 * width - half : 3 * width - half + 2, part : 2 * part].astype(F32)


def unpack_triple(place, own, recv, width):
    part = own.shape[2] // 2
    return call(
        unpack_triple_kernel,
        [shape((3, width, part), F32), shape((2, part), F32)],
        place, own, recv,
        scratch=[pltpu.VMEM((packed_rows(width), 2 * part), BF16)],
        name="unpack_triple",
    )


def swap_block_kernel(place_ref, a_ref, b_ref, c_ref, total_ref, send_ref):
    side = place_ref[1]
    total_ref[...] = a_ref[...].astype(F32) + b_ref[...].astype(F32) + c_ref[...].astype(F32)
    block = send_ref.shape[0]
    send_ref[...] = total_ref[rows_at(1 - side, block), :].astype(BF16)


def swap_block(place, a, b, c, block):
    return call(
        swap_block_kernel,
        [shape(a.shape, F32), shape((block, a.shape[1]), BF16)],
        place, a, b, c,
        name="swap_block",
    )


def unpack_weights_kernel(place_ref, total_ref, recv_ref, expand_ref, reduce_ref, mixer_ref):
    side = place_ref[1]
    block, double = expand_ref.shape
    chunk = double // 2
    high, part = reduce_ref.shape[1], mixer_ref.shape[1]
    mine = total_ref[rows_at(side, block), :]
    other = recv_ref[...].astype(F32)
    expand_ref[:, 0:chunk] = jnp.where(side == 0, mine, other)
    expand_ref[:, chunk:double] = jnp.where(side == 0, other, mine)
    reduce_ref[...] = total_ref[high : 2 * high, :].T
    half = block // 2
    mixer_ref[0:half, :] = total_ref[2 * high :, 0:part]
    mixer_ref[half:block, :] = total_ref[2 * high :, part : 2 * part]


def unpack_weights(place, total, recv, width):
    block, chunk = recv.shape
    part = width // 4
    return call(
        unpack_weights_kernel,
        [shape((block, 2 * chunk), F32), shape((chunk, part), F32), shape((block, part), F32)],
        place, total, recv,
        name="unpack_weights",
    )


def body(
    inputs,
    pass_ids,
    front_gain,
    front_shift,
    triple_weight,
    triple_bias,
    mixer_weight,
    mixer_bias,
    back_gain,
    back_shift,
    expand_weight,
    expand_bias,
    reduce_weight,
    reduce_bias,
    pass_table,
    cotangent,
):
    local_rows, width = inputs.shape
    seq_rows = pass_ids.shape[1]
    part = triple_weight.shape[2]
    wide_size, narrow_size = lax.axis_size("wide"), lax.axis_size("narrow")
    low_bits = wide_size.bit_length() - 4
    side_bit, x_bit, y_bit = 1 << low_bits, 2 << low_bits, 4 << low_bits

    wide, narrow = lax.axis_index("wide"), lax.axis_index("narrow")
    c, h, l = wide & 1, narrow >> 1, narrow & 1
    me = 2 * c + l
    top = wide >> low_bits
    side, quarter = top & 1, top >> 1
    x1, y1 = (wide >> 1) & 1, (wide >> 2) & 1
    stay = (c == h).astype(jnp.int32)
    place = jnp.stack(
        [
            me, side, quarter, narrow,
            jnp.where(c == 0, 2 * x1 + y1, 2 * y1 + x1),
            stay,
            jnp.where(h == 0, 2 * x1 + y1, 2 * y1 + x1),
        ]
    ).astype(jnp.int32)

    def send(value, target):
        pairs = []
        for w in range(wide_size):
            for n in range(narrow_size):
                to = target(w, n)
                if to is not None:
                    pairs.append((w * narrow_size + n, to[0] * narrow_size + to[1]))
        return lax.ppermute(value, AXES, pairs)

    def moved(w, n):
        return (w, n) if (w & 1) == (n >> 1) else (w ^ 1, n ^ 2)

    def home(w, n):
        return None if (w & 1) == (n >> 1) else (w, n ^ 2)

    def core(w, n):
        return (w ^ 1, n)

    def pair(w, n):
        return (w, n ^ 1)

    def diagonal(w, n):
        return (w ^ 1, n ^ 1)

    def across(w, n):
        return (w, n ^ 2)

    def sided(w, n):
        return (w ^ side_bit, n)

    def first(w, n):
        return (w ^ (y_bit if w & side_bit else x_bit), n)

    def second(w, n):
        return (w ^ (x_bit if w & side_bit else y_bit), n)

    def triple_first(w, n):
        return (w ^ (4 if w & 1 else 2), n)

    def triple_second(w, n):
        return (w ^ (2 if w & 1 else 4), n)

    def row(vector):
        return vector.reshape(1, -1)

    def add(*terms):
        return sum(t.astype(F32) for t in terms).astype(BF16)

    own_ids = pass_ids.reshape(seq_rows)
    x0 = send(inputs, moved)
    x1_rows = send(x0, pair)
    x2 = send(x0, core)
    x3 = send(x1_rows, core)
    half = packed_rows(width)
    flat = jnp.concatenate(
        [triple_weight.reshape(3 * width, part), triple_bias, jnp.zeros((2 * half - 3 * width - 2, part), BF16)], axis=0
    )
    packed = send(jnp.concatenate([flat[:half], flat[half:]], axis=1), moved)
    ids = jnp.where(stay == 1, own_ids, send(own_ids, core))
    cot_own = send(cotangent, moved)
    cot_other = send(cot_own, sided)

    shards = (x0, x1_rows, x2, x3)
    m0, m1, m2, m3, mixed_t, lse, normed, q, k, v, q_t, k_t, weight = attend_forward(
        place, shards, ids, row(front_gain), row(front_shift), packed
    )
    slots = (m0, send(m1, pair), send(m2, core), send(m3, diagonal))
    normed_two, unit_two, scale_two, middle, mixed_rows = mixer_part(
        place, slots, x0, mixer_weight, row(mixer_bias), row(back_gain), row(back_shift)
    )
    normed_other = send(normed_two, sided)
    second_own, second_send, grad_own, grad_send, active, grad_hidden, bias_sums = feed_part(
        place, normed_two, normed_other, cot_own, cot_other, expand_weight, row(expand_bias), reduce_weight
    )
    grad_recv = send(grad_send, sided)
    second_recv = send(second_send, sided)
    row_ids = lax.dynamic_slice_in_dim(ids, me * local_rows, local_rows).reshape(local_rows, 1)
    out_rows, grad_middle, grad_low, g0, g1, g2, g3, sums = joint_part(
        place, second_own, second_recv, grad_own, grad_recv, middle, unit_two, scale_two, cot_own, row_ids,
        mixer_weight, row(back_gain), row(reduce_bias), pass_table, bias_sums,
    )
    layer_out = send(out_rows, moved)
    grads = (g0, send(g1, pair), send(g2, core), send(g3, diagonal))
    mixer_send, mixer_keep = mixer_grads(place, mixed_rows, grad_low)
    mixer_recv = send(mixer_send, sided)
    weight_send, weight_keep = weight_grads(
        place, normed_two, normed_other, cot_own, cot_other, active, grad_hidden, mixer_keep, mixer_recv
    )
    n0, n1, n2, n3, grad_triple_rows = attend_backward(
        place, grads, q, k, v, q_t, k_t, mixed_t, lse, ids, weight
    )
    core_own = send(n2, core)
    core_pair = send(n3, core)
    pair_sum = send(add(n1, core_pair), pair)
    triple_send, triple_keep, all_sums = triple_grads(
        place, shards, (n0, n1, n2, n3), normed, grad_triple_rows, sums
    )
    grad_inputs = send(front_part(place, x0, n0, core_own, pair_sum, grad_middle, row(front_gain)), moved)

    triple_recv = send(triple_send, triple_first)
    triple_next = send(add(triple_keep[1], triple_recv[1]), triple_second)
    triple_sum = add(triple_keep[0], triple_recv[0], triple_next)
    bit = 8
    while bit < wide_size:
        triple_sum = add(triple_sum, send(triple_sum, lambda w, n, bit=bit: (w ^ bit, n)))
        bit *= 2
    triple_sum = add(triple_sum, send(triple_sum, home))
    triple_half = jnp.stack([triple_sum, send(triple_sum, triple_second)])
    triple_all = jnp.concatenate([triple_half, send(triple_half, triple_first)], axis=0)
    grad_triple, grad_triple_bias = unpack_triple(place, triple_all, send(triple_all, core), width)

    steps = [lambda w, n, bit=1 << i: (w ^ bit, n) for i in range(wide_size.bit_length() - 1)] + [pair, across]
    for step in steps:
        all_sums = all_sums + send(all_sums, step)

    first_recv = send(weight_send, first)
    second_recv_w = send(add(weight_keep[1], first_recv[1]), second)
    keep_a = add(weight_keep[0, 0:2], first_recv[0, 0:2], second_recv_w[0:2])
    send_a = add(weight_keep[0, 2:4], first_recv[0, 2:4], second_recv_w[2:4])
    recv_a = send(send_a, pair)
    recv_b = send(add(keep_a[1], recv_a[1]), across)
    total, swap = swap_block(place, keep_a[0], recv_a[0], recv_b, width // 8)
    total_expand, total_reduce, total_mixer = unpack_weights(place, total, send(swap, sided), width)
    if low_bits:
        size = 1 << low_bits
        peers = [[size * i + j for j in range(size)] for i in range(wide_size // size)]
        total_expand, total_reduce, total_mixer = (
            lax.psum_scatter(t, "wide", scatter_dimension=0, axis_index_groups=peers, tiled=True)
            for t in (total_expand, total_reduce, total_mixer)
        )
    passes = pass_table.shape[0]
    return (
        layer_out,
        grad_inputs,
        all_sums[16],
        all_sums[17],
        grad_triple,
        grad_triple_bias,
        total_mixer,
        all_sums[6],
        all_sums[7],
        all_sums[8],
        total_expand,
        all_sums[9:13].reshape(-1),
        total_reduce,
        all_sums[5],
        all_sums[0:passes],
    )


def solution(mesh):
    rows = P(AXES, None)
    block = P("wide", "narrow")
    return jax.shard_map(
        body,
        mesh=mesh,
        in_specs=(
            rows, P("wide", None), P(), P(), P(None, None, "narrow"), P(None, "narrow"),
            P(), P(), P(), P(), P(), P(), P(), P(), P(), rows,
        ),
        out_specs=(
            rows, rows, P(), P(), P(None, None, "narrow"), P(None, "narrow"), block,
            P(), P(), P(), block, P(), block, P(), P(),
        ),
        check_vma=False,
    )
```

```python
import math

import jax
import jax.numpy as jnp
from jax import lax
from jax.experimental import pallas as pl
from jax.experimental.pallas import tpu as pltpu
from jax.sharding import PartitionSpec as P


HEAD_DIM = 64
EPSILON = 1e-05
BLOCK = 256
HIDDEN = -1e30
F32 = jnp.float32
BF16 = jnp.bfloat16
MIB = 1024 * 1024
AXES = ("wide", "narrow")
NN = (((1,), (0,)), ((), ()))
NT = (((1,), (1,)), ((), ()))
TN = (((0,), (0,)), ((), ()))
GELU_A = math.sqrt(2.0 / math.pi)
GELU_B = 0.044715
shape = jax.ShapeDtypeStruct

FRONT_GAIN, FRONT_SHIFT, MIXER_BIAS, BACK_GAIN, BACK_SHIFT, REDUCE_BIAS, EXPAND_BIAS, TABLE = 0, 1, 2, 3, 4, 5, 6, 10
SUM_TABLE, SUM_COT, SUM_MIXER, SUM_GAIN, SUM_SHIFT, SUM_EXPAND = 0, 5, 6, 7, 8, 9
SUM_FRONT_GAIN, SUM_FRONT_SHIFT, SUM_TRIPLE = 16, 17, 18


def dot(left, right, dims=NN):
    return lax.dot_general(left, right, dims, preferred_element_type=F32)


def whole():
    return pl.BlockSpec(memory_space=pltpu.VMEM)


def call(kernel, outs, *arrays, scratch=(), vmem=12, name=None):
    return pl.pallas_call(
        kernel,
        out_shape=tuple(outs),
        in_specs=[pl.BlockSpec(memory_space=pltpu.SMEM)] + [whole()] * (len(arrays) - 1),
        out_specs=(whole(),) * len(outs),
        scratch_shapes=list(scratch),
        compiler_params=pltpu.CompilerParams(vmem_limit_bytes=vmem * MIB),
        name=name,
    )(*arrays)


def unit_rows(values):
    centred = values - jnp.mean(values, axis=-1, keepdims=True)
    scale = lax.rsqrt(jnp.mean(centred * centred, axis=-1, keepdims=True) + EPSILON)
    return centred * scale, scale


def norm_pullback(grad_out, unit, scale, gain):
    grad_unit = grad_out * gain
    inner = (
        grad_unit
        - jnp.mean(grad_unit, axis=-1, keepdims=True)
        - unit * jnp.mean(grad_unit * unit, axis=-1, keepdims=True)
    )
    return inner * scale


def column_sum(values):
    return jnp.sum(values, axis=0, keepdims=True)


def keep_head(block, head, axis):
    place = lax.broadcasted_iota(jnp.int32, block.shape, axis) // HEAD_DIM
    return jnp.where(place == head, block, jnp.zeros_like(block))


def rows_at(index, count):
    return pl.ds(pl.multiple_of(index * count, math.gcd(count, 64)), count)


def vector(vectors_ref, index):
    return vectors_ref[index : index + 1, :]


def pass_ids_of(place_ref, own_ref, other_ref, row_ref, col_ref):
    stay = jnp.full(own_ref.shape, place_ref[5], jnp.int32)
    ids = jnp.where(stay == 1, own_ref[...], other_ref[...]).astype(F32)
    row_ref[...] = ids
    rows = ids.shape[1]
    for start in range(0, rows, BLOCK):
        col_ref[start : start + BLOCK, :] = jnp.broadcast_to(ids[:, start : start + BLOCK], (128, BLOCK)).T


def visibility(ids_col_ref, ids_row_ref, start, keys):
    seen = ids_col_ref[0:keys, 0:1] <= ids_row_ref[:, start : start + BLOCK]
    key_place = lax.broadcasted_iota(jnp.int32, (keys, BLOCK), 0)
    query_place = lax.broadcasted_iota(jnp.int32, (keys, BLOCK), 1) + start
    return jnp.where(seen & (key_place <= query_place), 0.0, HIDDEN).astype(F32)


def vectors_kernel(place_ref, *refs):
    out_ref, table_ref, long_ref = refs[-1], refs[-2], refs[-3]
    width = out_ref.shape[1]
    out_ref[...] = jnp.zeros_like(out_ref)
    for index, ref in enumerate(refs[:-3]):
        out_ref[index : index + 1, :] = ref[...].astype(F32).reshape(1, width)
    for index in range(long_ref.shape[0] // width):
        part = long_ref[index * width : (index + 1) * width]
        out_ref[EXPAND_BIAS + index : EXPAND_BIAS + index + 1, :] = part.astype(F32).reshape(1, width)
    out_ref[TABLE : TABLE + table_ref.shape[0], :] = table_ref[...].astype(F32)


def gather_vectors(place, *arrays):
    return call(vectors_kernel, [shape((16, arrays[0].shape[0]), F32)], place, *arrays, vmem=4, name="gather_vectors")[0]


def attend_forward_kernel(
    place_ref, x0_ref, x1_ref, x2_ref, x3_ref, ids_own_ref, ids_other_ref, vectors_ref,
    weight_own_ref, p0_ref, p1_ref, p23_ref, bias_ref,
    m0_ref, m1_ref, m2_ref, m3_ref, mixed_t_ref, normed_ref, triple_ref, weight_ref,
    ids_row_ref, ids_col_ref, q_t_ref, v_t_ref, bias_t_ref, mixed_ref, straight_ref,
):
    me, stay, corner = place_ref[0], place_ref[5], place_ref[7]
    _, rows, part = triple_ref.shape
    local = x0_ref.shape[0]
    piece = p0_ref.shape[0]
    heads = part // HEAD_DIM
    gain = vector(vectors_ref, FRONT_GAIN)
    shift = vector(vectors_ref, FRONT_SHIFT)
    pass_ids_of(place_ref, ids_own_ref, ids_other_ref, ids_row_ref, ids_col_ref)

    @pl.when(stay == 1)
    def _():
        weight_ref[...] = weight_own_ref[...]

    @pl.when(stay == 0)
    def _():
        for slot, value in enumerate((p0_ref[...], p1_ref[...], p23_ref[0], p23_ref[1])):
            weight_ref[rows_at(corner ^ slot, piece), :] = value

    straight_ref[...] = weight_ref[...].T
    bias = bias_ref[...].astype(F32)
    for slot, x_ref in enumerate((x0_ref, x1_ref, x2_ref, x3_ref)):
        here = rows_at(me ^ slot, local)
        unit, _ = unit_rows(x_ref[...].astype(F32))
        normed = (unit * gain + shift).astype(BF16)
        normed_ref[here, :] = normed
        q = (dot(normed, straight_ref[:, 0:part]) + bias[0:1, :]).astype(BF16)
        triple_ref[0, here, :] = q * jnp.asarray(HEAD_DIM**-0.5, BF16)
        triple_ref[1, here, :] = dot(normed, straight_ref[:, part : 2 * part]).astype(BF16)
        triple_ref[2, here, :] = (dot(normed, straight_ref[:, 2 * part : 3 * part]) + bias[1:2, :]).astype(BF16)

    for start in range(0, rows, BLOCK):
        cols = slice(start, start + BLOCK)
        q_t_ref[:, cols] = triple_ref[0, cols, :].T
        v_t_ref[:, cols] = triple_ref[2, cols, :].T

    mixed_t_ref[part : part + 8, :] = jnp.zeros((8, rows), F32)
    for start in range(0, rows, BLOCK):
        keys = start + BLOCK
        cols = slice(start, keys)
        bias_t_ref[0:keys, :] = visibility(ids_col_ref, ids_row_ref, start, keys)
        for head in range(heads):
            here = slice(head * HEAD_DIM, (head + 1) * HEAD_DIM)
            scores = dot(triple_ref[1, 0:keys, :], keep_head(q_t_ref[:, cols], head, 0)) + bias_t_ref[0:keys, :]
            top = jnp.max(scores, axis=0, keepdims=True)
            weights = jnp.exp(scores - top)
            total = jnp.sum(weights, axis=0, keepdims=True)
            mixed_t_ref[here, cols] = dot(v_t_ref[here, 0:keys], weights.astype(BF16)) / total
            mixed_t_ref[part + head : part + head + 1, cols] = top + jnp.log(total)
        mixed_ref[cols, :] = mixed_t_ref[0:part, cols].T.astype(BF16)
    for slot, out_ref in enumerate((m0_ref, m1_ref, m2_ref, m3_ref)):
        pack_rows(out_ref, mixed_ref, me ^ slot)


def pack_rows(out_ref, rows_ref, index):
    half, part = out_ref.shape[0], out_ref.shape[1] // 2
    out_ref[:, 0:part] = rows_ref[rows_at(2 * index, half), :]
    out_ref[:, part : 2 * part] = rows_ref[rows_at(2 * index + 1, half), :]


def unpack_rows(rows_ref, packed_ref, index):
    half, part = packed_ref.shape[0], packed_ref.shape[1] // 2
    rows_ref[rows_at(2 * index, half), :] = packed_ref[:, 0:part]
    rows_ref[rows_at(2 * index + 1, half), :] = packed_ref[:, part : 2 * part]


def attend_forward(place, shards, ids_own, ids_other, vectors, weight, pieces, bias):
    local, width = shards[0].shape
    rows = ids_own.shape[1]
    part = weight.shape[0] // 3
    return call(
        attend_forward_kernel,
        [shape((local // 2, 2 * part), BF16)] * 4
        + [
            shape((part + 8, rows), F32),
            shape((rows, width), BF16),
            shape((3, rows, part), BF16),
            shape(weight.shape, BF16),
        ],
        place, *shards, ids_own, ids_other, vectors, weight, *pieces, bias,
        scratch=[
            pltpu.VMEM((1, rows), F32),
            pltpu.VMEM((rows, 128), F32),
            pltpu.VMEM((part, rows), BF16),
            pltpu.VMEM((part, rows), BF16),
            pltpu.VMEM((rows, BLOCK), F32),
            pltpu.VMEM((rows, part), BF16),
            pltpu.VMEM((width, 3 * part), BF16),
        ],
        vmem=20,
        name="attend_forward",
    )


def attend_backward_kernel(
    place_ref, g0_ref, g1_ref, g2_ref, g3_ref, triple_ref, mixed_t_ref, ids_own_ref, ids_other_ref, weight_ref,
    near_ref, far_ref, grad_triple_ref,
    grad_ref, grad_t_ref, delta_ref, grad_q_t_ref, grad_k_ref, grad_v_ref, bias_t_ref,
    ids_row_ref, ids_col_ref, q_t_ref, k_t_ref,
):
    me = place_ref[0]
    _, rows, part = triple_ref.shape
    local = near_ref.shape[1]
    heads = part // HEAD_DIM
    for slot, packed_ref in enumerate((g0_ref, g1_ref, g2_ref, g3_ref)):
        unpack_rows(grad_ref, packed_ref, me ^ slot)
    pass_ids_of(place_ref, ids_own_ref, ids_other_ref, ids_row_ref, ids_col_ref)
    for start in range(0, rows, BLOCK):
        cols = slice(start, start + BLOCK)
        q_t_ref[:, cols] = triple_ref[0, cols, :].T
        k_t_ref[:, cols] = triple_ref[1, cols, :].T
        grad_t = grad_ref[cols, :].T
        grad_t_ref[:, cols] = grad_t
        product = grad_t.astype(F32) * mixed_t_ref[0:part, cols]
        for head in range(heads):
            delta_ref[head : head + 1, cols] = column_sum(product[head * HEAD_DIM : (head + 1) * HEAD_DIM, :])
    grad_k_ref[...] = jnp.zeros_like(grad_k_ref)
    grad_v_ref[...] = jnp.zeros_like(grad_v_ref)
    for start in range(0, rows, BLOCK):
        keys = start + BLOCK
        cols = slice(start, keys)
        bias_t_ref[0:keys, :] = visibility(ids_col_ref, ids_row_ref, start, keys)
        for head in range(heads):
            here = slice(head * HEAD_DIM, (head + 1) * HEAD_DIM)
            scores = dot(triple_ref[1, 0:keys, :], keep_head(q_t_ref[:, cols], head, 0))
            probs = jnp.exp(scores + bias_t_ref[0:keys, :] - mixed_t_ref[part + head : part + head + 1, cols])
            grad_probs = dot(triple_ref[2, 0:keys, :], keep_head(grad_t_ref[:, cols], head, 0))
            grad_scores = (probs * (grad_probs - delta_ref[head : head + 1, cols])).astype(BF16)
            grad_v_ref[0:keys, :] += dot(probs.astype(BF16), keep_head(grad_ref[cols, :], head, 1))
            grad_k_ref[0:keys, :] += dot(grad_scores, keep_head(triple_ref[0, cols, :], head, 1))
            grad_q_t_ref[here, cols] = dot(k_t_ref[here, 0:keys], grad_scores)
    factor = HEAD_DIM**-0.5
    for start in range(0, rows, BLOCK):
        cols = slice(start, start + BLOCK)
        grad_triple_ref[0, cols, :] = (grad_q_t_ref[:, cols].T * factor).astype(BF16)
    grad_triple_ref[1] = grad_k_ref[...].astype(BF16)
    grad_triple_ref[2] = grad_v_ref[...].astype(BF16)
    for slot in range(4):
        here = rows_at(me ^ slot, local)
        target = near_ref if slot < 2 else far_ref
        target[slot % 2] = (
            dot(grad_triple_ref[0, here, :], weight_ref[0:part, :])
            + dot(grad_triple_ref[1, here, :], weight_ref[part : 2 * part, :])
            + dot(grad_triple_ref[2, here, :], weight_ref[2 * part : 3 * part, :])
        ).astype(BF16)


def attend_backward(place, grads, triple, mixed_t, ids_own, ids_other, weight):
    _, rows, part = triple.shape
    width = weight.shape[1]
    heads = part // HEAD_DIM
    pair = shape((2, rows // 4, width), BF16)
    return call(
        attend_backward_kernel,
        [pair, pair, shape((3, rows, part), BF16)],
        place, *grads, triple, mixed_t, ids_own, ids_other, weight,
        scratch=[
            pltpu.VMEM((rows, part), BF16),
            pltpu.VMEM((part, rows), BF16),
            pltpu.VMEM((heads, rows), F32),
            pltpu.VMEM((part, rows), F32),
            pltpu.VMEM((rows, part), F32),
            pltpu.VMEM((rows, part), F32),
            pltpu.VMEM((rows, BLOCK), F32),
            pltpu.VMEM((1, rows), F32),
            pltpu.VMEM((rows, 128), F32),
            pltpu.VMEM((part, rows), BF16),
            pltpu.VMEM((part, rows), BF16),
        ],
        vmem=16,
        name="attend_backward",
    )


def mixer_kernel(
    place_ref, m0_ref, m1_ref, m2_ref, m3_ref, x_ref, mixer_ref, vectors_ref,
    normed_ref, middle_ref, mixed_ref,
):
    me = place_ref[0]
    half, double = m0_ref.shape
    part = double // 2
    middle = x_ref[...].astype(F32) + vector(vectors_ref, MIXER_BIAS)
    for slot, packed_ref in enumerate((m0_ref, m1_ref, m2_ref, m3_ref)):
        cols = slice(slot * part, (slot + 1) * part)
        mixed_ref[0:half, cols] = packed_ref[:, 0:part]
        mixed_ref[half : 2 * half, cols] = packed_ref[:, part:double]
        middle += dot(mixed_ref[:, cols], mixer_ref[rows_at(me ^ slot, part), :])
    middle_ref[...] = middle
    unit, _ = unit_rows(middle)
    normed_ref[...] = (unit * vector(vectors_ref, BACK_GAIN) + vector(vectors_ref, BACK_SHIFT)).astype(BF16)


def mixer_part(place, packed, x, mixer, vectors):
    rows, width = x.shape
    return call(
        mixer_kernel,
        [shape((rows, width), BF16), shape((rows, width), F32), shape((rows, width), BF16)],
        place, *packed, x, mixer, vectors,
        name="mixer_part",
    )


def feed_kernel(
    place_ref, normed_own_ref, normed_other_ref, cot_own_ref, cot_other_ref, expand_ref, reduce_ref, vectors_ref,
    second_ref, grad_ref, send_ref, active_ref, grad_hidden_ref, bias_sum_ref,
    total_ref, back_ref,
):
    side = place_ref[1]
    rows = normed_own_ref.shape[0]
    chunk = active_ref.shape[1] // 4
    lane = lax.broadcasted_iota(jnp.int32, (1, 2 * chunk), 1) // chunk
    for index in range(4):
        block = pl.ds(pl.multiple_of((2 * index + side) * chunk, 128), chunk)
        expand = expand_ref[:, block]
        reduce = reduce_ref[block, :]
        bias = vectors_ref[EXPAND_BIAS + index : EXPAND_BIAS + index + 1, pl.ds(pl.multiple_of(side * chunk, 128), chunk)]
        sums = jnp.zeros((1, chunk), F32)
        for part, (normed_ref, cot_ref) in enumerate(((normed_own_ref, cot_own_ref), (normed_other_ref, cot_other_ref))):
            here = slice(part * rows, (part + 1) * rows)
            cols = slice(index * chunk, (index + 1) * chunk)
            hidden = dot(normed_ref[...], expand) + bias
            square = hidden * hidden
            bend = jnp.tanh(GELU_A * hidden * (1.0 + GELU_B * square))
            half = 0.5 * (1.0 + bend)
            active = (hidden * half).astype(BF16)
            active_ref[here, cols] = active
            second = dot(active, reduce)
            slope = half + (0.5 * GELU_A) * hidden * (1.0 - bend * bend) * (1.0 + (3.0 * GELU_B) * square)
            grad_hidden = (dot(cot_ref[...], reduce, NT) * slope).astype(BF16)
            grad_hidden_ref[here, cols] = grad_hidden
            sums += column_sum(grad_hidden.astype(F32))
            back = dot(grad_hidden, expand, NT)
            if index == 0:
                total_ref[here, :] = second
                back_ref[here, :] = back
            else:
                total_ref[here, :] += second
                back_ref[here, :] += back
        bias_sum_ref[index : index + 1, :] = jnp.where(lane == side, jnp.concatenate([sums, sums], axis=1), 0.0)
    second_ref[...] = total_ref[0:rows, :]
    grad_ref[...] = back_ref[0:rows, :]
    send_ref[0] = back_ref[rows : 2 * rows, :].astype(BF16)
    send_ref[1] = total_ref[rows : 2 * rows, :].astype(BF16)


def feed_part(place, normed_own, normed_other, cot_own, cot_other, expand, reduce, vectors):
    rows, width = normed_own.shape
    hidden = expand.shape[1]
    return call(
        feed_kernel,
        [
            shape((rows, width), F32),
            shape((rows, width), F32),
            shape((2, rows, width), BF16),
            shape((2 * rows, hidden // 2), BF16),
            shape((2 * rows, hidden // 2), BF16),
            shape((4, width), F32),
        ],
        place, normed_own, normed_other, cot_own, cot_other, expand, reduce, vectors,
        scratch=[
            pltpu.VMEM((2 * rows, width), F32),
            pltpu.VMEM((2 * rows, width), F32),
        ],
        vmem=20,
        name="feed_part",
    )


def joint_kernel(
    place_ref, grad_own_ref, recv_ref, middle_ref, cot_ref, mixer_ref, vectors_ref,
    grad_middle_ref, grad_low_ref, g0_ref, g1_ref, g2_ref, g3_ref,
):
    me = place_ref[0]
    half, double = g0_ref.shape
    part = double // 2
    grad_normed = grad_own_ref[...] + recv_ref[0].astype(F32)
    unit, scale = unit_rows(middle_ref[...])
    back = norm_pullback(grad_normed, unit, scale, vector(vectors_ref, BACK_GAIN))
    grad_middle = cot_ref[...].astype(F32) + back
    grad_middle_ref[...] = grad_middle
    grad_low = grad_middle.astype(BF16)
    grad_low_ref[...] = grad_low
    for slot, packed_ref in enumerate((g0_ref, g1_ref, g2_ref, g3_ref)):
        grad = dot(grad_low, mixer_ref[rows_at(me ^ slot, part), :], NT).astype(BF16)
        packed_ref[:, 0:part] = grad[0:half, :]
        packed_ref[:, part:double] = grad[half : 2 * half, :]


def joint_part(place, *arrays):
    rows, width = arrays[0].shape
    part = width // 4
    return call(
        joint_kernel,
        [shape((rows, width), F32), shape((rows, width), BF16)] + [shape((rows // 2, 2 * part), BF16)] * 4,
        place, *arrays,
        name="joint_part",
    )


def outer_kernel(
    place_ref, second_ref, grad_own_ref, recv_ref, middle_ref, cot_ref, grad_low_ref, mixed_ref,
    ids_own_ref, ids_other_ref, vectors_ref, bias_sum_ref,
    out_ref, sums_ref, mixer_send_ref, mixer_keep_ref,
    total_ref, ids_row_ref, ids_ref,
):
    me, side = place_ref[0], place_ref[1]
    rows = cot_ref.shape[0]
    cot = cot_ref[...].astype(F32)
    unit, _ = unit_rows(middle_ref[...])
    pass_ids_of(place_ref, ids_own_ref, ids_other_ref, ids_row_ref, ids_ref)
    grad_normed = grad_own_ref[...] + recv_ref[0].astype(F32)
    sums_ref[...] = jnp.zeros_like(sums_ref)
    embedded = jnp.zeros_like(cot)
    ids = ids_ref[rows_at(me, rows), 0:1]
    for index in range(5):
        chosen = ids == index
        embedded += jnp.where(chosen, vector(vectors_ref, TABLE + index), 0.0)
        sums_ref[SUM_TABLE + index : SUM_TABLE + index + 1, :] = column_sum(jnp.where(chosen, cot, 0.0))
    second = second_ref[...] + recv_ref[1].astype(F32) + vector(vectors_ref, REDUCE_BIAS)
    out_ref[...] = (middle_ref[...] + second + embedded).astype(BF16)
    sums_ref[SUM_COT : SUM_COT + 1, :] = column_sum(cot)
    sums_ref[SUM_MIXER : SUM_MIXER + 1, :] = column_sum(grad_low_ref[...].astype(F32))
    sums_ref[SUM_GAIN : SUM_GAIN + 1, :] = column_sum(grad_normed * unit)
    sums_ref[SUM_SHIFT : SUM_SHIFT + 1, :] = column_sum(grad_normed)
    sums_ref[SUM_EXPAND : SUM_EXPAND + 4, :] = bias_sum_ref[...]
    block = mixer_send_ref.shape[1]
    total_ref[...] = dot(mixed_ref[...], grad_low_ref[...], TN).astype(BF16)
    for slot in range(4):
        mixer_keep_ref[me ^ slot] = total_ref[rows_at(2 * slot + side, block), :]
        mixer_send_ref[me ^ slot] = total_ref[rows_at(2 * slot + (1 - side), block), :]


def outer_part(place, *arrays, seq_rows):
    rows, width = arrays[0].shape
    part = shape((4, width // 8, width), BF16)
    return call(
        outer_kernel,
        [shape((rows, width), BF16), shape((16, width), F32), part, part],
        place, *arrays,
        scratch=[pltpu.VMEM((width, width), BF16), pltpu.VMEM((1, seq_rows), F32), pltpu.VMEM((seq_rows, 128), F32)],
        name="outer_part",
    )


def slot_of(index, quarter, side):
    apart = index ^ quarter
    return jnp.where(side == 0, 2 * (apart & 1) + (apart >> 1), apart)


def order_of(index, me_n):
    apart = index ^ me_n
    return ((apart & 1) << 1) | (apart >> 1)


def reduce_grads_kernel(place_ref, cot_own_ref, cot_other_ref, active_ref, send_ref, keep_ref, cot_t_ref, stage_ref):
    side, quarter, me_n = place_ref[1], place_ref[2], place_ref[3]
    rows, width = cot_own_ref.shape
    chunk = active_ref.shape[1] // 4
    high = width // 4
    cot_t_ref[:, 0:rows] = cot_own_ref[...].T
    cot_t_ref[:, rows : 2 * rows] = cot_other_ref[...].T
    for index in range(4):
        reduce = dot(cot_t_ref[...], active_ref[:, index * chunk : (index + 1) * chunk]).astype(BF16)
        for other in range(4):
            stage_ref[slot_of(index, quarter, side), order_of(other, me_n)] = reduce[other * high : (other + 1) * high, :]
    keep_ref[...] = stage_ref[0:2]
    send_ref[...] = stage_ref[2:4]


def reduce_grads(place, cot_own, cot_other, active):
    rows, width = cot_own.shape
    block = (4, width // 4, active.shape[1] // 4)
    out = shape((2, *block), BF16)
    return call(
        reduce_grads_kernel,
        [out, out],
        place, cot_own, cot_other, active,
        scratch=[pltpu.VMEM((width, 2 * rows), BF16), pltpu.VMEM((4, *block), BF16)],
        name="reduce_grads",
    )


def expand_grads_kernel(
    place_ref, normed_own_ref, normed_other_ref, grad_hidden_ref, mixer_keep_ref, mixer_recv_ref,
    send_ref, keep_ref,
    normed_t_ref, stage_ref,
):
    side, quarter, me_n = place_ref[1], place_ref[2], place_ref[3]
    rows, width = normed_own_ref.shape
    chunk = grad_hidden_ref.shape[1] // 4
    high = width // 4
    normed_t_ref[:, 0:rows] = normed_own_ref[...].T
    normed_t_ref[:, rows : 2 * rows] = normed_other_ref[...].T
    for index in range(4):
        cols = slice(index * chunk, (index + 1) * chunk)
        expand = dot(normed_t_ref[...], grad_hidden_ref[:, cols]).astype(BF16)
        for other in range(4):
            stage_ref[slot_of(other, quarter, side), order_of(index, me_n), 0:high, :] = (
                expand[other * high : (other + 1) * high, :]
            )
        mixer = (mixer_keep_ref[index].astype(F32) + mixer_recv_ref[index].astype(F32)).astype(BF16)
        block = mixer.shape[0] // 2
        for other in range(4):
            piece = mixer[:, other * high : (other + 1) * high]
            stage_ref[slot_of(index, quarter, side), order_of(other, me_n), high:, :] = jnp.concatenate(
                [piece[0:block, :], piece[block : 2 * block, :]], axis=1
            )
    keep_ref[...] = stage_ref[0:2]
    send_ref[...] = stage_ref[2:4]


def expand_grads(place, normed_own, normed_other, grad_hidden, mixer_keep, mixer_recv):
    rows, width = normed_own.shape
    block = (4, width // 4 + width // 16, grad_hidden.shape[1] // 4)
    out = shape((2, *block), BF16)
    return call(
        expand_grads_kernel,
        [out, out],
        place, normed_own, normed_other, grad_hidden, mixer_keep, mixer_recv,
        scratch=[pltpu.VMEM((width, 2 * rows), BF16), pltpu.VMEM((4, *block), BF16)],
        name="expand_grads",
    )


def triple_grads_kernel(
    place_ref, x0_ref, x1_ref, x2_ref, x3_ref, near_ref, far_ref, normed_ref, grad_triple_ref, sums_in_ref,
    send_ref, keep_ref, sums_ref,
    weight_ref,
):
    me, mine = place_ref[0], place_ref[4]
    rows, width = normed_ref.shape
    part = grad_triple_ref.shape[2]
    gain_sum = jnp.zeros((1, width), F32)
    shift_sum = jnp.zeros((1, width), F32)
    for slot, x_ref in enumerate((x0_ref, x1_ref, x2_ref, x3_ref)):
        unit, _ = unit_rows(x_ref[...].astype(F32))
        grad = (near_ref if slot < 2 else far_ref)[slot % 2].astype(F32)
        gain_sum += column_sum(grad * unit)
        shift_sum += column_sum(grad)
    sums_ref[0:16, :] = sums_in_ref[...]
    sums_ref[16:24, :] = jnp.zeros((8, width), F32)
    sums_ref[SUM_FRONT_GAIN : SUM_FRONT_GAIN + 1, :] = gain_sum
    sums_ref[SUM_FRONT_SHIFT : SUM_FRONT_SHIFT + 1, :] = shift_sum
    group = lax.broadcasted_iota(jnp.int32, (1, width), 1) // part
    for row, index in ((0, 0), (1, 2)):
        bias = column_sum(grad_triple_ref[index].astype(F32))
        sums_ref[SUM_TRIPLE + row : SUM_TRIPLE + row + 1, :] = jnp.where(
            group == me, jnp.concatenate([bias] * (width // part), axis=1), 0.0
        )
    for index in range(3):
        weight_ref[index * part : (index + 1) * part, :] = dot(grad_triple_ref[index], normed_ref[...], TN).astype(BF16)
    piece = 3 * part // 4
    for slot in range(4):
        target = keep_ref if slot < 2 else send_ref
        target[slot % 2] = weight_ref[rows_at(mine ^ slot, piece), :]


def triple_grads(place, shards, near, far, normed, grad_triple, sums):
    rows, width = normed.shape
    part = grad_triple.shape[2]
    out = shape((2, 3 * part // 4, width), BF16)
    return call(
        triple_grads_kernel,
        [out, out, shape((24, width), F32)],
        place, *shards, near, far, normed, grad_triple, sums,
        scratch=[pltpu.VMEM((3 * part, width), BF16)],
        vmem=16,
        name="triple_grads",
    )


def front_kernel(place_ref, x_ref, near_ref, core_ref, pair_ref, grad_middle_ref, vectors_ref, out_ref):
    unit, scale = unit_rows(x_ref[...].astype(F32))
    grad = near_ref[0].astype(F32) + core_ref[0].astype(F32) + pair_ref[...].astype(F32)
    back = norm_pullback(grad, unit, scale, vector(vectors_ref, FRONT_GAIN))
    out_ref[...] = (grad_middle_ref[...] + back).astype(BF16)


def front_part(place, x, *arrays):
    return call(front_kernel, [shape(x.shape, BF16)], place, x, *arrays, name="front_part")[0]


def unpack_triple_kernel(place_ref, own_ref, recv_ref, out_ref):
    stay, mine = place_ref[5], place_ref[6]
    piece = own_ref.shape[1]

    @pl.when(stay == 1)
    def _():
        for slot in range(4):
            out_ref[rows_at(mine ^ slot, piece), :] = own_ref[slot].astype(F32)

    @pl.when(stay == 0)
    def _():
        for slot in range(4):
            out_ref[rows_at(mine ^ slot, piece), :] = recv_ref[slot].astype(F32)


def unpack_triple(place, own, recv):
    _, piece, width = own.shape
    return call(
        unpack_triple_kernel, [shape((4 * piece, width), F32)], place, own, recv, name="unpack_triple"
    )[0]


def swap_block_kernel(place_ref, a_ref, b_ref, c_ref, total_ref, send_ref):
    side = place_ref[1]
    total_ref[...] = a_ref[0].astype(F32) + b_ref[0].astype(F32) + c_ref[...].astype(F32)
    block = send_ref.shape[0]
    send_ref[...] = total_ref[rows_at(1 - side, block), :].astype(BF16)


def swap_block(place, a, b, c, block):
    return call(
        swap_block_kernel,
        [shape(c.shape, F32), shape((block, c.shape[1]), BF16)],
        place, a, b, c,
        name="swap_block",
    )


def unpack_weights_kernel(place_ref, total_ref, recv_ref, expand_ref, mixer_ref):
    side = place_ref[1]
    block, double = expand_ref.shape
    chunk = double // 2
    part = mixer_ref.shape[1]
    mine = total_ref[rows_at(side, block), :]
    other = recv_ref[...].astype(F32)
    first = jnp.full(mine.shape, side, jnp.int32) == 0
    expand_ref[:, 0:chunk] = jnp.where(first, mine, other)
    expand_ref[:, chunk:double] = jnp.where(first, other, mine)
    half = block // 2
    mixer_ref[0:half, :] = total_ref[2 * block :, 0:part]
    mixer_ref[half:block, :] = total_ref[2 * block :, part : 2 * part]


def unpack_weights(place, total, recv, width):
    block, chunk = recv.shape
    return call(
        unpack_weights_kernel,
        [shape((block, 2 * chunk), F32), shape((block, width // 4), F32)],
        place, total, recv,
        name="unpack_weights",
    )


def after(value, *earlier):
    return lax.optimization_barrier((value, earlier))[0]


def body(
    inputs,
    pass_ids,
    front_gain,
    front_shift,
    triple_weight,
    triple_bias,
    mixer_weight,
    mixer_bias,
    back_gain,
    back_shift,
    expand_weight,
    expand_bias,
    reduce_weight,
    reduce_bias,
    pass_table,
    cotangent,
):
    width = inputs.shape[1]
    part = triple_weight.shape[2]
    wide_size, narrow_size = lax.axis_size("wide"), lax.axis_size("narrow")
    low_bits = wide_size.bit_length() - 4
    side_bit, x_bit, y_bit = 1 << low_bits, 2 << low_bits, 4 << low_bits

    wide, narrow = lax.axis_index("wide"), lax.axis_index("narrow")
    c, h, l = wide & 1, narrow >> 1, narrow & 1
    me = 2 * c + l
    top = wide >> low_bits
    side, quarter = top & 1, top >> 1
    x1, y1 = (wide >> 1) & 1, (wide >> 2) & 1
    stay = (c == h).astype(jnp.int32)
    corner = 2 * y1 + x1
    place = jnp.stack(
        [
            me, side, quarter, narrow,
            jnp.where(c == 0, 2 * x1 + y1, corner),
            stay,
            jnp.where(h == 0, 2 * x1 + y1, corner),
            corner,
        ]
    ).astype(jnp.int32)

    def send(name, value, target):
        pairs = []
        for w in range(wide_size):
            for n in range(narrow_size):
                to = target(w, n)
                if to is not None:
                    pairs.append((w * narrow_size + n, to[0] * narrow_size + to[1]))
        with jax.named_scope(name):
            return lax.ppermute(value, AXES, pairs)

    def stays(w, n):
        return (w & 1) == (n >> 1)

    def moved(w, n):
        return (w, n) if stays(w, n) else (w ^ 1, n ^ 2)

    def home(w, n):
        return None if stays(w, n) else (w, n ^ 2)

    def lend(w, n):
        return (w, n ^ 2) if stays(w, n) else None

    def core(w, n):
        return (w ^ 1, n)

    def pair(w, n):
        return (w, n ^ 1)

    def diagonal(w, n):
        return (w ^ 1, n ^ 1)

    def across(w, n):
        return (w, n ^ 2)

    def sided(w, n):
        return (w ^ side_bit, n)

    def first(w, n):
        return (w ^ (y_bit if w & side_bit else x_bit), n)

    def second(w, n):
        return (w ^ (x_bit if w & side_bit else y_bit), n)

    def lent_x(w, n):
        return None if stays(w, n) else (w ^ 2, n)

    def lent_y(w, n):
        return None if stays(w, n) else (w ^ 4, n)

    def triple_first(w, n):
        return (w ^ (4 if w & 1 else 2), n)

    def triple_second(w, n):
        return (w ^ (2 if w & 1 else 4), n)

    def triple_first_stay(w, n):
        return triple_first(w, n) if stays(w, n) else None

    def triple_second_stay(w, n):
        return triple_second(w, n) if stays(w, n) else None

    def core_from_stay(w, n):
        return (w ^ 1, n) if stays(w, n) else None

    def add(*terms):
        return sum(t.astype(F32) for t in terms).astype(BF16)

    together = lax.optimization_barrier

    weight_t = jnp.swapaxes(triple_weight, 1, 2).reshape(3 * part, width)
    piece = 3 * part // 4
    lent = lax.dynamic_slice_in_dim(weight_t, corner * piece, piece)
    vectors = gather_vectors(
        place, front_gain, front_shift, mixer_bias, back_gain, back_shift, reduce_bias, expand_bias, pass_table
    )
    place, lent = together((place, lent))
    p0 = send("lend_weight", lent, lend)
    x0 = send("rows_move", after(inputs, lent), moved)
    ids_other = send("ids_core", pass_ids, core)
    bias = send("bias_move", triple_bias, moved)
    p0, bias, ids_other, vectors = together((p0, bias, ids_other, vectors))
    x1_rows = send("rows_pair", after(x0, p0), pair)
    p1 = send("lent_x", p0, lent_x)
    x1_rows, p1 = together((x1_rows, p1))
    x2 = send("rows_core", x0, core)
    x3 = send("pair_core", x1_rows, core)
    p23 = send("lent_y", jnp.stack([p0, p1]), lent_y)
    cot_own = send("cot_move", after(cotangent, x1_rows), moved)

    shards = (x0, x1_rows, x2, x3)
    m0, m1, m2, m3, mixed_t, normed, triple, weight = attend_forward(
        place, shards, pass_ids, ids_other, vectors, weight_t, (p0, p1, p23), bias
    )
    m1, m2, m3, cot_own = together(
        (send("m_pair", m1, pair), send("m_core", m2, core), send("m_diagonal", m3, diagonal), cot_own)
    )
    cot_other = send("cot_core", cot_own, sided)
    normed_two, middle, mixed_rows = mixer_part(place, (m0, m1, m2, m3), x0, mixer_weight, vectors)
    normed_other, cot_other = together((send("normed_core", normed_two, sided), cot_other))
    second_own, grad_own, feed_send, active, grad_hidden, bias_sums = feed_part(
        place, normed_two, normed_other, cot_own, cot_other, expand_weight, reduce_weight, vectors
    )
    feed_recv = send("feed_core", feed_send, sided)
    reduce_send, reduce_keep = reduce_grads(place, cot_own, cot_other, active)
    grad_own, feed_recv, reduce_send = together((grad_own, feed_recv, reduce_send))
    reduce_first = send("reduce_first", reduce_send, first)
    grad_middle, grad_low, g0, g1, g2, g3 = joint_part(
        place, grad_own, feed_recv, middle, cot_own, mixer_weight, vectors
    )
    g1, g2, g3 = send("g_pair", g1, pair), send("g_core", g2, core), send("g_diagonal", g3, diagonal)
    out_rows, sums, mixer_send, mixer_keep = outer_part(
        place, second_own, grad_own, feed_recv, middle, cot_own, grad_low, mixed_rows, pass_ids, ids_other, vectors,
        bias_sums, seq_rows=pass_ids.shape[1],
    )
    mixer_recv = send("mixer_core", mixer_send, sided)
    expand_send, expand_keep = expand_grads(
        place, normed_two, normed_other, grad_hidden, mixer_keep, mixer_recv
    )
    g1, g2, g3, expand_send, expand_keep, out_rows = together((g1, g2, g3, expand_send, expand_keep, out_rows))
    expand_first = send("expand_first", expand_send, first)
    layer_out = send("out_move", out_rows, moved)
    near, far, grad_triple_rows = attend_backward(
        place, (g0, g1, g2, g3), triple, mixed_t, pass_ids, ids_other, weight
    )

    def halved(keep, first_recv, second_recv):
        return (
            add(keep[0, 0:2], first_recv[0, 0:2], second_recv[0:2]),
            add(keep[0, 2:4], first_recv[0, 2:4], second_recv[2:4]),
        )

    sum_steps = [lambda w, n, bit=1 << i: (w ^ bit, n) for i in range(wide_size.bit_length() - 1)] + [pair, across]

    far, near, grad_triple_rows, reduce_first, layer_out = together(
        (far, near, grad_triple_rows, reduce_first, layer_out)
    )
    far_recv = send("far_core", far, core)
    reduce_second = send("reduce_second", add(reduce_keep[1], reduce_first[1]), second)
    triple_send, triple_keep, all_sums = triple_grads(place, shards, near, far, normed, grad_triple_rows, sums)
    far_recv, triple_send, triple_keep, all_sums, expand_first = together(
        (far_recv, triple_send, triple_keep, all_sums, expand_first)
    )

    triple_recv = send("triple_first", triple_send, triple_first)
    pair_recv = send("near_pair", add(near[1], far_recv[1]), pair)
    sums_recv = send("sums", all_sums, sum_steps[0])
    triple_recv, sums_recv, reduce_second = together((triple_recv, sums_recv, reduce_second))

    triple_next = send("triple_second", add(triple_keep[1], triple_recv[1]), triple_second)
    all_sums = all_sums + sums_recv
    sums_recv = send("sums", all_sums, sum_steps[1])
    reduce_a, reduce_b = halved(reduce_keep, reduce_first, reduce_second)
    reduce_pair = send("reduce_pair", reduce_b, pair)
    expand_second = send("expand_second", add(expand_keep[1], expand_first[1]), second)
    triple_next, sums_recv, pair_recv = together((triple_next, sums_recv, pair_recv))

    all_sums = all_sums + sums_recv
    triple_sum = add(triple_keep[0], triple_recv[0], triple_next)
    bit = 8
    while bit < wide_size:
        triple_sum = add(triple_sum, send("triple_more", triple_sum, lambda w, n, bit=bit: (w ^ bit, n)))
        bit *= 2
    triple_recv = send("triple_home", triple_sum, home)
    for step in sum_steps[2:-2]:
        all_sums = all_sums + send("sums", all_sums, step)
    grad_rows = front_part(place, x0, near, far_recv, pair_recv, grad_middle, vectors)
    grad_inputs = send("rows_home", grad_rows, moved)
    grad_rows, triple_recv, all_sums, reduce_pair = together((grad_rows, triple_recv, all_sums, reduce_pair))

    triple_sum = add(triple_sum, triple_recv)
    triple_recv = send("triple_spread", triple_sum, triple_second_stay)
    sums_recv = send("sums", all_sums, sum_steps[-2])
    reduce_across = send("reduce_across", add(reduce_a[1], reduce_pair[1]), across)
    expand_a, expand_b = halved(expand_keep, expand_first, expand_second)
    expand_pair = send("expand_pair", expand_b, pair)
    triple_recv, sums_recv = together((triple_recv, sums_recv))

    triple_half = jnp.stack([triple_sum, triple_recv])
    triple_recv = send("triple_spread_more", triple_half, triple_first_stay)
    all_sums = all_sums + sums_recv
    sums_recv = send("sums", all_sums, sum_steps[-1])
    triple_recv, sums_recv, expand_pair, reduce_across = together((triple_recv, sums_recv, expand_pair, reduce_across))

    expand_across = send("expand_across", add(expand_a[1], expand_pair[1]), across)
    all_sums = all_sums + sums_recv
    triple_all = jnp.concatenate([triple_half, triple_recv], axis=0)
    triple_recv = send("triple_core", triple_all, core_from_stay)
    total_reduce = reduce_a[0].astype(F32) + reduce_pair[0].astype(F32) + reduce_across.astype(F32)
    grad_triple = unpack_triple(place, triple_all, triple_recv)
    expand_across, grad_triple, total_reduce = together((expand_across, grad_triple, total_reduce))

    total, swap = swap_block(place, expand_a, expand_pair, expand_across, width // 8)
    total_expand, total_mixer = unpack_weights(place, total, send("expand_core", swap, sided), width)
    grad_triple = jnp.swapaxes(grad_triple.reshape(3, part, width), 1, 2)
    if low_bits:
        size = 1 << low_bits
        peers = [[size * i + j for j in range(size)] for i in range(wide_size // size)]
        total_expand, total_reduce, total_mixer = (
            lax.psum_scatter(t, "wide", scatter_dimension=d, axis_index_groups=peers, tiled=True)
            for t, d in ((total_expand, 0), (total_reduce, 1), (total_mixer, 0))
        )
    total_reduce = total_reduce.T
    grad_triple_bias = lax.dynamic_slice_in_dim(all_sums[SUM_TRIPLE : SUM_TRIPLE + 2], narrow * part, part, axis=1)

    return (
        layer_out,
        grad_inputs,
        all_sums[SUM_FRONT_GAIN],
        all_sums[SUM_FRONT_SHIFT],
        grad_triple,
        grad_triple_bias,
        total_mixer,
        all_sums[SUM_MIXER],
        all_sums[SUM_GAIN],
        all_sums[SUM_SHIFT],
        total_expand,
        all_sums[SUM_EXPAND : SUM_EXPAND + 4].reshape(-1),
        total_reduce,
        all_sums[SUM_COT],
        all_sums[0 : pass_table.shape[0]],
    )


def solution(mesh):
    rows = P(AXES, None)
    block = P("wide", "narrow")
    return jax.shard_map(
        body,
        mesh=mesh,
        in_specs=(
            rows, P("wide", None), P(), P(), P(None, None, "narrow"), P(None, "narrow"),
            P(), P(), P(), P(), P(), P(), P(), P(), P(), rows,
        ),
        out_specs=(
            rows, rows, P(), P(), P(None, None, "narrow"), P(None, "narrow"), block,
            P(), P(), P(), block, P(), block, P(), P(),
        ),
        check_vma=False,
    )
```

```python
import math

import jax
import jax.numpy as jnp
from jax import lax
from jax.experimental import pallas as pl
from jax.experimental.pallas import tpu as pltpu
from jax.sharding import PartitionSpec as P


HEAD_DIM = 64
EPSILON = 1e-05
BLOCK = 256
HIDDEN = -1e30
F32 = jnp.float32
BF16 = jnp.bfloat16
MIB = 1024 * 1024
AXES = ("wide", "narrow")
NN = (((1,), (0,)), ((), ()))
NT = (((1,), (1,)), ((), ()))
TN = (((0,), (0,)), ((), ()))
GELU_A = math.sqrt(2.0 / math.pi)
GELU_B = 0.044715
shape = jax.ShapeDtypeStruct

FRONT_GAIN, FRONT_SHIFT, MIXER_BIAS, BACK_GAIN, BACK_SHIFT, REDUCE_BIAS, EXPAND_BIAS, TABLE = 0, 1, 2, 3, 4, 5, 6, 10
SUM_TABLE, SUM_COT, SUM_MIXER, SUM_GAIN, SUM_SHIFT, SUM_EXPAND = 0, 5, 6, 7, 8, 9
SUM_FRONT_GAIN, SUM_FRONT_SHIFT, SUM_TRIPLE = 16, 17, 18
SUMS = 24


def dot(left, right, dims=NN):
    return lax.dot_general(left, right, dims, preferred_element_type=F32)


def whole():
    return pl.BlockSpec(memory_space=pltpu.VMEM)


def call(kernel, outs, *arrays, scratch=(), vmem=12, name=None):
    return pl.pallas_call(
        kernel,
        out_shape=tuple(outs),
        in_specs=[pl.BlockSpec(memory_space=pltpu.SMEM)] + [whole()] * (len(arrays) - 1),
        out_specs=(whole(),) * len(outs),
        scratch_shapes=list(scratch),
        compiler_params=pltpu.CompilerParams(vmem_limit_bytes=vmem * MIB),
        name=name,
    )(*arrays)


def unit_rows(values):
    centred = values - jnp.mean(values, axis=-1, keepdims=True)
    scale = lax.rsqrt(jnp.mean(centred * centred, axis=-1, keepdims=True) + EPSILON)
    return centred * scale, scale


def norm_pullback(grad_out, unit, scale, gain):
    grad_unit = grad_out * gain
    inner = (
        grad_unit
        - jnp.mean(grad_unit, axis=-1, keepdims=True)
        - unit * jnp.mean(grad_unit * unit, axis=-1, keepdims=True)
    )
    return inner * scale


def column_sum(values):
    return jnp.sum(values, axis=0, keepdims=True)


def put_sums(packet_ref, start, sums):
    high = sums.astype(BF16)
    packet_ref[start : start + SUMS, :] = high
    packet_ref[start + SUMS : start + 2 * SUMS, :] = (sums - high.astype(F32)).astype(BF16)


def get_sums(packet_ref, start):
    return packet_ref[start : start + SUMS, :].astype(F32) + packet_ref[start + SUMS : start + 2 * SUMS, :].astype(F32)


def keep_head(block, head, axis):
    place = lax.broadcasted_iota(jnp.int32, block.shape, axis) // HEAD_DIM
    return jnp.where(place == head, block, jnp.zeros_like(block))


def rows_at(index, count):
    return pl.ds(pl.multiple_of(index * count, math.gcd(count, 64)), count)


def vector(vectors_ref, index):
    return vectors_ref[index : index + 1, :]


def pass_ids_of(tail_ref, row_ref, col_ref):
    width = tail_ref.shape[1]
    rows = row_ref.shape[1]
    tail = tail_ref[...].astype(F32)
    row_ref[:, 0:width] = tail[1:2, :]
    row_ref[:, width:rows] = tail[2:3, 0 : rows - width]
    for start in range(0, rows, BLOCK):
        col_ref[start : start + BLOCK, :] = jnp.broadcast_to(row_ref[:, start : start + BLOCK], (128, BLOCK)).T


def visibility(ids_col_ref, ids_row_ref, start, keys):
    seen = ids_col_ref[0:keys, 0:1] <= ids_row_ref[:, start : start + BLOCK]
    key_place = lax.broadcasted_iota(jnp.int32, (keys, BLOCK), 0)
    query_place = lax.broadcasted_iota(jnp.int32, (keys, BLOCK), 1) + start
    return jnp.where(seen & (key_place <= query_place), 0.0, HIDDEN).astype(F32)


def vectors_kernel(place_ref, bias_ref, ids_ref, *refs):
    tail_ref, out_ref, table_ref, long_ref = refs[-1], refs[-2], refs[-3], refs[-4]
    width = out_ref.shape[1]
    out_ref[...] = jnp.zeros_like(out_ref)
    for index, ref in enumerate(refs[:-4]):
        out_ref[index : index + 1, :] = ref[...].astype(F32).reshape(1, width)
    for index in range(long_ref.shape[0] // width):
        part = long_ref[index * width : (index + 1) * width]
        out_ref[EXPAND_BIAS + index : EXPAND_BIAS + index + 1, :] = part.astype(F32).reshape(1, width)
    out_ref[TABLE : TABLE + table_ref.shape[0], :] = table_ref[...].astype(F32)
    ids = ids_ref[...].astype(F32)
    bias = bias_ref[...].astype(F32)
    rest, double = ids.shape[1] - width, 2 * bias.shape[1]
    tail = [
        jnp.concatenate([bias[0:1, :], bias[1:2, :], jnp.zeros((1, width - double), F32)], axis=1),
        ids[:, 0:width],
        jnp.concatenate([ids[:, width:], jnp.zeros((1, width - rest), F32)], axis=1),
        jnp.zeros((13, width), F32),
    ]
    tail_ref[...] = jnp.concatenate(tail, axis=0).astype(BF16)


def gather_vectors(place, bias, ids, *arrays):
    width = arrays[0].shape[0]
    return call(
        vectors_kernel,
        [shape((16, width), F32), shape((16, width), BF16)],
        place, bias, ids, *arrays,
        vmem=4,
        name="gather_vectors",
    )


def attend_forward_kernel(
    place_ref, x0_ref, x1_ref, x2_ref, x3_ref, tail_ref, vectors_ref, weight_own_ref, p0_ref, p1_ref, p2_ref, p3_ref,
    m0_ref, m1_ref, m2_ref, m3_ref, mixed_t_ref, normed_ref, triple_ref, weight_ref,
    ids_row_ref, ids_col_ref, q_t_ref, v_t_ref, bias_t_ref, mixed_ref, straight_ref,
):
    me, stay, corner = place_ref[0], place_ref[5], place_ref[7]
    _, rows, part = triple_ref.shape
    local = x0_ref.shape[0]
    piece = p0_ref.shape[0]
    heads = part // HEAD_DIM
    gain = vector(vectors_ref, FRONT_GAIN)
    shift = vector(vectors_ref, FRONT_SHIFT)
    pass_ids_of(tail_ref, ids_row_ref, ids_col_ref)

    @pl.when(stay == 1)
    def _():
        weight_ref[...] = weight_own_ref[...]

    @pl.when(stay == 0)
    def _():
        for slot, value in enumerate((p0_ref, p1_ref, p2_ref, p3_ref)):
            weight_ref[rows_at(corner ^ slot, piece), :] = value[...]

    straight_ref[...] = weight_ref[...].T
    bias = tail_ref[0:1, 0 : 2 * part].astype(F32)
    for slot, x_ref in enumerate((x0_ref, x1_ref, x2_ref, x3_ref)):
        here = rows_at(me ^ slot, local)
        unit, _ = unit_rows(x_ref[...].astype(F32))
        normed = (unit * gain + shift).astype(BF16)
        normed_ref[here, :] = normed
        q = (dot(normed, straight_ref[:, 0:part]) + bias[:, 0:part]).astype(BF16)
        triple_ref[0, here, :] = q * jnp.asarray(HEAD_DIM**-0.5, BF16)
        triple_ref[1, here, :] = dot(normed, straight_ref[:, part : 2 * part]).astype(BF16)
        triple_ref[2, here, :] = (dot(normed, straight_ref[:, 2 * part : 3 * part]) + bias[:, part : 2 * part]).astype(BF16)

    for start in range(0, rows, BLOCK):
        cols = slice(start, start + BLOCK)
        q_t_ref[:, cols] = triple_ref[0, cols, :].T
        v_t_ref[:, cols] = triple_ref[2, cols, :].T

    mixed_t_ref[part : part + 8, :] = jnp.zeros((8, rows), F32)
    for start in range(0, rows, BLOCK):
        keys = start + BLOCK
        cols = slice(start, keys)
        bias_t_ref[0:keys, :] = visibility(ids_col_ref, ids_row_ref, start, keys)
        for head in range(heads):
            here = slice(head * HEAD_DIM, (head + 1) * HEAD_DIM)
            scores = dot(triple_ref[1, 0:keys, :], keep_head(q_t_ref[:, cols], head, 0)) + bias_t_ref[0:keys, :]
            top = jnp.max(scores, axis=0, keepdims=True)
            weights = jnp.exp(scores - top)
            total = jnp.sum(weights, axis=0, keepdims=True)
            mixed_t_ref[here, cols] = dot(v_t_ref[here, 0:keys], weights.astype(BF16)) / total
            mixed_t_ref[part + head : part + head + 1, cols] = top + jnp.log(total)
        mixed_ref[cols, :] = mixed_t_ref[0:part, cols].T.astype(BF16)
    for slot, out_ref in enumerate((m0_ref, m1_ref, m2_ref, m3_ref)):
        pack_rows(out_ref, mixed_ref, me ^ slot)


def pack_rows(out_ref, rows_ref, index):
    half, part = out_ref.shape[0], out_ref.shape[1] // 2
    out_ref[:, 0:part] = rows_ref[rows_at(2 * index, half), :]
    out_ref[:, part : 2 * part] = rows_ref[rows_at(2 * index + 1, half), :]


def unpack_rows(rows_ref, packed_ref, index):
    half, part = packed_ref.shape[0], packed_ref.shape[1] // 2
    rows_ref[rows_at(2 * index, half), :] = packed_ref[:, 0:part]
    rows_ref[rows_at(2 * index + 1, half), :] = packed_ref[:, part : 2 * part]


def attend_forward(place, shards, tail, vectors, weight, pieces):
    local, width = shards[0].shape
    rows = 4 * local
    part = weight.shape[0] // 3
    return call(
        attend_forward_kernel,
        [shape((local // 2, 2 * part), BF16)] * 4
        + [
            shape((part + 8, rows), F32),
            shape((rows, width), BF16),
            shape((3, rows, part), BF16),
            shape(weight.shape, BF16),
        ],
        place, *shards, tail, vectors, weight, *pieces,
        scratch=[
            pltpu.VMEM((1, rows), F32),
            pltpu.VMEM((rows, 128), F32),
            pltpu.VMEM((part, rows), BF16),
            pltpu.VMEM((part, rows), BF16),
            pltpu.VMEM((rows, BLOCK), F32),
            pltpu.VMEM((rows, part), BF16),
            pltpu.VMEM((width, 3 * part), BF16),
        ],
        vmem=16,
        name="attend_forward",
    )


def attend_backward_kernel(
    place_ref, g0_ref, g1_ref, g2_ref, g3_ref, triple_ref, mixed_t_ref, tail_ref, weight_ref,
    near_ref, far_ref, grad_triple_ref,
    grad_ref, grad_t_ref, delta_ref, grad_q_t_ref, grad_k_ref, grad_v_ref, bias_t_ref,
    ids_row_ref, ids_col_ref, q_t_ref, k_t_ref,
):
    me = place_ref[0]
    _, rows, part = triple_ref.shape
    local = near_ref.shape[1]
    heads = part // HEAD_DIM
    for slot, packed_ref in enumerate((g0_ref, g1_ref, g2_ref, g3_ref)):
        unpack_rows(grad_ref, packed_ref, me ^ slot)
    pass_ids_of(tail_ref, ids_row_ref, ids_col_ref)
    for start in range(0, rows, BLOCK):
        cols = slice(start, start + BLOCK)
        q_t_ref[:, cols] = triple_ref[0, cols, :].T
        k_t_ref[:, cols] = triple_ref[1, cols, :].T
        grad_t = grad_ref[cols, :].T
        grad_t_ref[:, cols] = grad_t
        product = grad_t.astype(F32) * mixed_t_ref[0:part, cols]
        for head in range(heads):
            delta_ref[head : head + 1, cols] = column_sum(product[head * HEAD_DIM : (head + 1) * HEAD_DIM, :])
    grad_k_ref[...] = jnp.zeros_like(grad_k_ref)
    grad_v_ref[...] = jnp.zeros_like(grad_v_ref)
    for start in range(0, rows, BLOCK):
        keys = start + BLOCK
        cols = slice(start, keys)
        bias_t_ref[0:keys, :] = visibility(ids_col_ref, ids_row_ref, start, keys)
        for head in range(heads):
            here = slice(head * HEAD_DIM, (head + 1) * HEAD_DIM)
            scores = dot(triple_ref[1, 0:keys, :], keep_head(q_t_ref[:, cols], head, 0))
            probs = jnp.exp(scores + bias_t_ref[0:keys, :] - mixed_t_ref[part + head : part + head + 1, cols])
            grad_probs = dot(triple_ref[2, 0:keys, :], keep_head(grad_t_ref[:, cols], head, 0))
            grad_scores = (probs * (grad_probs - delta_ref[head : head + 1, cols])).astype(BF16)
            grad_v_ref[0:keys, :] += dot(probs.astype(BF16), keep_head(grad_ref[cols, :], head, 1))
            grad_k_ref[0:keys, :] += dot(grad_scores, keep_head(triple_ref[0, cols, :], head, 1))
            grad_q_t_ref[here, cols] = dot(k_t_ref[here, 0:keys], grad_scores)
    factor = HEAD_DIM**-0.5
    for start in range(0, rows, BLOCK):
        cols = slice(start, start + BLOCK)
        grad_triple_ref[0, cols, :] = (grad_q_t_ref[:, cols].T * factor).astype(BF16)
    grad_triple_ref[1] = grad_k_ref[...].astype(BF16)
    grad_triple_ref[2] = grad_v_ref[...].astype(BF16)
    for slot in range(4):
        here = rows_at(me ^ slot, local)
        target = near_ref if slot < 2 else far_ref
        target[slot % 2] = (
            dot(grad_triple_ref[0, here, :], weight_ref[0:part, :])
            + dot(grad_triple_ref[1, here, :], weight_ref[part : 2 * part, :])
            + dot(grad_triple_ref[2, here, :], weight_ref[2 * part : 3 * part, :])
        ).astype(BF16)


def attend_backward(place, grads, triple, mixed_t, tail, weight):
    _, rows, part = triple.shape
    width = weight.shape[1]
    heads = part // HEAD_DIM
    pair = shape((2, rows // 4, width), BF16)
    return call(
        attend_backward_kernel,
        [pair, pair, shape((3, rows, part), BF16)],
        place, *grads, triple, mixed_t, tail, weight,
        scratch=[
            pltpu.VMEM((rows, part), BF16),
            pltpu.VMEM((part, rows), BF16),
            pltpu.VMEM((heads, rows), F32),
            pltpu.VMEM((part, rows), F32),
            pltpu.VMEM((rows, part), F32),
            pltpu.VMEM((rows, part), F32),
            pltpu.VMEM((rows, BLOCK), F32),
            pltpu.VMEM((1, rows), F32),
            pltpu.VMEM((rows, 128), F32),
            pltpu.VMEM((part, rows), BF16),
            pltpu.VMEM((part, rows), BF16),
        ],
        vmem=16,
        name="attend_backward",
    )


def mixer_kernel(
    place_ref, m0_ref, m1_ref, m2_ref, m3_ref, x_ref, mixer_ref, vectors_ref, _later_ref,
    normed_ref, middle_ref, mixed_ref,
):
    me = place_ref[0]
    half, double = m0_ref.shape
    part = double // 2
    middle = x_ref[...].astype(F32) + vector(vectors_ref, MIXER_BIAS)
    for slot, packed_ref in enumerate((m0_ref, m1_ref, m2_ref, m3_ref)):
        cols = slice(slot * part, (slot + 1) * part)
        mixed_ref[0:half, cols] = packed_ref[:, 0:part]
        mixed_ref[half : 2 * half, cols] = packed_ref[:, part:double]
        middle += dot(mixed_ref[:, cols], mixer_ref[rows_at(me ^ slot, part), :])
    middle_ref[...] = middle
    unit, _ = unit_rows(middle)
    normed_ref[...] = (unit * vector(vectors_ref, BACK_GAIN) + vector(vectors_ref, BACK_SHIFT)).astype(BF16)


def mixer_part(place, packed, x, mixer, vectors, later):
    rows, width = x.shape
    return call(
        mixer_kernel,
        [shape((rows, width), BF16), shape((rows, width), F32), shape((rows, width), BF16)],
        place, *packed, x, mixer, vectors, later,
        name="mixer_part",
    )


def feed_kernel(
    place_ref, normed_own_ref, normed_other_ref, cot_own_ref, cot_other_ref, expand_ref, reduce_ref, vectors_ref,
    second_ref, grad_ref, send_ref, active_ref, grad_hidden_ref, bias_sum_ref,
    total_ref, back_ref,
):
    side = place_ref[1]
    rows = normed_own_ref.shape[0]
    chunk = active_ref.shape[1] // 4
    lane = lax.broadcasted_iota(jnp.int32, (1, 2 * chunk), 1) // chunk
    for index in range(4):
        block = pl.ds(pl.multiple_of((2 * index + side) * chunk, 128), chunk)
        expand = expand_ref[:, block]
        reduce = reduce_ref[block, :]
        bias = vectors_ref[EXPAND_BIAS + index : EXPAND_BIAS + index + 1, pl.ds(pl.multiple_of(side * chunk, 128), chunk)]
        sums = jnp.zeros((1, chunk), F32)
        for part, (normed_ref, cot_ref) in enumerate(((normed_own_ref, cot_own_ref), (normed_other_ref, cot_other_ref))):
            here = slice(part * rows, (part + 1) * rows)
            cols = slice(index * chunk, (index + 1) * chunk)
            hidden = dot(normed_ref[...], expand) + bias
            square = hidden * hidden
            bend = jnp.tanh(GELU_A * hidden * (1.0 + GELU_B * square))
            half = 0.5 * (1.0 + bend)
            active = (hidden * half).astype(BF16)
            active_ref[here, cols] = active
            second = dot(active, reduce)
            slope = half + (0.5 * GELU_A) * hidden * (1.0 - bend * bend) * (1.0 + (3.0 * GELU_B) * square)
            grad_hidden = (dot(cot_ref[...], reduce, NT) * slope).astype(BF16)
            grad_hidden_ref[here, cols] = grad_hidden
            sums += column_sum(grad_hidden.astype(F32))
            back = dot(grad_hidden, expand, NT)
            if index == 0:
                total_ref[here, :] = second
                back_ref[here, :] = back
            else:
                total_ref[here, :] += second
                back_ref[here, :] += back
        bias_sum_ref[index : index + 1, :] = jnp.where(lane == side, jnp.concatenate([sums, sums], axis=1), 0.0)
    second_ref[...] = total_ref[0:rows, :]
    grad_ref[...] = back_ref[0:rows, :]
    send_ref[0] = back_ref[rows : 2 * rows, :].astype(BF16)
    send_ref[1] = total_ref[rows : 2 * rows, :].astype(BF16)


def feed_part(place, normed_own, normed_other, cot_own, cot_other, expand, reduce, vectors):
    rows, width = normed_own.shape
    hidden = expand.shape[1]
    return call(
        feed_kernel,
        [
            shape((rows, width), F32),
            shape((rows, width), F32),
            shape((2, rows, width), BF16),
            shape((2 * rows, hidden // 2), BF16),
            shape((2 * rows, hidden // 2), BF16),
            shape((4, width), F32),
        ],
        place, normed_own, normed_other, cot_own, cot_other, expand, reduce, vectors,
        scratch=[
            pltpu.VMEM((2 * rows, width), F32),
            pltpu.VMEM((2 * rows, width), F32),
        ],
        vmem=16,
        name="feed_part",
    )


def joint_kernel(
    place_ref, grad_own_ref, recv_ref, middle_ref, cot_ref, mixer_ref, vectors_ref,
    grad_middle_ref, grad_low_ref, g0_ref, g1_ref, g2_ref, g3_ref,
):
    me = place_ref[0]
    half, double = g0_ref.shape
    part = double // 2
    grad_normed = grad_own_ref[...] + recv_ref[0].astype(F32)
    unit, scale = unit_rows(middle_ref[...])
    back = norm_pullback(grad_normed, unit, scale, vector(vectors_ref, BACK_GAIN))
    grad_middle = cot_ref[...].astype(F32) + back
    grad_middle_ref[...] = grad_middle
    grad_low = grad_middle.astype(BF16)
    grad_low_ref[...] = grad_low
    for slot, packed_ref in enumerate((g0_ref, g1_ref, g2_ref, g3_ref)):
        grad = dot(grad_low, mixer_ref[rows_at(me ^ slot, part), :], NT).astype(BF16)
        packed_ref[:, 0:part] = grad[0:half, :]
        packed_ref[:, part:double] = grad[half : 2 * half, :]


def joint_part(place, *arrays):
    rows, width = arrays[0].shape
    part = width // 4
    return call(
        joint_kernel,
        [shape((rows, width), F32), shape((rows, width), BF16)] + [shape((rows // 2, 2 * part), BF16)] * 4,
        place, *arrays,
        name="joint_part",
    )


def outer_kernel(
    place_ref, second_ref, grad_own_ref, recv_ref, middle_ref, cot_ref, grad_low_ref, mixed_ref,
    tail_ref, vectors_ref, bias_sum_ref,
    out_ref, sums_ref, mixer_send_ref, mixer_keep_ref,
    total_ref, ids_row_ref, ids_ref,
):
    me, side = place_ref[0], place_ref[1]
    rows = cot_ref.shape[0]
    cot = cot_ref[...].astype(F32)
    unit, _ = unit_rows(middle_ref[...])
    pass_ids_of(tail_ref, ids_row_ref, ids_ref)
    grad_normed = grad_own_ref[...] + recv_ref[0].astype(F32)
    sums_ref[...] = jnp.zeros_like(sums_ref)
    passes = lax.broadcasted_iota(jnp.int32, (rows, 128), 1).astype(F32)
    chosen = (ids_ref[rows_at(me, rows), :] == passes).astype(BF16)
    table = vectors_ref[TABLE : TABLE + 5, :]
    embedded = dot(chosen, jnp.concatenate([table, jnp.zeros((123, table.shape[1]), F32)], axis=0).astype(BF16))
    sums_ref[SUM_TABLE : SUM_TABLE + 5, :] = dot(chosen, cot_ref[...], TN)[0:5, :]
    second = second_ref[...] + recv_ref[1].astype(F32) + vector(vectors_ref, REDUCE_BIAS)
    out_ref[...] = (middle_ref[...] + second + embedded).astype(BF16)
    sums_ref[SUM_COT : SUM_COT + 1, :] = column_sum(cot)
    sums_ref[SUM_MIXER : SUM_MIXER + 1, :] = column_sum(grad_low_ref[...].astype(F32))
    sums_ref[SUM_GAIN : SUM_GAIN + 1, :] = column_sum(grad_normed * unit)
    sums_ref[SUM_SHIFT : SUM_SHIFT + 1, :] = column_sum(grad_normed)
    sums_ref[SUM_EXPAND : SUM_EXPAND + 4, :] = bias_sum_ref[...]
    block = mixer_send_ref.shape[1]
    total_ref[...] = dot(mixed_ref[...], grad_low_ref[...], TN).astype(BF16)
    for slot in range(4):
        mixer_keep_ref[me ^ slot] = total_ref[rows_at(2 * slot + side, block), :]
        mixer_send_ref[me ^ slot] = total_ref[rows_at(2 * slot + (1 - side), block), :]


def outer_part(place, *arrays, seq_rows):
    rows, width = arrays[0].shape
    part = shape((4, width // 8, width), BF16)
    return call(
        outer_kernel,
        [shape((rows, width), BF16), shape((16, width), F32), part, part],
        place, *arrays,
        scratch=[pltpu.VMEM((width, width), BF16), pltpu.VMEM((1, seq_rows), F32), pltpu.VMEM((seq_rows, 128), F32)],
        name="outer_part",
    )


def slot_of(index, quarter, side):
    apart = index ^ quarter
    return jnp.where(side == 0, 2 * (apart & 1) + (apart >> 1), apart)


def order_of(index, me_n):
    apart = index ^ me_n
    return ((apart & 1) << 1) | (apart >> 1)


def reduce_grads_kernel(place_ref, cot_own_ref, cot_other_ref, active_ref, send_ref, keep_ref, cot_t_ref, stage_ref):
    side, quarter, me_n = place_ref[1], place_ref[2], place_ref[3]
    rows, width = cot_own_ref.shape
    chunk = active_ref.shape[1] // 4
    high = width // 4
    cot_t_ref[:, 0:rows] = cot_own_ref[...].T
    cot_t_ref[:, rows : 2 * rows] = cot_other_ref[...].T

    def one_chunk(index, carry):
        cols = pl.ds(pl.multiple_of(index * chunk, 128), chunk)
        reduce = dot(cot_t_ref[...], active_ref[:, cols]).astype(BF16)
        for other in range(4):
            stage_ref[slot_of(index, quarter, side), order_of(other, me_n)] = reduce[other * high : (other + 1) * high, :]
        return carry

    lax.fori_loop(0, 4, one_chunk, 0)
    keep_ref[...] = stage_ref[0:2]
    send_ref[...] = stage_ref[2:4]


def reduce_grads(place, cot_own, cot_other, active):
    rows, width = cot_own.shape
    block = (4, width // 4, active.shape[1] // 4)
    out = shape((2, *block), BF16)
    return call(
        reduce_grads_kernel,
        [out, out],
        place, cot_own, cot_other, active,
        scratch=[pltpu.VMEM((width, 2 * rows), BF16), pltpu.VMEM((4, *block), BF16)],
        name="reduce_grads",
    )


def expand_grads_kernel(
    place_ref, normed_own_ref, normed_other_ref, grad_hidden_ref, mixer_keep_ref, mixer_recv_ref,
    send_ref, keep_ref,
    normed_t_ref, stage_ref,
):
    side, quarter, me_n = place_ref[1], place_ref[2], place_ref[3]
    rows, width = normed_own_ref.shape
    chunk = grad_hidden_ref.shape[1] // 4
    high = width // 4
    normed_t_ref[:, 0:rows] = normed_own_ref[...].T
    normed_t_ref[:, rows : 2 * rows] = normed_other_ref[...].T

    def one_chunk(index, carry):
        cols = pl.ds(pl.multiple_of(index * chunk, 128), chunk)
        expand = dot(normed_t_ref[...], grad_hidden_ref[:, cols]).astype(BF16)
        for other in range(4):
            stage_ref[slot_of(other, quarter, side), order_of(index, me_n), 0:high, :] = (
                expand[other * high : (other + 1) * high, :]
            )
        mixer = (mixer_keep_ref[index].astype(F32) + mixer_recv_ref[index].astype(F32)).astype(BF16)
        block = mixer.shape[0] // 2
        for other in range(4):
            piece = mixer[:, other * high : (other + 1) * high]
            stage_ref[slot_of(index, quarter, side), order_of(other, me_n), high:, :] = jnp.concatenate(
                [piece[0:block, :], piece[block : 2 * block, :]], axis=1
            )
        return carry

    lax.fori_loop(0, 4, one_chunk, 0)
    keep_ref[...] = stage_ref[0:2]
    send_ref[...] = stage_ref[2:4]


def expand_grads(place, normed_own, normed_other, grad_hidden, mixer_keep, mixer_recv):
    rows, width = normed_own.shape
    block = (4, width // 4 + width // 16, grad_hidden.shape[1] // 4)
    out = shape((2, *block), BF16)
    return call(
        expand_grads_kernel,
        [out, out],
        place, normed_own, normed_other, grad_hidden, mixer_keep, mixer_recv,
        scratch=[pltpu.VMEM((width, 2 * rows), BF16), pltpu.VMEM((4, *block), BF16)],
        name="expand_grads",
    )


def triple_grads_kernel(
    place_ref, x0_ref, x1_ref, x2_ref, x3_ref, near_ref, far_ref, normed_ref, grad_triple_ref, sums_in_ref,
    t0_ref, t1_ref, t2_ref, t3_ref, packet_ref, sums_ref,
    weight_ref,
):
    me, corner = place_ref[0], place_ref[7]
    rows, width = normed_ref.shape
    part = grad_triple_ref.shape[2]
    gain_sum = jnp.zeros((1, width), F32)
    shift_sum = jnp.zeros((1, width), F32)
    for slot, x_ref in enumerate((x0_ref, x1_ref, x2_ref, x3_ref)):
        unit, _ = unit_rows(x_ref[...].astype(F32))
        grad = (near_ref if slot < 2 else far_ref)[slot % 2].astype(F32)
        gain_sum += column_sum(grad * unit)
        shift_sum += column_sum(grad)
    sums_ref[0:16, :] = sums_in_ref[...]
    sums_ref[16:24, :] = jnp.zeros((8, width), F32)
    sums_ref[SUM_FRONT_GAIN : SUM_FRONT_GAIN + 1, :] = gain_sum
    sums_ref[SUM_FRONT_SHIFT : SUM_FRONT_SHIFT + 1, :] = shift_sum
    group = lax.broadcasted_iota(jnp.int32, (1, width), 1) // part
    for row, index in ((0, 0), (1, 2)):
        bias = column_sum(grad_triple_ref[index].astype(F32))
        sums_ref[SUM_TRIPLE + row : SUM_TRIPLE + row + 1, :] = jnp.where(
            group == me, jnp.concatenate([bias] * (width // part), axis=1), 0.0
        )
    for index in range(3):
        weight_ref[index * part : (index + 1) * part, :] = dot(grad_triple_ref[index], normed_ref[...], TN).astype(BF16)
    piece = 3 * part // 4
    for slot, target in enumerate((t0_ref, t1_ref, t2_ref, t3_ref)):
        target[...] = weight_ref[rows_at(corner ^ slot, piece), :]
    local = far_ref.shape[1]
    packet_ref[0:local, :] = far_ref[0]
    packet_ref[local : 2 * local, :] = far_ref[1]
    put_sums(packet_ref, 2 * local, sums_ref[...])


def triple_grads(place, shards, near, far, normed, grad_triple, sums):
    rows, width = normed.shape
    part = grad_triple.shape[2]
    return call(
        triple_grads_kernel,
        [shape((3 * part // 4, width), BF16)] * 4
        + [shape((rows // 2 + 2 * SUMS, width), BF16), shape((SUMS, width), F32)],
        place, *shards, near, far, normed, grad_triple, sums,
        scratch=[pltpu.VMEM((3 * part, width), BF16)],
        vmem=16,
        name="triple_grads",
    )


def pair_kernel(place_ref, near_ref, sent_ref, recv_ref, packet_ref, own_ref):
    local = near_ref.shape[1]
    own_ref[...] = near_ref[0].astype(F32) + recv_ref[0:local, :].astype(F32)
    packet_ref[0:local, :] = (near_ref[1].astype(F32) + recv_ref[local : 2 * local, :].astype(F32)).astype(BF16)
    put_sums(packet_ref, local, get_sums(sent_ref, 2 * local) + get_sums(recv_ref, 2 * local))


def pair_part(place, near, sent, recv):
    _, local, width = near.shape
    return call(
        pair_kernel,
        [shape((local + 2 * SUMS, width), BF16), shape((local, width), F32)],
        place, near, sent, recv,
        name="pair_part",
    )


def home_kernel(place_ref, t0_ref, t1_ref, t2_ref, t3_ref, sent_ref, recv_ref, packet_ref):
    piece = t0_ref.shape[0]
    local = sent_ref.shape[0] - 2 * SUMS
    total = t0_ref[...].astype(F32) + t1_ref[...].astype(F32) + t2_ref[...].astype(F32) + t3_ref[...].astype(F32)
    packet_ref[0:piece, :] = total.astype(BF16)
    put_sums(packet_ref, piece, get_sums(sent_ref, local) + get_sums(recv_ref, local))


def home_part(place, pieces, sent, recv):
    piece, width = pieces[0].shape
    return call(
        home_kernel, [shape((piece + 2 * SUMS, width), BF16)], place, *pieces, sent, recv, name="home_part"
    )[0]


def front_kernel(place_ref, x_ref, own_ref, recv_ref, grad_middle_ref, vectors_ref, out_ref):
    unit, scale = unit_rows(x_ref[...].astype(F32))
    grad = own_ref[...] + recv_ref[0 : own_ref.shape[0], :].astype(F32)
    back = norm_pullback(grad, unit, scale, vector(vectors_ref, FRONT_GAIN))
    out_ref[...] = (grad_middle_ref[...] + back).astype(BF16)


def front_part(place, x, *arrays):
    return call(front_kernel, [shape(x.shape, BF16)], place, x, *arrays, name="front_part")[0]


def spread_kernel(place_ref, sent_ref, recv_ref, packet_ref):
    piece = sent_ref.shape[0] - 2 * SUMS
    packet_ref[0:piece, :] = (sent_ref[0:piece, :].astype(F32) + recv_ref[0:piece, :].astype(F32)).astype(BF16)
    put_sums(packet_ref, piece, get_sums(sent_ref, piece) + get_sums(recv_ref, piece))


def spread_part(place, sent, recv):
    return call(spread_kernel, [shape(sent.shape, BF16)], place, sent, recv, name="spread_part")[0]


def last_kernel(place_ref, s0_ref, s1_ref, s2_ref, s3_ref, a_ref, b_ref, c_ref, packet_ref, total_ref):
    side, corner = place_ref[1], place_ref[7]
    piece = s0_ref.shape[0] - 2 * SUMS
    for slot, ref in enumerate((s0_ref, s1_ref, s2_ref, s3_ref)):
        packet_ref[rows_at(corner ^ slot, piece), :] = ref[0:piece, :]
    put_sums(
        packet_ref,
        4 * piece,
        (get_sums(s0_ref, piece) + get_sums(s1_ref, piece)) + (get_sums(s2_ref, piece) + get_sums(s3_ref, piece)),
    )
    total_ref[...] = a_ref[0].astype(F32) + b_ref[0].astype(F32) + c_ref[...].astype(F32)
    half = (packet_ref.shape[0] - 4 * piece - 2 * SUMS)
    chunk = total_ref.shape[1]
    start = 4 * piece + 2 * SUMS
    packet_ref[start:, 0:chunk] = total_ref[rows_at(2 * (1 - side), half), :].astype(BF16)
    packet_ref[start:, chunk : 2 * chunk] = total_ref[rows_at(2 * (1 - side) + 1, half), :].astype(BF16)


def last_part(place, packets, a, b, c):
    rows, width = packets[0].shape
    piece = rows - 2 * SUMS
    block = width // 8
    return call(
        last_kernel,
        [shape((4 * piece + 2 * SUMS + block // 2, width), BF16), shape(c.shape, F32)],
        place, *packets, a, b, c,
        name="last_part",
    )


def results_kernel(
    place_ref, sent_ref, recv_ref, total_ref, ra_ref, rb_ref, rc_ref, layer_ref, rows_ref,
    triple_ref, expand_ref, mixer_ref, reduce_ref, layer_out_ref, rows_out_ref, triple_bias_ref, table_ref,
    front_gain_ref, front_shift_ref, mixer_bias_ref, back_gain_ref, back_shift_ref, expand_bias_ref, reduce_bias_ref,
    sums_ref,
):
    side, me_n, stay = place_ref[1], place_ref[3], place_ref[5]
    layer_out_ref[...] = layer_ref[...]
    rows_out_ref[...] = rows_ref[...]
    weights, width = triple_ref.shape
    part = mixer_ref.shape[1]

    @pl.when(stay == 1)
    def _():
        triple_ref[...] = sent_ref[0:weights, :].astype(F32)
        sums_ref[...] = get_sums(sent_ref, weights)

    @pl.when(stay == 0)
    def _():
        triple_ref[...] = recv_ref[0:weights, :].astype(F32)
        sums_ref[...] = get_sums(recv_ref, weights)

    block, double = expand_ref.shape
    chunk, half = double // 2, block // 2
    start = weights + 2 * SUMS
    for index in range(2):
        mine = total_ref[rows_at(2 * side + index, half), :]
        other = recv_ref[start:, index * chunk : (index + 1) * chunk].astype(F32)
        first = jnp.full(mine.shape, side, jnp.int32) == 0
        here = slice(index * half, (index + 1) * half)
        expand_ref[here, 0:chunk] = jnp.where(first, mine, other)
        expand_ref[here, chunk:double] = jnp.where(first, other, mine)
        mixer_ref[here, :] = total_ref[2 * block :, index * part : (index + 1) * part]
    reduce_ref[...] = ra_ref[0].astype(F32) + rb_ref[0].astype(F32) + rc_ref[...].astype(F32)
    pair = sums_ref[SUM_TRIPLE : SUM_TRIPLE + 2, :]
    bias = jnp.zeros((2, part), F32)
    for group in range(width // part):
        mine = jnp.full(bias.shape, me_n, jnp.int32) == group
        bias = jnp.where(mine, pair[:, group * part : (group + 1) * part], bias)
    triple_bias_ref[...] = bias
    table_ref[...] = sums_ref[SUM_TABLE : SUM_TABLE + table_ref.shape[0], :]
    for index, ref in (
        (SUM_FRONT_GAIN, front_gain_ref), (SUM_FRONT_SHIFT, front_shift_ref), (SUM_MIXER, mixer_bias_ref),
        (SUM_GAIN, back_gain_ref), (SUM_SHIFT, back_shift_ref), (SUM_COT, reduce_bias_ref),
    ):
        ref[...] = sums_ref[index : index + 1, :].reshape(width)
    for index in range(4):
        expand_bias_ref[index * width : (index + 1) * width] = (
            sums_ref[SUM_EXPAND + index : SUM_EXPAND + index + 1, :].reshape(width)
        )


def results(place, sent, recv, total, ra, rb, rc, layer, rows, passes):
    width = sent.shape[1]
    block = width // 8
    piece = (sent.shape[0] - 2 * SUMS - block // 2) // 4
    row = shape((width,), F32)
    return call(
        results_kernel,
        [
            shape((4 * piece, width), F32), shape((block, width), F32), shape((block, width // 4), F32),
            shape(rc.shape, F32), shape(layer.shape, BF16), shape(rows.shape, BF16),
            shape((2, width // 4), F32), shape((passes, width), F32),
            row, row, row, row, row, shape((4 * width,), F32), row,
        ],
        place, sent, recv, total, ra, rb, rc, layer, rows,
        scratch=[pltpu.VMEM((SUMS, width), F32)],
        name="results",
    )


def after(value, *earlier):
    return lax.optimization_barrier((value, earlier))[0]


def body(
    inputs,
    pass_ids,
    front_gain,
    front_shift,
    triple_weight,
    triple_bias,
    mixer_weight,
    mixer_bias,
    back_gain,
    back_shift,
    expand_weight,
    expand_bias,
    reduce_weight,
    reduce_bias,
    pass_table,
    cotangent,
):
    width = inputs.shape[1]
    part = triple_weight.shape[2]
    wide_size, narrow_size = lax.axis_size("wide"), lax.axis_size("narrow")
    low_bits = wide_size.bit_length() - 4
    side_bit, x_bit, y_bit = 1 << low_bits, 2 << low_bits, 4 << low_bits

    wide, narrow = lax.axis_index("wide"), lax.axis_index("narrow")
    c, h, l = wide & 1, narrow >> 1, narrow & 1
    me = 2 * c + l
    top = wide >> low_bits
    side, quarter = top & 1, top >> 1
    x1, y1 = (wide >> 1) & 1, (wide >> 2) & 1
    stay = (c == h).astype(jnp.int32)
    corner = 2 * y1 + x1
    place = jnp.stack(
        [
            me, side, quarter, narrow,
            jnp.where(c == 0, 2 * x1 + y1, corner),
            stay,
            jnp.where(h == 0, 2 * x1 + y1, corner),
            corner,
        ]
    ).astype(jnp.int32)

    def send(name, value, target):
        pairs = []
        for w in range(wide_size):
            for n in range(narrow_size):
                to = target(w, n)
                if to is not None:
                    pairs.append((w * narrow_size + n, to[0] * narrow_size + to[1]))
        with jax.named_scope(name):
            return lax.ppermute(value, AXES, pairs)

    def stays(w, n):
        return (w & 1) == (n >> 1)

    def moved(w, n):
        return (w, n) if stays(w, n) else (w ^ 1, n ^ 2)

    def home(w, n):
        return None if stays(w, n) else (w, n ^ 2)

    def lend(w, n):
        return (w, n ^ 2) if stays(w, n) else None

    def core(w, n):
        return (w ^ 1, n)

    def pair(w, n):
        return (w, n ^ 1)

    def diagonal(w, n):
        return (w ^ 1, n ^ 1)

    def across(w, n):
        return (w, n ^ 2)

    def sided(w, n):
        return (w ^ side_bit, n)

    def first(w, n):
        return (w ^ (y_bit if w & side_bit else x_bit), n)

    def second(w, n):
        return (w ^ (x_bit if w & side_bit else y_bit), n)

    def step_x(w, n):
        return (w ^ 2, n)

    def step_y(w, n):
        return (w ^ 4, n)

    def step_xy(w, n):
        return (w ^ 6, n)

    def of_stay(target):
        return lambda w, n: target(w, n) if stays(w, n) else None

    def of_moved(target):
        return lambda w, n: None if stays(w, n) else target(w, n)

    def add(*terms):
        return sum(t.astype(F32) for t in terms).astype(BF16)

    together = lax.optimization_barrier

    weight_t = jnp.swapaxes(triple_weight, 1, 2).reshape(3 * part, width)
    piece = 3 * part // 4
    lent = lax.dynamic_slice_in_dim(weight_t, corner * piece, piece)
    place, lent = together((place, lent))
    p0 = send("lend_weight", lent, lend)
    x0 = send("rows_move", after(inputs, lent), moved)
    x1_stay = send("rows_pair", inputs, of_stay(pair))
    vectors, tail = gather_vectors(
        place, triple_bias, pass_ids,
        front_gain, front_shift, mixer_bias, back_gain, back_shift, reduce_bias, expand_bias, pass_table,
    )
    tail = send("tail_move", tail, moved)
    x0, p0, x1_stay, vectors, tail = together((x0, p0, x1_stay, vectors, tail))
    x1_moved = send("rows_pair", x0, of_moved(pair))
    p1, p2, p3 = (send("lent", p0, of_moved(step)) for step in (step_x, step_y, step_xy))
    x1_moved, p1, p2, p3 = together((x1_moved, p1, p2, p3))
    x1_rows = jnp.where(stay == 1, x1_stay, x1_moved)
    x2 = send("rows_core", x0, core)
    x3 = send("pair_core", x1_rows, core)
    cot_own = send("cot_move", after(cotangent, x1_rows), moved)

    shards = (x0, x1_rows, x2, x3)
    m0, m1, m2, m3, mixed_t, normed, triple, weight = attend_forward(
        place, shards, tail, vectors, weight_t, (p0, p1, p2, p3)
    )
    m1, m2, m3, cot_own = together(
        (send("m_pair", m1, pair), send("m_core", m2, core), send("m_diagonal", m3, diagonal), cot_own)
    )
    cot_other = send("cot_core", cot_own, sided)
    normed_two, middle, mixed_rows = mixer_part(place, (m0, m1, m2, m3), x0, mixer_weight, vectors, reduce_weight)
    normed_other, cot_other = together((send("normed_core", normed_two, sided), cot_other))
    second_own, grad_own, feed_send, active, grad_hidden, bias_sums = feed_part(
        place, normed_two, normed_other, cot_own, cot_other, expand_weight, reduce_weight, vectors
    )
    feed_recv = send("feed_core", feed_send, sided)
    reduce_send, reduce_keep = reduce_grads(place, cot_own, cot_other, active)
    grad_own, feed_recv, reduce_send = together((grad_own, feed_recv, reduce_send))
    reduce_first = send("reduce_first", reduce_send, first)
    grad_middle, grad_low, g0, g1, g2, g3 = joint_part(
        place, grad_own, feed_recv, middle, cot_own, mixer_weight, vectors
    )
    g1, g2, g3 = send("g_pair", g1, pair), send("g_core", g2, core), send("g_diagonal", g3, diagonal)
    out_rows, sums, mixer_send, mixer_keep = outer_part(
        place, second_own, grad_own, feed_recv, middle, cot_own, grad_low, mixed_rows, tail, vectors, bias_sums,
        seq_rows=pass_ids.shape[1],
    )
    mixer_recv = send("mixer_core", mixer_send, sided)
    expand_send, expand_keep = expand_grads(
        place, normed_two, normed_other, grad_hidden, mixer_keep, mixer_recv
    )
    g1, g2, g3, expand_send, expand_keep, out_rows, reduce_first = together(
        (g1, g2, g3, expand_send, expand_keep, out_rows, reduce_first)
    )
    reduce_second = send("reduce_second", add(reduce_keep[1], reduce_first[1]), second)
    expand_first = send("expand_first", expand_send, first)
    layer_out = send("out_move", out_rows, moved)
    near, far, grad_triple_rows = attend_backward(
        place, (g0, g1, g2, g3), triple, mixed_t, tail, weight
    )

    def halved(keep, first_recv, second_recv):
        return (
            add(keep[0, 0:2], first_recv[0, 0:2], second_recv[0:2]),
            add(keep[0, 2:4], first_recv[0, 2:4], second_recv[2:4]),
        )

    far, near, grad_triple_rows, reduce_second, layer_out = together(
        (far, near, grad_triple_rows, reduce_second, layer_out)
    )
    reduce_a, reduce_b = halved(reduce_keep, reduce_first, reduce_second)
    reduce_pair = send("reduce_pair", reduce_b, pair)
    t0, t1, t2, t3, core_packet, all_sums = triple_grads(place, shards, near, far, normed, grad_triple_rows, sums)
    core_recv, expand_first, reduce_pair = together((send("far_core", core_packet, core), expand_first, reduce_pair))

    pair_packet, own_rows = pair_part(place, near, core_packet, core_recv)
    pair_recv = send("near_pair", pair_packet, pair)
    t1, t2, t3 = send("triple_x", t1, step_x), send("triple_y", t2, step_y), send("triple_xy", t3, step_xy)
    expand_second = send("expand_second", add(expand_keep[1], expand_first[1]), second)
    reduce_across = send("reduce_across", add(reduce_a[1], reduce_pair[1]), across)
    t1, t2, t3, pair_recv, expand_second, reduce_across = together(
        (t1, t2, t3, pair_recv, expand_second, reduce_across)
    )

    home_packet = home_part(place, (t0, t1, t2, t3), pair_packet, pair_recv)
    home_recv = send("triple_home", home_packet, home)
    grad_rows = front_part(place, x0, own_rows, pair_recv, grad_middle, vectors)
    grad_inputs = send("rows_home", grad_rows, moved)
    expand_a, expand_b = halved(expand_keep, expand_first, expand_second)
    expand_pair = send("expand_pair", expand_b, pair)
    home_recv, expand_pair, grad_rows = together((home_recv, expand_pair, grad_rows))

    spread = spread_part(place, home_packet, home_recv)
    s1, s2, s3 = (send("triple_spread", spread, of_stay(step)) for step in (step_x, step_y, step_xy))
    expand_across = send("expand_across", add(expand_a[1], expand_pair[1]), across)
    s1, s2, s3, expand_across, grad_inputs = together((s1, s2, s3, expand_across, grad_inputs))

    last_packet, total = last_part(place, (spread, s1, s2, s3), expand_a, expand_pair, expand_across)
    last_recv = send("last_core", last_packet, core)
    (
        grad_triple, total_expand, total_mixer, total_reduce, layer_out, grad_inputs, grad_triple_bias, grad_table,
        grad_front_gain, grad_front_shift, grad_mixer_bias, grad_back_gain, grad_back_shift, grad_expand_bias,
        grad_reduce_bias,
    ) = results(
        place, last_packet, last_recv, total, reduce_a, reduce_pair, reduce_across, layer_out, grad_inputs,
        pass_table.shape[0],
    )
    grad_triple = jnp.swapaxes(grad_triple.reshape(3, part, width), 1, 2)
    if low_bits:
        size = 1 << low_bits
        peers = [[size * i + j for j in range(size)] for i in range(wide_size // size)]
        total_expand, total_reduce, total_mixer = (
            lax.psum_scatter(t, "wide", scatter_dimension=d, axis_index_groups=peers, tiled=True)
            for t, d in ((total_expand, 0), (total_reduce, 1), (total_mixer, 0))
        )
        peers = [[i + 8 * j for j in range(wide_size // 8)] for i in range(8)]
        (
            grad_triple, grad_triple_bias, grad_table, grad_front_gain, grad_front_shift, grad_mixer_bias,
            grad_back_gain, grad_back_shift, grad_expand_bias, grad_reduce_bias,
        ) = lax.psum(
            (
                grad_triple, grad_triple_bias, grad_table, grad_front_gain, grad_front_shift, grad_mixer_bias,
                grad_back_gain, grad_back_shift, grad_expand_bias, grad_reduce_bias,
            ),
            "wide", axis_index_groups=peers,
        )
    return (
        layer_out,
        grad_inputs,
        grad_front_gain,
        grad_front_shift,
        grad_triple,
        grad_triple_bias,
        total_mixer,
        grad_mixer_bias,
        grad_back_gain,
        grad_back_shift,
        total_expand,
        grad_expand_bias,
        total_reduce.T,
        grad_reduce_bias,
        grad_table,
    )


def solution(mesh):
    rows = P(AXES, None)
    block = P("wide", "narrow")
    return jax.shard_map(
        body,
        mesh=mesh,
        in_specs=(
            rows, P("wide", None), P(), P(), P(None, None, "narrow"), P(None, "narrow"),
            P(), P(), P(), P(), P(), P(), P(), P(), P(), rows,
        ),
        out_specs=(
            rows, rows, P(), P(), P(None, None, "narrow"), P(None, "narrow"), block,
            P(), P(), P(), block, P(), block, P(), P(),
        ),
        check_vma=False,
    )
```

```python
import math

import jax
import jax.numpy as jnp
from jax import lax
from jax.experimental import pallas as pl
from jax.experimental.pallas import tpu as pltpu
from jax.sharding import PartitionSpec as P


HEAD_DIM = 64
EPSILON = 1e-05
BLOCK = 256
LONG_FORWARD, LONG_BACKWARD = 768, 1280
HIDDEN = -1e30
F32 = jnp.float32
BF16 = jnp.bfloat16
MIB = 1024 * 1024
AXES = ("wide", "narrow")
NN = (((1,), (0,)), ((), ()))
NT = (((1,), (1,)), ((), ()))
TN = (((0,), (0,)), ((), ()))
GELU_A = math.sqrt(2.0 / math.pi)
GELU_B = 0.044715
shape = jax.ShapeDtypeStruct

FRONT_GAIN, FRONT_SHIFT, MIXER_BIAS, BACK_GAIN, BACK_SHIFT, REDUCE_BIAS, EXPAND_BIAS, TABLE = 0, 1, 2, 3, 4, 5, 6, 10
SUM_TABLE, SUM_COT, SUM_MIXER, SUM_GAIN, SUM_SHIFT, SUM_EXPAND = 0, 5, 6, 7, 8, 9
SUM_FRONT_GAIN, SUM_FRONT_SHIFT, SUM_TRIPLE = 16, 17, 18
SUMS = 24


def dot(left, right, dims=NN):
    return lax.dot_general(left, right, dims, preferred_element_type=F32)


def whole():
    return pl.BlockSpec(memory_space=pltpu.VMEM)


def call(kernel, outs, *arrays, scratch=(), vmem=12, name=None):
    return pl.pallas_call(
        kernel,
        out_shape=tuple(outs),
        in_specs=[pl.BlockSpec(memory_space=pltpu.SMEM)] + [whole()] * (len(arrays) - 1),
        out_specs=(whole(),) * len(outs),
        scratch_shapes=list(scratch),
        compiler_params=pltpu.CompilerParams(vmem_limit_bytes=vmem * MIB),
        name=name,
    )(*arrays)


def unit_rows(values):
    centred = values - jnp.mean(values, axis=-1, keepdims=True)
    scale = lax.rsqrt(jnp.mean(centred * centred, axis=-1, keepdims=True) + EPSILON)
    return centred * scale, scale


def norm_pullback(grad_out, unit, scale, gain):
    grad_unit = grad_out * gain
    inner = (
        grad_unit
        - jnp.mean(grad_unit, axis=-1, keepdims=True)
        - unit * jnp.mean(grad_unit * unit, axis=-1, keepdims=True)
    )
    return inner * scale


def column_sum(values):
    return jnp.sum(values, axis=0, keepdims=True)


def put_sums(packet_ref, start, sums):
    high = sums.astype(BF16)
    packet_ref[start : start + SUMS, :] = high
    packet_ref[start + SUMS : start + 2 * SUMS, :] = (sums - high.astype(F32)).astype(BF16)


def get_sums(packet_ref, start):
    return packet_ref[start : start + SUMS, :].astype(F32) + packet_ref[start + SUMS : start + 2 * SUMS, :].astype(F32)


def keep_head(block, head, axis):
    place = lax.broadcasted_iota(jnp.int32, block.shape, axis) // HEAD_DIM
    return jnp.where(place == head, block, jnp.zeros_like(block))


def rows_at(index, count):
    if isinstance(index, int):
        return slice(index * count, (index + 1) * count)
    return pl.ds(pl.multiple_of(index * count, math.gcd(count, 64)), count)


def each_head(heads, one_head, looped):
    if looped:
        lax.fori_loop(0, heads, lambda head, carry: one_head(head) or carry, 0)
    else:
        for head in range(heads):
            one_head(head)


def vector(vectors_ref, index):
    return vectors_ref[index : index + 1, :]


def pass_ids_of(tail_ref, row_ref, col_ref):
    width = tail_ref.shape[1]
    rows = row_ref.shape[1]
    tail = tail_ref[...].astype(F32)
    row_ref[:, 0:width] = tail[1:2, :]
    row_ref[:, width:rows] = tail[2:3, 0 : rows - width]
    for start in range(0, rows, BLOCK):
        col_ref[start : start + BLOCK, :] = jnp.broadcast_to(row_ref[:, start : start + BLOCK], (128, BLOCK)).T


def visibility(ids_col_ref, ids_row_ref, start, keys):
    seen = ids_col_ref[0:keys, 0:1] <= ids_row_ref[:, start : start + BLOCK]
    key_place = lax.broadcasted_iota(jnp.int32, (keys, BLOCK), 0)
    query_place = lax.broadcasted_iota(jnp.int32, (keys, BLOCK), 1) + start
    return jnp.where(seen & (key_place <= query_place), 0.0, HIDDEN).astype(F32)


def vectors_kernel(place_ref, bias_ref, ids_ref, *refs):
    tail_ref, out_ref, table_ref, long_ref = refs[-1], refs[-2], refs[-3], refs[-4]
    width = out_ref.shape[1]
    out_ref[...] = jnp.zeros_like(out_ref)
    for index, ref in enumerate(refs[:-4]):
        out_ref[index : index + 1, :] = ref[...].astype(F32).reshape(1, width)
    for index in range(long_ref.shape[0] // width):
        part = long_ref[index * width : (index + 1) * width]
        out_ref[EXPAND_BIAS + index : EXPAND_BIAS + index + 1, :] = part.astype(F32).reshape(1, width)
    out_ref[TABLE : TABLE + table_ref.shape[0], :] = table_ref[...].astype(F32)
    ids = ids_ref[...].astype(F32)
    bias = bias_ref[...].astype(F32)
    rest, double = ids.shape[1] - width, 2 * bias.shape[1]
    tail = [
        jnp.concatenate([bias[0:1, :], bias[1:2, :], jnp.zeros((1, width - double), F32)], axis=1),
        ids[:, 0:width],
        jnp.concatenate([ids[:, width:], jnp.zeros((1, width - rest), F32)], axis=1),
        jnp.zeros((13, width), F32),
    ]
    tail_ref[...] = jnp.concatenate(tail, axis=0).astype(BF16)


def gather_vectors(place, bias, ids, *arrays):
    width = arrays[0].shape[0]
    return call(
        vectors_kernel,
        [shape((16, width), F32), shape((16, width), BF16)],
        place, bias, ids, *arrays,
        vmem=4,
        name="gather_vectors",
    )


def attend_forward_kernel(
    place_ref, x0_ref, x1_ref, x2_ref, x3_ref, tail_ref, vectors_ref, weight_own_ref, p0_ref, p1_ref, p2_ref, p3_ref,
    m0_ref, m1_ref, m2_ref, m3_ref, mixed_t_ref, normed_ref, triple_ref, weight_ref,
    ids_row_ref, ids_col_ref, q_t_ref, v_t_ref, bias_t_ref, mixed_ref, straight_ref,
):
    me, stay, corner = place_ref[0], place_ref[5], place_ref[7]
    _, rows, part = triple_ref.shape
    local = x0_ref.shape[0]
    piece = p0_ref.shape[0]
    heads = part // HEAD_DIM
    gain = vector(vectors_ref, FRONT_GAIN)
    shift = vector(vectors_ref, FRONT_SHIFT)
    pass_ids_of(tail_ref, ids_row_ref, ids_col_ref)

    @pl.when(stay == 1)
    def _():
        weight_ref[...] = weight_own_ref[...]

    @pl.when(stay == 0)
    def _():
        for slot, value in enumerate((p0_ref, p1_ref, p2_ref, p3_ref)):
            weight_ref[rows_at(corner ^ slot, piece), :] = value[...]

    straight_ref[...] = weight_ref[...].T
    bias = tail_ref[0:1, 0 : 2 * part].astype(F32)
    for slot, x_ref in enumerate((x0_ref, x1_ref, x2_ref, x3_ref)):
        here = rows_at(me ^ slot, local)
        unit, _ = unit_rows(x_ref[...].astype(F32))
        normed = (unit * gain + shift).astype(BF16)
        normed_ref[here, :] = normed
        q = (dot(normed, straight_ref[:, 0:part]) + bias[:, 0:part]).astype(BF16)
        triple_ref[0, here, :] = q * jnp.asarray(HEAD_DIM**-0.5, BF16)
        triple_ref[1, here, :] = dot(normed, straight_ref[:, part : 2 * part]).astype(BF16)
        triple_ref[2, here, :] = (dot(normed, straight_ref[:, 2 * part : 3 * part]) + bias[:, part : 2 * part]).astype(BF16)

    for start in range(0, rows, BLOCK):
        cols = slice(start, start + BLOCK)
        q_t_ref[:, cols] = triple_ref[0, cols, :].T
        v_t_ref[:, cols] = triple_ref[2, cols, :].T

    mixed_t_ref[part : part + 8, :] = jnp.zeros((8, rows), F32)
    for start in range(0, rows, BLOCK):
        keys = start + BLOCK
        cols = slice(start, keys)
        bias_t_ref[0:keys, :] = visibility(ids_col_ref, ids_row_ref, start, keys)

        def one_head(head, keys=keys, cols=cols):
            here = rows_at(head, HEAD_DIM)
            scores = dot(triple_ref[1, 0:keys, :], keep_head(q_t_ref[:, cols], head, 0)) + bias_t_ref[0:keys, :]
            top = jnp.max(scores, axis=0, keepdims=True)
            weights = jnp.exp(scores - top)
            total = jnp.sum(weights, axis=0, keepdims=True)
            mixed_t_ref[here, cols] = dot(v_t_ref[here, 0:keys], weights.astype(BF16)) / total
            mixed_t_ref[pl.ds(part + head, 1), cols] = top + jnp.log(total)

        each_head(heads, one_head, keys > LONG_FORWARD)
        mixed_ref[cols, :] = mixed_t_ref[0:part, cols].T.astype(BF16)
    for slot, out_ref in enumerate((m0_ref, m1_ref, m2_ref, m3_ref)):
        pack_rows(out_ref, mixed_ref, me ^ slot)


def pack_rows(out_ref, rows_ref, index):
    half, part = out_ref.shape[0], out_ref.shape[1] // 2
    out_ref[:, 0:part] = rows_ref[rows_at(2 * index, half), :]
    out_ref[:, part : 2 * part] = rows_ref[rows_at(2 * index + 1, half), :]


def unpack_rows(rows_ref, packed_ref, index):
    half, part = packed_ref.shape[0], packed_ref.shape[1] // 2
    rows_ref[rows_at(2 * index, half), :] = packed_ref[:, 0:part]
    rows_ref[rows_at(2 * index + 1, half), :] = packed_ref[:, part : 2 * part]


def attend_forward(place, shards, tail, vectors, weight, pieces):
    local, width = shards[0].shape
    rows = 4 * local
    part = weight.shape[0] // 3
    return call(
        attend_forward_kernel,
        [shape((local // 2, 2 * part), BF16)] * 4
        + [
            shape((part + 8, rows), F32),
            shape((rows, width), BF16),
            shape((3, rows, part), BF16),
            shape(weight.shape, BF16),
        ],
        place, *shards, tail, vectors, weight, *pieces,
        scratch=[
            pltpu.VMEM((1, rows), F32),
            pltpu.VMEM((rows, 128), F32),
            pltpu.VMEM((part, rows), BF16),
            pltpu.VMEM((part, rows), BF16),
            pltpu.VMEM((rows, BLOCK), F32),
            pltpu.VMEM((rows, part), BF16),
            pltpu.VMEM((width, 3 * part), BF16),
        ],
        vmem=16,
        name="attend_forward",
    )


def attend_backward_kernel(
    place_ref, g0_ref, g1_ref, g2_ref, g3_ref, triple_ref, mixed_t_ref, tail_ref, weight_ref,
    near_ref, far_ref, grad_triple_ref,
    grad_ref, grad_t_ref, delta_ref, grad_q_t_ref, grad_k_ref, grad_v_ref, bias_t_ref,
    ids_row_ref, ids_col_ref, q_t_ref, k_t_ref,
):
    me = place_ref[0]
    _, rows, part = triple_ref.shape
    local = near_ref.shape[1]
    heads = part // HEAD_DIM
    for slot, packed_ref in enumerate((g0_ref, g1_ref, g2_ref, g3_ref)):
        unpack_rows(grad_ref, packed_ref, me ^ slot)
    pass_ids_of(tail_ref, ids_row_ref, ids_col_ref)
    for start in range(0, rows, BLOCK):
        cols = slice(start, start + BLOCK)
        q_t_ref[:, cols] = triple_ref[0, cols, :].T
        k_t_ref[:, cols] = triple_ref[1, cols, :].T
        grad_t = grad_ref[cols, :].T
        grad_t_ref[:, cols] = grad_t
        product = grad_t.astype(F32) * mixed_t_ref[0:part, cols]
        for head in range(heads):
            delta_ref[head : head + 1, cols] = column_sum(product[head * HEAD_DIM : (head + 1) * HEAD_DIM, :])
    grad_k_ref[...] = jnp.zeros_like(grad_k_ref)
    grad_v_ref[...] = jnp.zeros_like(grad_v_ref)
    for start in range(0, rows, BLOCK):
        keys = start + BLOCK
        cols = slice(start, keys)
        bias_t_ref[0:keys, :] = visibility(ids_col_ref, ids_row_ref, start, keys)

        def one_head(head, keys=keys, cols=cols):
            here = rows_at(head, HEAD_DIM)
            scores = dot(triple_ref[1, 0:keys, :], keep_head(q_t_ref[:, cols], head, 0))
            probs = jnp.exp(scores + bias_t_ref[0:keys, :] - mixed_t_ref[pl.ds(part + head, 1), cols])
            grad_probs = dot(triple_ref[2, 0:keys, :], keep_head(grad_t_ref[:, cols], head, 0))
            grad_scores = (probs * (grad_probs - delta_ref[pl.ds(head, 1), cols])).astype(BF16)
            grad_v_ref[0:keys, :] += dot(probs.astype(BF16), keep_head(grad_ref[cols, :], head, 1))
            grad_k_ref[0:keys, :] += dot(grad_scores, keep_head(triple_ref[0, cols, :], head, 1))
            grad_q_t_ref[here, cols] = dot(k_t_ref[here, 0:keys], grad_scores)

        each_head(heads, one_head, keys > LONG_BACKWARD)
    factor = HEAD_DIM**-0.5
    for start in range(0, rows, BLOCK):
        cols = slice(start, start + BLOCK)
        grad_triple_ref[0, cols, :] = (grad_q_t_ref[:, cols].T * factor).astype(BF16)
    grad_triple_ref[1] = grad_k_ref[...].astype(BF16)
    grad_triple_ref[2] = grad_v_ref[...].astype(BF16)
    for slot in range(4):
        here = rows_at(me ^ slot, local)
        target = near_ref if slot < 2 else far_ref
        target[slot % 2] = (
            dot(grad_triple_ref[0, here, :], weight_ref[0:part, :])
            + dot(grad_triple_ref[1, here, :], weight_ref[part : 2 * part, :])
            + dot(grad_triple_ref[2, here, :], weight_ref[2 * part : 3 * part, :])
        ).astype(BF16)


def attend_backward(place, grads, triple, mixed_t, tail, weight):
    _, rows, part = triple.shape
    width = weight.shape[1]
    heads = part // HEAD_DIM
    pair = shape((2, rows // 4, width), BF16)
    return call(
        attend_backward_kernel,
        [pair, pair, shape((3, rows, part), BF16)],
        place, *grads, triple, mixed_t, tail, weight,
        scratch=[
            pltpu.VMEM((rows, part), BF16),
            pltpu.VMEM((part, rows), BF16),
            pltpu.VMEM((heads, rows), F32),
            pltpu.VMEM((part, rows), F32),
            pltpu.VMEM((rows, part), F32),
            pltpu.VMEM((rows, part), F32),
            pltpu.VMEM((rows, BLOCK), F32),
            pltpu.VMEM((1, rows), F32),
            pltpu.VMEM((rows, 128), F32),
            pltpu.VMEM((part, rows), BF16),
            pltpu.VMEM((part, rows), BF16),
        ],
        vmem=16,
        name="attend_backward",
    )


def mixer_kernel(
    place_ref, m0_ref, m1_ref, m2_ref, m3_ref, x_ref, mixer_ref, vectors_ref, _later_ref,
    normed_ref, middle_ref, mixed_ref,
):
    me = place_ref[0]
    half, double = m0_ref.shape
    part = double // 2
    middle = x_ref[...].astype(F32) + vector(vectors_ref, MIXER_BIAS)
    for slot, packed_ref in enumerate((m0_ref, m1_ref, m2_ref, m3_ref)):
        cols = slice(slot * part, (slot + 1) * part)
        mixed_ref[0:half, cols] = packed_ref[:, 0:part]
        mixed_ref[half : 2 * half, cols] = packed_ref[:, part:double]
        middle += dot(mixed_ref[:, cols], mixer_ref[rows_at(me ^ slot, part), :])
    middle_ref[...] = middle
    unit, _ = unit_rows(middle)
    normed_ref[...] = (unit * vector(vectors_ref, BACK_GAIN) + vector(vectors_ref, BACK_SHIFT)).astype(BF16)


def mixer_part(place, packed, x, mixer, vectors, later):
    rows, width = x.shape
    return call(
        mixer_kernel,
        [shape((rows, width), BF16), shape((rows, width), F32), shape((rows, width), BF16)],
        place, *packed, x, mixer, vectors, later,
        name="mixer_part",
    )


def feed_kernel(
    place_ref, normed_own_ref, normed_other_ref, cot_own_ref, cot_other_ref, expand_ref, reduce_ref, vectors_ref,
    second_ref, grad_ref, send_ref, active_ref, grad_hidden_ref, bias_sum_ref,
    total_ref, back_ref,
):
    side = place_ref[1]
    rows = normed_own_ref.shape[0]
    chunk = active_ref.shape[1] // 4
    lane = lax.broadcasted_iota(jnp.int32, (1, 2 * chunk), 1) // chunk
    total_ref[...] = jnp.zeros_like(total_ref)
    back_ref[...] = jnp.zeros_like(back_ref)

    def one_chunk(index, carry):
        block = pl.ds(pl.multiple_of((2 * index + side) * chunk, 128), chunk)
        expand = expand_ref[:, block]
        reduce = reduce_ref[block, :]
        bias = vectors_ref[pl.ds(EXPAND_BIAS + index, 1), pl.ds(pl.multiple_of(side * chunk, 128), chunk)]
        sums = jnp.zeros((1, chunk), F32)
        for part, (normed_ref, cot_ref) in enumerate(((normed_own_ref, cot_own_ref), (normed_other_ref, cot_other_ref))):
            here = slice(part * rows, (part + 1) * rows)
            cols = pl.ds(pl.multiple_of(index * chunk, 128), chunk)
            hidden = dot(normed_ref[...], expand) + bias
            square = hidden * hidden
            bend = jnp.tanh(GELU_A * hidden * (1.0 + GELU_B * square))
            half = 0.5 * (1.0 + bend)
            active = (hidden * half).astype(BF16)
            active_ref[here, cols] = active
            total_ref[here, :] += dot(active, reduce)
            slope = half + (0.5 * GELU_A) * hidden * (1.0 - bend * bend) * (1.0 + (3.0 * GELU_B) * square)
            grad_hidden = (dot(cot_ref[...], reduce, NT) * slope).astype(BF16)
            grad_hidden_ref[here, cols] = grad_hidden
            sums += column_sum(grad_hidden.astype(F32))
            back_ref[here, :] += dot(grad_hidden, expand, NT)
        bias_sum_ref[pl.ds(index, 1), :] = jnp.where(lane == side, jnp.concatenate([sums, sums], axis=1), 0.0)
        return carry

    lax.fori_loop(0, 4, one_chunk, 0)
    second_ref[...] = total_ref[0:rows, :]
    grad_ref[...] = back_ref[0:rows, :]
    send_ref[0] = back_ref[rows : 2 * rows, :].astype(BF16)
    send_ref[1] = total_ref[rows : 2 * rows, :].astype(BF16)


def feed_part(place, normed_own, normed_other, cot_own, cot_other, expand, reduce, vectors):
    rows, width = normed_own.shape
    hidden = expand.shape[1]
    return call(
        feed_kernel,
        [
            shape((rows, width), F32),
            shape((rows, width), F32),
            shape((2, rows, width), BF16),
            shape((2 * rows, hidden // 2), BF16),
            shape((2 * rows, hidden // 2), BF16),
            shape((4, width), F32),
        ],
        place, normed_own, normed_other, cot_own, cot_other, expand, reduce, vectors,
        scratch=[
            pltpu.VMEM((2 * rows, width), F32),
            pltpu.VMEM((2 * rows, width), F32),
        ],
        vmem=16,
        name="feed_part",
    )


def joint_kernel(
    place_ref, grad_own_ref, recv_ref, middle_ref, cot_ref, mixer_ref, vectors_ref,
    grad_middle_ref, grad_low_ref, g0_ref, g1_ref, g2_ref, g3_ref,
):
    me = place_ref[0]
    half, double = g0_ref.shape
    part = double // 2
    grad_normed = grad_own_ref[...] + recv_ref[0].astype(F32)
    unit, scale = unit_rows(middle_ref[...])
    back = norm_pullback(grad_normed, unit, scale, vector(vectors_ref, BACK_GAIN))
    grad_middle = cot_ref[...].astype(F32) + back
    grad_middle_ref[...] = grad_middle
    grad_low = grad_middle.astype(BF16)
    grad_low_ref[...] = grad_low
    for slot, packed_ref in enumerate((g0_ref, g1_ref, g2_ref, g3_ref)):
        grad = dot(grad_low, mixer_ref[rows_at(me ^ slot, part), :], NT).astype(BF16)
        packed_ref[:, 0:part] = grad[0:half, :]
        packed_ref[:, part:double] = grad[half : 2 * half, :]


def joint_part(place, *arrays):
    rows, width = arrays[0].shape
    part = width // 4
    return call(
        joint_kernel,
        [shape((rows, width), F32), shape((rows, width), BF16)] + [shape((rows // 2, 2 * part), BF16)] * 4,
        place, *arrays,
        name="joint_part",
    )


def outer_kernel(
    place_ref, second_ref, grad_own_ref, recv_ref, middle_ref, cot_ref, grad_low_ref, mixed_ref,
    tail_ref, vectors_ref, bias_sum_ref,
    out_ref, sums_ref, mixer_send_ref, mixer_keep_ref,
    total_ref, ids_row_ref, ids_ref,
):
    me, side = place_ref[0], place_ref[1]
    rows = cot_ref.shape[0]
    cot = cot_ref[...].astype(F32)
    unit, _ = unit_rows(middle_ref[...])
    pass_ids_of(tail_ref, ids_row_ref, ids_ref)
    grad_normed = grad_own_ref[...] + recv_ref[0].astype(F32)
    sums_ref[...] = jnp.zeros_like(sums_ref)
    passes = lax.broadcasted_iota(jnp.int32, (rows, 128), 1).astype(F32)
    chosen = (ids_ref[rows_at(me, rows), :] == passes).astype(BF16)
    table = vectors_ref[TABLE : TABLE + 5, :]
    embedded = dot(chosen, jnp.concatenate([table, jnp.zeros((123, table.shape[1]), F32)], axis=0).astype(BF16))
    sums_ref[SUM_TABLE : SUM_TABLE + 5, :] = dot(chosen, cot_ref[...], TN)[0:5, :]
    second = second_ref[...] + recv_ref[1].astype(F32) + vector(vectors_ref, REDUCE_BIAS)
    out_ref[...] = (middle_ref[...] + second + embedded).astype(BF16)
    sums_ref[SUM_COT : SUM_COT + 1, :] = column_sum(cot)
    sums_ref[SUM_MIXER : SUM_MIXER + 1, :] = column_sum(grad_low_ref[...].astype(F32))
    sums_ref[SUM_GAIN : SUM_GAIN + 1, :] = column_sum(grad_normed * unit)
    sums_ref[SUM_SHIFT : SUM_SHIFT + 1, :] = column_sum(grad_normed)
    sums_ref[SUM_EXPAND : SUM_EXPAND + 4, :] = bias_sum_ref[...]
    block = mixer_send_ref.shape[1]
    total_ref[...] = dot(mixed_ref[...], grad_low_ref[...], TN).astype(BF16)
    for slot in range(4):
        mixer_keep_ref[me ^ slot] = total_ref[rows_at(2 * slot + side, block), :]
        mixer_send_ref[me ^ slot] = total_ref[rows_at(2 * slot + (1 - side), block), :]


def outer_part(place, *arrays, seq_rows):
    rows, width = arrays[0].shape
    part = shape((4, width // 8, width), BF16)
    return call(
        outer_kernel,
        [shape((rows, width), BF16), shape((16, width), F32), part, part],
        place, *arrays,
        scratch=[pltpu.VMEM((width, width), BF16), pltpu.VMEM((1, seq_rows), F32), pltpu.VMEM((seq_rows, 128), F32)],
        name="outer_part",
    )


def flip(index):
    return ((index & 1) << 1) | (index >> 1)


def quarter_at(slot, quarter, side):
    return quarter ^ jnp.where(side == 0, flip(slot), slot)


def transposed_rows(out_ref, own_ref, other_ref, spare_ref, places):
    rows, width = own_ref.shape
    part = width // 4
    spare_ref[:, 0:rows] = own_ref[...].T
    spare_ref[:, rows : 2 * rows] = other_ref[...].T
    for index, place in enumerate(places):
        out_ref[index * part : (index + 1) * part, :] = spare_ref[rows_at(place, part), :]


def reduce_grads_kernel(place_ref, cot_own_ref, cot_other_ref, active_ref, send_ref, keep_ref, cot_t_ref, spare_ref):
    side, quarter, me_n = place_ref[1], place_ref[2], place_ref[3]
    chunk = active_ref.shape[1] // 4
    part = send_ref.shape[2]
    transposed_rows(cot_t_ref, cot_own_ref, cot_other_ref, spare_ref, [me_n ^ flip(index) for index in range(4)])
    for base, target in ((0, keep_ref), (2, send_ref)):

        def one_slot(step, carry, base=base, target=target):
            cols = pl.ds(pl.multiple_of(quarter_at(base + step, quarter, side) * chunk, 128), chunk)
            reduce = dot(cot_t_ref[...], active_ref[:, cols]).astype(BF16)
            for index in range(4):
                target[step, index] = reduce[index * part : (index + 1) * part, :]
            return carry

        lax.fori_loop(0, 2, one_slot, 0)


def reduce_grads(place, cot_own, cot_other, active):
    rows, width = cot_own.shape
    out = shape((2, 4, width // 4, active.shape[1] // 4), BF16)
    return call(
        reduce_grads_kernel,
        [out, out],
        place, cot_own, cot_other, active,
        scratch=[pltpu.VMEM((width, 2 * rows), BF16), pltpu.VMEM((width, 2 * rows), BF16)],
        name="reduce_grads",
    )


def expand_grads_kernel(
    place_ref, normed_own_ref, normed_other_ref, grad_hidden_ref, mixer_keep_ref, mixer_recv_ref,
    send_ref, keep_ref,
    normed_t_ref, spare_ref,
):
    side, quarter, me_n = place_ref[1], place_ref[2], place_ref[3]
    width = normed_own_ref.shape[1]
    chunk = grad_hidden_ref.shape[1] // 4
    high = width // 4
    quarters = [quarter_at(slot, quarter, side) for slot in range(4)]
    transposed_rows(normed_t_ref, normed_own_ref, normed_other_ref, spare_ref, quarters)

    def one_chunk(index, carry):
        cols = pl.ds(pl.multiple_of((me_n ^ flip(index)) * chunk, 128), chunk)
        expand = dot(normed_t_ref[...], grad_hidden_ref[:, cols]).astype(BF16)
        for slot in range(4):
            target = keep_ref if slot < 2 else send_ref
            target[slot % 2, index, 0:high, :] = expand[slot * high : (slot + 1) * high, :]
        return carry

    lax.fori_loop(0, 4, one_chunk, 0)
    for base, target in ((0, keep_ref), (2, send_ref)):

        def one_slot(step, carry, base=base, target=target):
            place = quarter_at(base + step, quarter, side)
            mixer = (mixer_keep_ref[place].astype(F32) + mixer_recv_ref[place].astype(F32)).astype(BF16)
            block = mixer.shape[0] // 2
            for other in range(4):
                piece = mixer[:, other * high : (other + 1) * high]
                target[step, flip(other ^ me_n), high:, :] = jnp.concatenate(
                    [piece[0:block, :], piece[block : 2 * block, :]], axis=1
                )
            return carry

        lax.fori_loop(0, 2, one_slot, 0)


def expand_grads(place, normed_own, normed_other, grad_hidden, mixer_keep, mixer_recv):
    rows, width = normed_own.shape
    out = shape((2, 4, width // 4 + width // 16, grad_hidden.shape[1] // 4), BF16)
    return call(
        expand_grads_kernel,
        [out, out],
        place, normed_own, normed_other, grad_hidden, mixer_keep, mixer_recv,
        scratch=[pltpu.VMEM((width, 2 * rows), BF16), pltpu.VMEM((width, 2 * rows), BF16)],
        name="expand_grads",
    )


def triple_grads_kernel(
    place_ref, x0_ref, x1_ref, x2_ref, x3_ref, near_ref, far_ref, normed_ref, grad_triple_ref, sums_in_ref,
    t0_ref, t1_ref, t2_ref, t3_ref, packet_ref, sums_ref,
    weight_ref,
):
    me, corner = place_ref[0], place_ref[7]
    rows, width = normed_ref.shape
    part = grad_triple_ref.shape[2]
    def sum_block(step, sums):
        here = rows_at(step, 64)
        gain_sum, shift_sum = sums
        for slot, x_ref in enumerate((x0_ref, x1_ref, x2_ref, x3_ref)):
            unit, _ = unit_rows(x_ref[here, :].astype(F32))
            grad = (near_ref if slot < 2 else far_ref)[slot % 2, here, :].astype(F32)
            gain_sum += (grad * unit).reshape(8, 8, width).sum(axis=0)
            shift_sum += grad.reshape(8, 8, width).sum(axis=0)
        return gain_sum, shift_sum

    gain_sum, shift_sum = lax.fori_loop(
        0, rows // 256, sum_block, (jnp.zeros((8, width), F32), jnp.zeros((8, width), F32))
    )
    gain_sum, shift_sum = column_sum(gain_sum), column_sum(shift_sum)
    sums_ref[0:16, :] = sums_in_ref[...]
    sums_ref[16:24, :] = jnp.zeros((8, width), F32)
    sums_ref[SUM_FRONT_GAIN : SUM_FRONT_GAIN + 1, :] = gain_sum
    sums_ref[SUM_FRONT_SHIFT : SUM_FRONT_SHIFT + 1, :] = shift_sum
    group = lax.broadcasted_iota(jnp.int32, (1, width), 1) // part
    for row, index in ((0, 0), (1, 2)):
        bias = column_sum(grad_triple_ref[index].astype(F32))
        sums_ref[SUM_TRIPLE + row : SUM_TRIPLE + row + 1, :] = jnp.where(
            group == me, jnp.concatenate([bias] * (width // part), axis=1), 0.0
        )
    for index in range(3):
        weight_ref[index * part : (index + 1) * part, :] = dot(grad_triple_ref[index], normed_ref[...], TN).astype(BF16)
    piece = 3 * part // 4
    for slot, target in enumerate((t0_ref, t1_ref, t2_ref, t3_ref)):
        target[...] = weight_ref[rows_at(corner ^ slot, piece), :]
    local = far_ref.shape[1]
    packet_ref[0:local, :] = far_ref[0]
    packet_ref[local : 2 * local, :] = far_ref[1]
    put_sums(packet_ref, 2 * local, sums_ref[...])


def triple_grads(place, shards, near, far, normed, grad_triple, sums):
    rows, width = normed.shape
    part = grad_triple.shape[2]
    return call(
        triple_grads_kernel,
        [shape((3 * part // 4, width), BF16)] * 4
        + [shape((rows // 2 + 2 * SUMS, width), BF16), shape((SUMS, width), F32)],
        place, *shards, near, far, normed, grad_triple, sums,
        scratch=[pltpu.VMEM((3 * part, width), BF16)],
        vmem=16,
        name="triple_grads",
    )


def pair_kernel(place_ref, near_ref, sent_ref, recv_ref, packet_ref, own_ref):
    local = near_ref.shape[1]
    own_ref[...] = near_ref[0].astype(F32) + recv_ref[0:local, :].astype(F32)
    packet_ref[0:local, :] = (near_ref[1].astype(F32) + recv_ref[local : 2 * local, :].astype(F32)).astype(BF16)
    put_sums(packet_ref, local, get_sums(sent_ref, 2 * local) + get_sums(recv_ref, 2 * local))


def pair_part(place, near, sent, recv):
    _, local, width = near.shape
    return call(
        pair_kernel,
        [shape((local + 2 * SUMS, width), BF16), shape((local, width), F32)],
        place, near, sent, recv,
        name="pair_part",
    )


def home_kernel(place_ref, t0_ref, t1_ref, t2_ref, t3_ref, sent_ref, recv_ref, packet_ref):
    piece = t0_ref.shape[0]
    local = sent_ref.shape[0] - 2 * SUMS
    total = t0_ref[...].astype(F32) + t1_ref[...].astype(F32) + t2_ref[...].astype(F32) + t3_ref[...].astype(F32)
    packet_ref[0:piece, :] = total.astype(BF16)
    put_sums(packet_ref, piece, get_sums(sent_ref, local) + get_sums(recv_ref, local))


def home_part(place, pieces, sent, recv):
    piece, width = pieces[0].shape
    return call(
        home_kernel, [shape((piece + 2 * SUMS, width), BF16)], place, *pieces, sent, recv, name="home_part"
    )[0]


def front_kernel(place_ref, x_ref, own_ref, recv_ref, grad_middle_ref, vectors_ref, out_ref):
    unit, scale = unit_rows(x_ref[...].astype(F32))
    grad = own_ref[...] + recv_ref[0 : own_ref.shape[0], :].astype(F32)
    back = norm_pullback(grad, unit, scale, vector(vectors_ref, FRONT_GAIN))
    out_ref[...] = (grad_middle_ref[...] + back).astype(BF16)


def front_part(place, x, *arrays):
    return call(front_kernel, [shape(x.shape, BF16)], place, x, *arrays, name="front_part")[0]


def spread_kernel(place_ref, sent_ref, recv_ref, packet_ref):
    piece = sent_ref.shape[0] - 2 * SUMS
    packet_ref[0:piece, :] = (sent_ref[0:piece, :].astype(F32) + recv_ref[0:piece, :].astype(F32)).astype(BF16)
    put_sums(packet_ref, piece, get_sums(sent_ref, piece) + get_sums(recv_ref, piece))


def spread_part(place, sent, recv):
    return call(spread_kernel, [shape(sent.shape, BF16)], place, sent, recv, name="spread_part")[0]


def last_kernel(place_ref, s0_ref, s1_ref, s2_ref, s3_ref, a_ref, b_ref, c_ref, packet_ref, total_ref):
    side, corner = place_ref[1], place_ref[7]
    piece = s0_ref.shape[0] - 2 * SUMS
    for slot, ref in enumerate((s0_ref, s1_ref, s2_ref, s3_ref)):
        packet_ref[rows_at(corner ^ slot, piece), :] = ref[0:piece, :]
    put_sums(
        packet_ref,
        4 * piece,
        (get_sums(s0_ref, piece) + get_sums(s1_ref, piece)) + (get_sums(s2_ref, piece) + get_sums(s3_ref, piece)),
    )
    total_ref[...] = a_ref[0].astype(F32) + b_ref[0].astype(F32) + c_ref[...].astype(F32)
    half = (packet_ref.shape[0] - 4 * piece - 2 * SUMS)
    chunk = total_ref.shape[1]
    start = 4 * piece + 2 * SUMS
    packet_ref[start:, 0:chunk] = total_ref[rows_at(2 * (1 - side), half), :].astype(BF16)
    packet_ref[start:, chunk : 2 * chunk] = total_ref[rows_at(2 * (1 - side) + 1, half), :].astype(BF16)


def last_part(place, packets, a, b, c):
    rows, width = packets[0].shape
    piece = rows - 2 * SUMS
    block = width // 8
    return call(
        last_kernel,
        [shape((4 * piece + 2 * SUMS + block // 2, width), BF16), shape(c.shape, F32)],
        place, *packets, a, b, c,
        name="last_part",
    )


def results_kernel(
    place_ref, sent_ref, recv_ref, total_ref, ra_ref, rb_ref, rc_ref, layer_ref, rows_ref,
    triple_ref, expand_ref, mixer_ref, reduce_ref, layer_out_ref, rows_out_ref, triple_bias_ref, table_ref,
    front_gain_ref, front_shift_ref, mixer_bias_ref, back_gain_ref, back_shift_ref, expand_bias_ref, reduce_bias_ref,
    sums_ref,
):
    side, me_n, stay = place_ref[1], place_ref[3], place_ref[5]
    layer_out_ref[...] = layer_ref[...]
    rows_out_ref[...] = rows_ref[...]
    weights, width = triple_ref.shape
    part = mixer_ref.shape[1]

    @pl.when(stay == 1)
    def _():
        triple_ref[...] = sent_ref[0:weights, :].astype(F32)
        sums_ref[...] = get_sums(sent_ref, weights)

    @pl.when(stay == 0)
    def _():
        triple_ref[...] = recv_ref[0:weights, :].astype(F32)
        sums_ref[...] = get_sums(recv_ref, weights)

    block, double = expand_ref.shape
    chunk, half = double // 2, block // 2
    start = weights + 2 * SUMS
    for index in range(2):
        mine = total_ref[rows_at(2 * side + index, half), :]
        other = recv_ref[start:, index * chunk : (index + 1) * chunk].astype(F32)
        first = jnp.full(mine.shape, side, jnp.int32) == 0
        here = slice(index * half, (index + 1) * half)
        expand_ref[here, 0:chunk] = jnp.where(first, mine, other)
        expand_ref[here, chunk:double] = jnp.where(first, other, mine)
        mixer_ref[here, :] = total_ref[2 * block :, index * part : (index + 1) * part]
    reduce_ref[...] = ra_ref[0].astype(F32) + rb_ref[0].astype(F32) + rc_ref[...].astype(F32)
    pair = sums_ref[SUM_TRIPLE : SUM_TRIPLE + 2, :]
    bias = jnp.zeros((2, part), F32)
    for group in range(width // part):
        mine = jnp.full(bias.shape, me_n, jnp.int32) == group
        bias = jnp.where(mine, pair[:, group * part : (group + 1) * part], bias)
    triple_bias_ref[...] = bias
    table_ref[...] = sums_ref[SUM_TABLE : SUM_TABLE + table_ref.shape[0], :]
    for index, ref in (
        (SUM_FRONT_GAIN, front_gain_ref), (SUM_FRONT_SHIFT, front_shift_ref), (SUM_MIXER, mixer_bias_ref),
        (SUM_GAIN, back_gain_ref), (SUM_SHIFT, back_shift_ref), (SUM_COT, reduce_bias_ref),
    ):
        ref[...] = sums_ref[index : index + 1, :].reshape(width)
    for index in range(4):
        expand_bias_ref[index * width : (index + 1) * width] = (
            sums_ref[SUM_EXPAND + index : SUM_EXPAND + index + 1, :].reshape(width)
        )


def results(place, sent, recv, total, ra, rb, rc, layer, rows, passes):
    width = sent.shape[1]
    block = width // 8
    piece = (sent.shape[0] - 2 * SUMS - block // 2) // 4
    row = shape((width,), F32)
    return call(
        results_kernel,
        [
            shape((4 * piece, width), F32), shape((block, width), F32), shape((block, width // 4), F32),
            shape(rc.shape, F32), shape(layer.shape, BF16), shape(rows.shape, BF16),
            shape((2, width // 4), F32), shape((passes, width), F32),
            row, row, row, row, row, shape((4 * width,), F32), row,
        ],
        place, sent, recv, total, ra, rb, rc, layer, rows,
        scratch=[pltpu.VMEM((SUMS, width), F32)],
        name="results",
    )


def after(value, *earlier):
    return lax.optimization_barrier((value, earlier))[0]


def body(
    inputs,
    pass_ids,
    front_gain,
    front_shift,
    triple_weight,
    triple_bias,
    mixer_weight,
    mixer_bias,
    back_gain,
    back_shift,
    expand_weight,
    expand_bias,
    reduce_weight,
    reduce_bias,
    pass_table,
    cotangent,
):
    width = inputs.shape[1]
    part = triple_weight.shape[2]
    wide_size, narrow_size = lax.axis_size("wide"), lax.axis_size("narrow")
    low_bits = wide_size.bit_length() - 4
    side_bit, x_bit, y_bit = 1 << low_bits, 2 << low_bits, 4 << low_bits

    wide, narrow = lax.axis_index("wide"), lax.axis_index("narrow")
    c, h, l = wide & 1, narrow >> 1, narrow & 1
    me = 2 * c + l
    top = wide >> low_bits
    side, quarter = top & 1, top >> 1
    x1, y1 = (wide >> 1) & 1, (wide >> 2) & 1
    stay = (c == h).astype(jnp.int32)
    corner = 2 * y1 + x1
    place = jnp.stack(
        [
            me, side, quarter, narrow,
            jnp.where(c == 0, 2 * x1 + y1, corner),
            stay,
            jnp.where(h == 0, 2 * x1 + y1, corner),
            corner,
        ]
    ).astype(jnp.int32)

    def send(name, value, target):
        pairs = []
        for w in range(wide_size):
            for n in range(narrow_size):
                to = target(w, n)
                if to is not None:
                    pairs.append((w * narrow_size + n, to[0] * narrow_size + to[1]))
        with jax.named_scope(name):
            return lax.ppermute(value, AXES, pairs)

    def stays(w, n):
        return (w & 1) == (n >> 1)

    def moved(w, n):
        return (w, n) if stays(w, n) else (w ^ 1, n ^ 2)

    def home(w, n):
        return None if stays(w, n) else (w, n ^ 2)

    def lend(w, n):
        return (w, n ^ 2) if stays(w, n) else None

    def core(w, n):
        return (w ^ 1, n)

    def pair(w, n):
        return (w, n ^ 1)

    def diagonal(w, n):
        return (w ^ 1, n ^ 1)

    def across(w, n):
        return (w, n ^ 2)

    def sided(w, n):
        return (w ^ side_bit, n)

    def first(w, n):
        return (w ^ (y_bit if w & side_bit else x_bit), n)

    def second(w, n):
        return (w ^ (x_bit if w & side_bit else y_bit), n)

    def step_x(w, n):
        return (w ^ 2, n)

    def step_y(w, n):
        return (w ^ 4, n)

    def step_xy(w, n):
        return (w ^ 6, n)

    def of_stay(target):
        return lambda w, n: target(w, n) if stays(w, n) else None

    def of_moved(target):
        return lambda w, n: None if stays(w, n) else target(w, n)

    def add(*terms):
        return sum(t.astype(F32) for t in terms).astype(BF16)

    together = lax.optimization_barrier

    weight_t = jnp.swapaxes(triple_weight, 1, 2).reshape(3 * part, width)
    piece = 3 * part // 4
    lent = lax.dynamic_slice_in_dim(weight_t, corner * piece, piece)
    place, lent = together((place, lent))
    p0 = send("lend_weight", lent, lend)
    x0 = send("rows_move", after(inputs, lent), moved)
    x1_stay = send("rows_pair", inputs, of_stay(pair))
    vectors, tail = gather_vectors(
        place, triple_bias, pass_ids,
        front_gain, front_shift, mixer_bias, back_gain, back_shift, reduce_bias, expand_bias, pass_table,
    )
    tail = send("tail_move", tail, moved)
    x0, p0, x1_stay, vectors, tail = together((x0, p0, x1_stay, vectors, tail))
    x1_moved = send("rows_pair", x0, of_moved(pair))
    p1, p2, p3 = (send("lent", p0, of_moved(step)) for step in (step_x, step_y, step_xy))
    x1_moved, p1, p2, p3 = together((x1_moved, p1, p2, p3))
    x1_rows = jnp.where(stay == 1, x1_stay, x1_moved)
    x2 = send("rows_core", x0, core)
    x3 = send("pair_core", x1_rows, core)
    cot_own = send("cot_move", after(cotangent, x1_rows), moved)

    shards = (x0, x1_rows, x2, x3)
    m0, m1, m2, m3, mixed_t, normed, triple, weight = attend_forward(
        place, shards, tail, vectors, weight_t, (p0, p1, p2, p3)
    )
    m1, m2, m3, cot_own = together(
        (send("m_pair", m1, pair), send("m_core", m2, core), send("m_diagonal", m3, diagonal), cot_own)
    )
    cot_other = send("cot_core", cot_own, sided)
    normed_two, middle, mixed_rows = mixer_part(place, (m0, m1, m2, m3), x0, mixer_weight, vectors, reduce_weight)
    normed_other, cot_other = together((send("normed_core", normed_two, sided), cot_other))
    second_own, grad_own, feed_send, active, grad_hidden, bias_sums = feed_part(
        place, normed_two, normed_other, cot_own, cot_other, expand_weight, reduce_weight, vectors
    )
    feed_recv = send("feed_core", feed_send, sided)
    reduce_send, reduce_keep = reduce_grads(place, cot_own, cot_other, active)
    grad_own, feed_recv, reduce_send = together((grad_own, feed_recv, reduce_send))
    reduce_first = send("reduce_first", reduce_send, first)
    grad_middle, grad_low, g0, g1, g2, g3 = joint_part(
        place, grad_own, feed_recv, middle, cot_own, mixer_weight, vectors
    )
    g1, g2, g3 = send("g_pair", g1, pair), send("g_core", g2, core), send("g_diagonal", g3, diagonal)
    out_rows, sums, mixer_send, mixer_keep = outer_part(
        place, second_own, grad_own, feed_recv, middle, cot_own, grad_low, mixed_rows, tail, vectors, bias_sums,
        seq_rows=pass_ids.shape[1],
    )
    mixer_recv = send("mixer_core", mixer_send, sided)
    expand_send, expand_keep = expand_grads(
        place, normed_two, normed_other, grad_hidden, mixer_keep, mixer_recv
    )
    g1, g2, g3, expand_send, expand_keep, out_rows, reduce_first = together(
        (g1, g2, g3, expand_send, expand_keep, out_rows, reduce_first)
    )
    reduce_second = send("reduce_second", add(reduce_keep[1], reduce_first[1]), second)
    expand_first = send("expand_first", expand_send, first)
    layer_out = send("out_move", out_rows, moved)
    near, far, grad_triple_rows = attend_backward(
        place, (g0, g1, g2, g3), triple, mixed_t, tail, weight
    )

    def halved(keep, first_recv, second_recv):
        return (
            add(keep[0, 0:2], first_recv[0, 0:2], second_recv[0:2]),
            add(keep[0, 2:4], first_recv[0, 2:4], second_recv[2:4]),
        )

    far, near, grad_triple_rows, reduce_second, layer_out = together(
        (far, near, grad_triple_rows, reduce_second, layer_out)
    )
    reduce_a, reduce_b = halved(reduce_keep, reduce_first, reduce_second)
    reduce_pair = send("reduce_pair", reduce_b, pair)
    t0, t1, t2, t3, core_packet, all_sums = triple_grads(place, shards, near, far, normed, grad_triple_rows, sums)
    core_recv, expand_first, reduce_pair = together((send("far_core", core_packet, core), expand_first, reduce_pair))

    pair_packet, own_rows = pair_part(place, near, core_packet, core_recv)
    pair_recv = send("near_pair", pair_packet, pair)
    t1, t2, t3 = send("triple_x", t1, step_x), send("triple_y", t2, step_y), send("triple_xy", t3, step_xy)
    expand_second = send("expand_second", add(expand_keep[1], expand_first[1]), second)
    reduce_across = send("reduce_across", add(reduce_a[1], reduce_pair[1]), across)
    t1, t2, t3, pair_recv, expand_second, reduce_across = together(
        (t1, t2, t3, pair_recv, expand_second, reduce_across)
    )

    home_packet = home_part(place, (t0, t1, t2, t3), pair_packet, pair_recv)
    home_recv = send("triple_home", home_packet, home)
    grad_rows = front_part(place, x0, own_rows, pair_recv, grad_middle, vectors)
    grad_inputs = send("rows_home", grad_rows, moved)
    expand_a, expand_b = halved(expand_keep, expand_first, expand_second)
    expand_pair = send("expand_pair", expand_b, pair)
    home_recv, expand_pair, grad_rows = together((home_recv, expand_pair, grad_rows))

    spread = spread_part(place, home_packet, home_recv)
    s1, s2, s3 = (send("triple_spread", spread, of_stay(step)) for step in (step_x, step_y, step_xy))
    expand_across = send("expand_across", add(expand_a[1], expand_pair[1]), across)
    s1, s2, s3, expand_across, grad_inputs = together((s1, s2, s3, expand_across, grad_inputs))

    last_packet, total = last_part(place, (spread, s1, s2, s3), expand_a, expand_pair, expand_across)
    last_recv = send("last_core", last_packet, core)
    (
        grad_triple, total_expand, total_mixer, total_reduce, layer_out, grad_inputs, grad_triple_bias, grad_table,
        grad_front_gain, grad_front_shift, grad_mixer_bias, grad_back_gain, grad_back_shift, grad_expand_bias,
        grad_reduce_bias,
    ) = results(
        place, last_packet, last_recv, total, reduce_a, reduce_pair, reduce_across, layer_out, grad_inputs,
        pass_table.shape[0],
    )
    grad_triple = jnp.swapaxes(grad_triple.reshape(3, part, width), 1, 2)
    if low_bits:
        size = 1 << low_bits
        peers = [[size * i + j for j in range(size)] for i in range(wide_size // size)]
        total_expand, total_reduce, total_mixer = (
            lax.psum_scatter(t, "wide", scatter_dimension=d, axis_index_groups=peers, tiled=True)
            for t, d in ((total_expand, 0), (total_reduce, 1), (total_mixer, 0))
        )
        peers = [[i + 8 * j for j in range(wide_size // 8)] for i in range(8)]
        (
            grad_triple, grad_triple_bias, grad_table, grad_front_gain, grad_front_shift, grad_mixer_bias,
            grad_back_gain, grad_back_shift, grad_expand_bias, grad_reduce_bias,
        ) = lax.psum(
            (
                grad_triple, grad_triple_bias, grad_table, grad_front_gain, grad_front_shift, grad_mixer_bias,
                grad_back_gain, grad_back_shift, grad_expand_bias, grad_reduce_bias,
            ),
            "wide", axis_index_groups=peers,
        )
    return (
        layer_out,
        grad_inputs,
        grad_front_gain,
        grad_front_shift,
        grad_triple,
        grad_triple_bias,
        total_mixer,
        grad_mixer_bias,
        grad_back_gain,
        grad_back_shift,
        total_expand,
        grad_expand_bias,
        total_reduce.T,
        grad_reduce_bias,
        grad_table,
    )


def solution(mesh):
    rows = P(AXES, None)
    block = P("wide", "narrow")
    return jax.shard_map(
        body,
        mesh=mesh,
        in_specs=(
            rows, P("wide", None), P(), P(), P(None, None, "narrow"), P(None, "narrow"),
            P(), P(), P(), P(), P(), P(), P(), P(), P(), rows,
        ),
        out_specs=(
            rows, rows, P(), P(), P(None, None, "narrow"), P(None, "narrow"), block,
            P(), P(), P(), block, P(), block, P(), P(),
        ),
        check_vma=False,
    )
```

```python
import math

import jax
import jax.numpy as jnp
from jax import lax
from jax.experimental import pallas as pl
from jax.experimental.pallas import tpu as pltpu
from jax.sharding import PartitionSpec as P


HEAD_DIM = 64
EPSILON = 1e-05
BLOCK = 256
LONG_FORWARD, LONG_BACKWARD = 768, 1280
HIDDEN = -1e30
F32 = jnp.float32
BF16 = jnp.bfloat16
MIB = 1024 * 1024
AXES = ("wide", "narrow")
NN = (((1,), (0,)), ((), ()))
NT = (((1,), (1,)), ((), ()))
TN = (((0,), (0,)), ((), ()))
GELU_A = math.sqrt(2.0 / math.pi)
GELU_B = 0.044715
shape = jax.ShapeDtypeStruct

FRONT_GAIN, FRONT_SHIFT, MIXER_BIAS, BACK_GAIN, BACK_SHIFT, REDUCE_BIAS, EXPAND_BIAS, TABLE = 0, 1, 2, 3, 4, 5, 6, 10
SUM_TABLE, SUM_COT, SUM_MIXER, SUM_GAIN, SUM_SHIFT, SUM_EXPAND = 0, 5, 6, 7, 8, 9
SUM_FRONT_GAIN, SUM_FRONT_SHIFT, SUM_TRIPLE = 16, 17, 18
SUMS = 24


def dot(left, right, dims=NN):
    return lax.dot_general(left, right, dims, preferred_element_type=F32)


def whole():
    return pl.BlockSpec(memory_space=pltpu.VMEM)


def call(kernel, outs, *arrays, scratch=(), vmem=12, name=None):
    return pl.pallas_call(
        kernel,
        out_shape=tuple(outs),
        in_specs=[pl.BlockSpec(memory_space=pltpu.SMEM)] + [whole()] * (len(arrays) - 1),
        out_specs=(whole(),) * len(outs),
        scratch_shapes=list(scratch),
        compiler_params=pltpu.CompilerParams(vmem_limit_bytes=vmem * MIB),
        name=name,
    )(*arrays)


def unit_rows(values):
    centred = values - jnp.mean(values, axis=-1, keepdims=True)
    scale = lax.rsqrt(jnp.mean(centred * centred, axis=-1, keepdims=True) + EPSILON)
    return centred * scale, scale


def norm_pullback(grad_out, unit, scale, gain):
    grad_unit = grad_out * gain
    inner = (
        grad_unit
        - jnp.mean(grad_unit, axis=-1, keepdims=True)
        - unit * jnp.mean(grad_unit * unit, axis=-1, keepdims=True)
    )
    return inner * scale


def column_sum(values):
    return jnp.sum(values, axis=0, keepdims=True)


def put_sums(packet_ref, start, sums):
    high = sums.astype(BF16)
    packet_ref[start : start + SUMS, :] = high
    packet_ref[start + SUMS : start + 2 * SUMS, :] = (sums - high.astype(F32)).astype(BF16)


def get_sums(packet_ref, start):
    return packet_ref[start : start + SUMS, :].astype(F32) + packet_ref[start + SUMS : start + 2 * SUMS, :].astype(F32)


def keep_head(block, head, axis):
    place = lax.broadcasted_iota(jnp.int32, block.shape, axis) // HEAD_DIM
    return jnp.where(place == head, block, jnp.zeros_like(block))


def rows_at(index, count):
    if isinstance(index, int):
        return slice(index * count, (index + 1) * count)
    return pl.ds(pl.multiple_of(index * count, math.gcd(count, 64)), count)


def each_head(heads, one_head, looped):
    if looped:
        lax.fori_loop(0, heads, lambda head, carry: one_head(head) or carry, 0)
    else:
        for head in range(heads):
            one_head(head)


def vector(vectors_ref, index):
    return vectors_ref[index : index + 1, :]


def pass_ids_of(tail_ref, row_ref, col_ref):
    width = tail_ref.shape[1]
    rows = row_ref.shape[1]
    tail = tail_ref[...].astype(F32)
    row_ref[:, 0:width] = tail[1:2, :]
    row_ref[:, width:rows] = tail[2:3, 0 : rows - width]
    for start in range(0, rows, BLOCK):
        col_ref[start : start + BLOCK, :] = jnp.broadcast_to(row_ref[:, start : start + BLOCK], (128, BLOCK)).T


def visibility(ids_col_ref, ids_row_ref, start, keys):
    seen = ids_col_ref[0:keys, 0:1] <= ids_row_ref[:, start : start + BLOCK]
    key_place = lax.broadcasted_iota(jnp.int32, (keys, BLOCK), 0)
    query_place = lax.broadcasted_iota(jnp.int32, (keys, BLOCK), 1) + start
    return jnp.where(seen & (key_place <= query_place), 0.0, HIDDEN).astype(F32)


def vectors_kernel(place_ref, bias_ref, ids_ref, *refs):
    tail_ref, out_ref, table_ref, long_ref = refs[-1], refs[-2], refs[-3], refs[-4]
    width = out_ref.shape[1]
    out_ref[...] = jnp.zeros_like(out_ref)
    for index, ref in enumerate(refs[:-4]):
        out_ref[index : index + 1, :] = ref[...].astype(F32).reshape(1, width)
    for index in range(long_ref.shape[0] // width):
        part = long_ref[index * width : (index + 1) * width]
        out_ref[EXPAND_BIAS + index : EXPAND_BIAS + index + 1, :] = part.astype(F32).reshape(1, width)
    out_ref[TABLE : TABLE + table_ref.shape[0], :] = table_ref[...].astype(F32)
    ids = ids_ref[...].astype(F32)
    bias = bias_ref[...].astype(F32)
    rest, double = ids.shape[1] - width, 2 * bias.shape[1]
    tail = [
        jnp.concatenate([bias[0:1, :], bias[1:2, :], jnp.zeros((1, width - double), F32)], axis=1),
        ids[:, 0:width],
        jnp.concatenate([ids[:, width:], jnp.zeros((1, width - rest), F32)], axis=1),
        jnp.zeros((13, width), F32),
    ]
    tail_ref[...] = jnp.concatenate(tail, axis=0).astype(BF16)


def gather_vectors(place, bias, ids, *arrays):
    width = arrays[0].shape[0]
    return call(
        vectors_kernel,
        [shape((16, width), F32), shape((16, width), BF16)],
        place, bias, ids, *arrays,
        vmem=4,
        name="gather_vectors",
    )


def attend_forward_kernel(
    place_ref, x0_ref, x1_ref, x2_ref, x3_ref, tail_ref, vectors_ref, weight_own_ref, p0_ref, p1_ref, p2_ref, p3_ref,
    m0_ref, m1_ref, m2_ref, m3_ref, mixed_t_ref, normed_ref, triple_ref, weight_ref,
    ids_row_ref, ids_col_ref, q_t_ref, v_t_ref, bias_t_ref, mixed_ref, straight_ref,
):
    me, stay, corner = place_ref[0], place_ref[5], place_ref[7]
    _, rows, part = triple_ref.shape
    local = x0_ref.shape[0]
    piece = p0_ref.shape[0]
    heads = part // HEAD_DIM
    gain = vector(vectors_ref, FRONT_GAIN)
    shift = vector(vectors_ref, FRONT_SHIFT)
    pass_ids_of(tail_ref, ids_row_ref, ids_col_ref)

    @pl.when(stay == 1)
    def _():
        weight_ref[...] = weight_own_ref[...]

    @pl.when(stay == 0)
    def _():
        for slot, value in enumerate((p0_ref, p1_ref, p2_ref, p3_ref)):
            weight_ref[rows_at(corner ^ slot, piece), :] = value[...]

    straight_ref[...] = weight_ref[...].T
    bias = tail_ref[0:1, 0 : 2 * part].astype(F32)
    for slot, x_ref in enumerate((x0_ref, x1_ref, x2_ref, x3_ref)):
        here = rows_at(me ^ slot, local)
        unit, _ = unit_rows(x_ref[...].astype(F32))
        normed = (unit * gain + shift).astype(BF16)
        normed_ref[here, :] = normed
        q = (dot(normed, straight_ref[:, 0:part]) + bias[:, 0:part]).astype(BF16)
        triple_ref[0, here, :] = q * jnp.asarray(HEAD_DIM**-0.5, BF16)
        triple_ref[1, here, :] = dot(normed, straight_ref[:, part : 2 * part]).astype(BF16)
        triple_ref[2, here, :] = (dot(normed, straight_ref[:, 2 * part : 3 * part]) + bias[:, part : 2 * part]).astype(BF16)

    for start in range(0, rows, BLOCK):
        cols = slice(start, start + BLOCK)
        q_t_ref[:, cols] = triple_ref[0, cols, :].T
        v_t_ref[:, cols] = triple_ref[2, cols, :].T

    mixed_t_ref[part : part + 8, :] = jnp.zeros((8, rows), F32)
    for start in range(0, rows, BLOCK):
        keys = start + BLOCK
        cols = slice(start, keys)
        bias_t_ref[0:keys, :] = visibility(ids_col_ref, ids_row_ref, start, keys)

        def one_head(head, keys=keys, cols=cols):
            here = rows_at(head, HEAD_DIM)
            scores = dot(triple_ref[1, 0:keys, :], keep_head(q_t_ref[:, cols], head, 0)) + bias_t_ref[0:keys, :]
            top = jnp.max(scores, axis=0, keepdims=True)
            weights = jnp.exp(scores - top)
            total = jnp.sum(weights, axis=0, keepdims=True)
            mixed_t_ref[here, cols] = dot(v_t_ref[here, 0:keys], weights.astype(BF16)) / total
            mixed_t_ref[pl.ds(part + head, 1), cols] = top + jnp.log(total)

        each_head(heads, one_head, keys > LONG_FORWARD)
        mixed_ref[cols, :] = mixed_t_ref[0:part, cols].T.astype(BF16)
    for slot, out_ref in enumerate((m0_ref, m1_ref, m2_ref, m3_ref)):
        pack_rows(out_ref, mixed_ref, me ^ slot)


def pack_rows(out_ref, rows_ref, index):
    half, part = out_ref.shape[0], out_ref.shape[1] // 2
    out_ref[:, 0:part] = rows_ref[rows_at(2 * index, half), :]
    out_ref[:, part : 2 * part] = rows_ref[rows_at(2 * index + 1, half), :]


def unpack_rows(rows_ref, packed_ref, index):
    half, part = packed_ref.shape[0], packed_ref.shape[1] // 2
    rows_ref[rows_at(2 * index, half), :] = packed_ref[:, 0:part]
    rows_ref[rows_at(2 * index + 1, half), :] = packed_ref[:, part : 2 * part]


def attend_forward(place, shards, tail, vectors, weight, pieces):
    local, width = shards[0].shape
    rows = 4 * local
    part = weight.shape[0] // 3
    return call(
        attend_forward_kernel,
        [shape((local // 2, 2 * part), BF16)] * 4
        + [
            shape((part + 8, rows), F32),
            shape((rows, width), BF16),
            shape((3, rows, part), BF16),
            shape(weight.shape, BF16),
        ],
        place, *shards, tail, vectors, weight, *pieces,
        scratch=[
            pltpu.VMEM((1, rows), F32),
            pltpu.VMEM((rows, 128), F32),
            pltpu.VMEM((part, rows), BF16),
            pltpu.VMEM((part, rows), BF16),
            pltpu.VMEM((rows, BLOCK), F32),
            pltpu.VMEM((rows, part), BF16),
            pltpu.VMEM((width, 3 * part), BF16),
        ],
        vmem=16,
        name="attend_forward",
    )


def attend_backward_kernel(
    place_ref, g0_ref, g1_ref, g2_ref, g3_ref, triple_ref, mixed_t_ref, tail_ref, weight_ref,
    near_ref, far_ref, grad_triple_ref,
    grad_ref, grad_t_ref, delta_ref, grad_q_t_ref, grad_k_ref, grad_v_ref, bias_t_ref,
    ids_row_ref, ids_col_ref, q_t_ref, k_t_ref,
):
    me = place_ref[0]
    _, rows, part = triple_ref.shape
    local = near_ref.shape[1]
    heads = part // HEAD_DIM
    for slot, packed_ref in enumerate((g0_ref, g1_ref, g2_ref, g3_ref)):
        unpack_rows(grad_ref, packed_ref, me ^ slot)
    pass_ids_of(tail_ref, ids_row_ref, ids_col_ref)
    for start in range(0, rows, BLOCK):
        cols = slice(start, start + BLOCK)
        q_t_ref[:, cols] = triple_ref[0, cols, :].T
        k_t_ref[:, cols] = triple_ref[1, cols, :].T
        grad_t = grad_ref[cols, :].T
        grad_t_ref[:, cols] = grad_t
        product = grad_t.astype(F32) * mixed_t_ref[0:part, cols]
        for head in range(heads):
            delta_ref[head : head + 1, cols] = column_sum(product[head * HEAD_DIM : (head + 1) * HEAD_DIM, :])
    grad_k_ref[...] = jnp.zeros_like(grad_k_ref)
    grad_v_ref[...] = jnp.zeros_like(grad_v_ref)
    for start in range(0, rows, BLOCK):
        keys = start + BLOCK
        cols = slice(start, keys)
        bias_t_ref[0:keys, :] = visibility(ids_col_ref, ids_row_ref, start, keys)

        def one_head(head, keys=keys, cols=cols):
            here = rows_at(head, HEAD_DIM)
            scores = dot(triple_ref[1, 0:keys, :], keep_head(q_t_ref[:, cols], head, 0))
            probs = jnp.exp(scores + bias_t_ref[0:keys, :] - mixed_t_ref[pl.ds(part + head, 1), cols])
            grad_probs = dot(triple_ref[2, 0:keys, :], keep_head(grad_t_ref[:, cols], head, 0))
            grad_scores = (probs * (grad_probs - delta_ref[pl.ds(head, 1), cols])).astype(BF16)
            grad_v_ref[0:keys, :] += dot(probs.astype(BF16), keep_head(grad_ref[cols, :], head, 1))
            grad_k_ref[0:keys, :] += dot(grad_scores, keep_head(triple_ref[0, cols, :], head, 1))
            grad_q_t_ref[here, cols] = dot(k_t_ref[here, 0:keys], grad_scores)

        each_head(heads, one_head, keys > LONG_BACKWARD)
    factor = HEAD_DIM**-0.5
    for start in range(0, rows, BLOCK):
        cols = slice(start, start + BLOCK)
        grad_triple_ref[0, cols, :] = (grad_q_t_ref[:, cols].T * factor).astype(BF16)
    grad_triple_ref[1] = grad_k_ref[...].astype(BF16)
    grad_triple_ref[2] = grad_v_ref[...].astype(BF16)
    for slot in range(4):
        here = rows_at(me ^ slot, local)
        target = near_ref if slot < 2 else far_ref
        target[slot % 2] = (
            dot(grad_triple_ref[0, here, :], weight_ref[0:part, :])
            + dot(grad_triple_ref[1, here, :], weight_ref[part : 2 * part, :])
            + dot(grad_triple_ref[2, here, :], weight_ref[2 * part : 3 * part, :])
        ).astype(BF16)


def attend_backward(place, grads, triple, mixed_t, tail, weight):
    _, rows, part = triple.shape
    width = weight.shape[1]
    heads = part // HEAD_DIM
    pair = shape((2, rows // 4, width), BF16)
    return call(
        attend_backward_kernel,
        [pair, pair, shape((3, rows, part), BF16)],
        place, *grads, triple, mixed_t, tail, weight,
        scratch=[
            pltpu.VMEM((rows, part), BF16),
            pltpu.VMEM((part, rows), BF16),
            pltpu.VMEM((heads, rows), F32),
            pltpu.VMEM((part, rows), F32),
            pltpu.VMEM((rows, part), F32),
            pltpu.VMEM((rows, part), F32),
            pltpu.VMEM((rows, BLOCK), F32),
            pltpu.VMEM((1, rows), F32),
            pltpu.VMEM((rows, 128), F32),
            pltpu.VMEM((part, rows), BF16),
            pltpu.VMEM((part, rows), BF16),
        ],
        vmem=16,
        name="attend_backward",
    )


def mixer_kernel(
    place_ref, m0_ref, m1_ref, m2_ref, m3_ref, x_ref, mixer_ref, vectors_ref, _later_ref,
    normed_ref, middle_ref, mixed_ref,
):
    me = place_ref[0]
    half, double = m0_ref.shape
    part = double // 2
    middle = x_ref[...].astype(F32) + vector(vectors_ref, MIXER_BIAS)
    for slot, packed_ref in enumerate((m0_ref, m1_ref, m2_ref, m3_ref)):
        cols = slice(slot * part, (slot + 1) * part)
        mixed_ref[0:half, cols] = packed_ref[:, 0:part]
        mixed_ref[half : 2 * half, cols] = packed_ref[:, part:double]
        middle += dot(mixed_ref[:, cols], mixer_ref[rows_at(me ^ slot, part), :])
    middle_ref[...] = middle
    unit, _ = unit_rows(middle)
    normed_ref[...] = (unit * vector(vectors_ref, BACK_GAIN) + vector(vectors_ref, BACK_SHIFT)).astype(BF16)


def mixer_part(place, packed, x, mixer, vectors, later):
    rows, width = x.shape
    return call(
        mixer_kernel,
        [shape((rows, width), BF16), shape((rows, width), F32), shape((rows, width), BF16)],
        place, *packed, x, mixer, vectors, later,
        name="mixer_part",
    )


def feed_kernel(
    place_ref, normed_own_ref, normed_other_ref, cot_own_ref, cot_other_ref, expand_ref, reduce_ref, vectors_ref,
    second_ref, grad_ref, send_ref, active_ref, grad_hidden_ref, bias_sum_ref,
    total_ref, back_ref,
):
    side = place_ref[1]
    rows = normed_own_ref.shape[0]
    chunk = active_ref.shape[1] // 4
    lane = lax.broadcasted_iota(jnp.int32, (1, 2 * chunk), 1) // chunk
    total_ref[...] = jnp.zeros_like(total_ref)
    back_ref[...] = jnp.zeros_like(back_ref)

    def one_chunk(index, carry):
        block = pl.ds(pl.multiple_of((2 * index + side) * chunk, 128), chunk)
        expand = expand_ref[:, block]
        reduce = reduce_ref[block, :]
        bias = vectors_ref[pl.ds(EXPAND_BIAS + index, 1), pl.ds(pl.multiple_of(side * chunk, 128), chunk)]
        sums = jnp.zeros((1, chunk), F32)
        for part, (normed_ref, cot_ref) in enumerate(((normed_own_ref, cot_own_ref), (normed_other_ref, cot_other_ref))):
            here = slice(part * rows, (part + 1) * rows)
            cols = pl.ds(pl.multiple_of(index * chunk, 128), chunk)
            hidden = dot(normed_ref[...], expand) + bias
            square = hidden * hidden
            bend = jnp.tanh(GELU_A * hidden * (1.0 + GELU_B * square))
            half = 0.5 * (1.0 + bend)
            active = (hidden * half).astype(BF16)
            active_ref[here, cols] = active
            total_ref[here, :] += dot(active, reduce)
            slope = half + (0.5 * GELU_A) * hidden * (1.0 - bend * bend) * (1.0 + (3.0 * GELU_B) * square)
            grad_hidden = (dot(cot_ref[...], reduce, NT) * slope).astype(BF16)
            grad_hidden_ref[here, cols] = grad_hidden
            sums += column_sum(grad_hidden.astype(F32))
            back_ref[here, :] += dot(grad_hidden, expand, NT)
        bias_sum_ref[pl.ds(index, 1), :] = jnp.where(lane == side, jnp.concatenate([sums, sums], axis=1), 0.0)
        return carry

    lax.fori_loop(0, 4, one_chunk, 0)
    second_ref[...] = total_ref[0:rows, :]
    grad_ref[...] = back_ref[0:rows, :]
    send_ref[0] = back_ref[rows : 2 * rows, :].astype(BF16)
    send_ref[1] = total_ref[rows : 2 * rows, :].astype(BF16)


def feed_part(place, normed_own, normed_other, cot_own, cot_other, expand, reduce, vectors):
    rows, width = normed_own.shape
    hidden = expand.shape[1]
    return call(
        feed_kernel,
        [
            shape((rows, width), F32),
            shape((rows, width), F32),
            shape((2, rows, width), BF16),
            shape((2 * rows, hidden // 2), BF16),
            shape((2 * rows, hidden // 2), BF16),
            shape((4, width), F32),
        ],
        place, normed_own, normed_other, cot_own, cot_other, expand, reduce, vectors,
        scratch=[
            pltpu.VMEM((2 * rows, width), F32),
            pltpu.VMEM((2 * rows, width), F32),
        ],
        vmem=16,
        name="feed_part",
    )


def joint_kernel(
    place_ref, grad_own_ref, recv_ref, middle_ref, cot_ref, mixer_ref, vectors_ref,
    grad_middle_ref, grad_low_ref, g0_ref, g1_ref, g2_ref, g3_ref,
):
    me = place_ref[0]
    half, double = g0_ref.shape
    part = double // 2
    grad_normed = grad_own_ref[...] + recv_ref[0].astype(F32)
    unit, scale = unit_rows(middle_ref[...])
    back = norm_pullback(grad_normed, unit, scale, vector(vectors_ref, BACK_GAIN))
    grad_middle = cot_ref[...].astype(F32) + back
    grad_middle_ref[...] = grad_middle
    grad_low = grad_middle.astype(BF16)
    grad_low_ref[...] = grad_low
    for slot, packed_ref in enumerate((g0_ref, g1_ref, g2_ref, g3_ref)):
        grad = dot(grad_low, mixer_ref[rows_at(me ^ slot, part), :], NT).astype(BF16)
        packed_ref[:, 0:part] = grad[0:half, :]
        packed_ref[:, part:double] = grad[half : 2 * half, :]


def joint_part(place, *arrays):
    rows, width = arrays[0].shape
    part = width // 4
    return call(
        joint_kernel,
        [shape((rows, width), F32), shape((rows, width), BF16)] + [shape((rows // 2, 2 * part), BF16)] * 4,
        place, *arrays,
        name="joint_part",
    )


def outer_kernel(
    place_ref, second_ref, grad_own_ref, recv_ref, middle_ref, cot_ref, grad_low_ref, mixed_ref,
    tail_ref, vectors_ref, bias_sum_ref,
    out_ref, sums_ref, mixer_send_ref, mixer_keep_ref,
    total_ref, ids_row_ref, ids_ref,
):
    me, side = place_ref[0], place_ref[1]
    rows = cot_ref.shape[0]
    cot = cot_ref[...].astype(F32)
    unit, _ = unit_rows(middle_ref[...])
    pass_ids_of(tail_ref, ids_row_ref, ids_ref)
    grad_normed = grad_own_ref[...] + recv_ref[0].astype(F32)
    sums_ref[...] = jnp.zeros_like(sums_ref)
    passes = lax.broadcasted_iota(jnp.int32, (rows, 128), 1).astype(F32)
    chosen = (ids_ref[rows_at(me, rows), :] == passes).astype(BF16)
    table = vectors_ref[TABLE : TABLE + 5, :]
    embedded = dot(chosen, jnp.concatenate([table, jnp.zeros((123, table.shape[1]), F32)], axis=0).astype(BF16))
    sums_ref[SUM_TABLE : SUM_TABLE + 5, :] = dot(chosen, cot_ref[...], TN)[0:5, :]
    second = second_ref[...] + recv_ref[1].astype(F32) + vector(vectors_ref, REDUCE_BIAS)
    out_ref[...] = (middle_ref[...] + second + embedded).astype(BF16)
    sums_ref[SUM_COT : SUM_COT + 1, :] = column_sum(cot)
    sums_ref[SUM_MIXER : SUM_MIXER + 1, :] = column_sum(grad_low_ref[...].astype(F32))
    sums_ref[SUM_GAIN : SUM_GAIN + 1, :] = column_sum(grad_normed * unit)
    sums_ref[SUM_SHIFT : SUM_SHIFT + 1, :] = column_sum(grad_normed)
    sums_ref[SUM_EXPAND : SUM_EXPAND + 4, :] = bias_sum_ref[...]
    block = mixer_send_ref.shape[1]
    total_ref[...] = dot(mixed_ref[...], grad_low_ref[...], TN).astype(BF16)
    for slot in range(4):
        mixer_keep_ref[me ^ slot] = total_ref[rows_at(2 * slot + side, block), :]
        mixer_send_ref[me ^ slot] = total_ref[rows_at(2 * slot + (1 - side), block), :]


def outer_part(place, *arrays, seq_rows):
    rows, width = arrays[0].shape
    part = shape((4, width // 8, width), BF16)
    return call(
        outer_kernel,
        [shape((rows, width), BF16), shape((16, width), F32), part, part],
        place, *arrays,
        scratch=[pltpu.VMEM((width, width), BF16), pltpu.VMEM((1, seq_rows), F32), pltpu.VMEM((seq_rows, 128), F32)],
        name="outer_part",
    )


def flip(index):
    return ((index & 1) << 1) | (index >> 1)


def quarter_at(slot, quarter, side):
    return quarter ^ jnp.where(side == 0, flip(slot), slot)


def transposed_rows(out_ref, own_ref, other_ref, spare_ref, places):
    rows, width = own_ref.shape
    part = width // 4
    spare_ref[:, 0:rows] = own_ref[...].T
    spare_ref[:, rows : 2 * rows] = other_ref[...].T
    for index, place in enumerate(places):
        out_ref[index * part : (index + 1) * part, :] = spare_ref[rows_at(place, part), :]


def reduce_grads_kernel(place_ref, cot_own_ref, cot_other_ref, active_ref, send_ref, keep_ref, cot_t_ref, spare_ref):
    side, quarter, me_n = place_ref[1], place_ref[2], place_ref[3]
    chunk = active_ref.shape[1] // 4
    part = send_ref.shape[2]
    transposed_rows(cot_t_ref, cot_own_ref, cot_other_ref, spare_ref, [me_n ^ flip(index) for index in range(4)])
    for base, target in ((0, keep_ref), (2, send_ref)):

        def one_slot(step, carry, base=base, target=target):
            cols = pl.ds(pl.multiple_of(quarter_at(base + step, quarter, side) * chunk, 128), chunk)
            reduce = dot(cot_t_ref[...], active_ref[:, cols]).astype(BF16)
            for index in range(4):
                target[step, index] = reduce[index * part : (index + 1) * part, :]
            return carry

        lax.fori_loop(0, 2, one_slot, 0)


def reduce_grads(place, cot_own, cot_other, active):
    rows, width = cot_own.shape
    out = shape((2, 4, width // 4, active.shape[1] // 4), BF16)
    return call(
        reduce_grads_kernel,
        [out, out],
        place, cot_own, cot_other, active,
        scratch=[pltpu.VMEM((width, 2 * rows), BF16), pltpu.VMEM((width, 2 * rows), BF16)],
        name="reduce_grads",
    )


def expand_grads_kernel(
    place_ref, normed_own_ref, normed_other_ref, grad_hidden_ref, mixer_keep_ref, mixer_recv_ref,
    send_ref, keep_ref,
    normed_t_ref, spare_ref,
):
    side, quarter, me_n = place_ref[1], place_ref[2], place_ref[3]
    width = normed_own_ref.shape[1]
    chunk = grad_hidden_ref.shape[1] // 4
    high = width // 4
    quarters = [quarter_at(slot, quarter, side) for slot in range(4)]
    transposed_rows(normed_t_ref, normed_own_ref, normed_other_ref, spare_ref, quarters)

    def one_chunk(index, carry):
        cols = pl.ds(pl.multiple_of((me_n ^ flip(index)) * chunk, 128), chunk)
        expand = dot(normed_t_ref[...], grad_hidden_ref[:, cols]).astype(BF16)
        for slot in range(4):
            target = keep_ref if slot < 2 else send_ref
            target[slot % 2, index, 0:high, :] = expand[slot * high : (slot + 1) * high, :]
        return carry

    lax.fori_loop(0, 4, one_chunk, 0)
    for base, target in ((0, keep_ref), (2, send_ref)):

        def one_slot(step, carry, base=base, target=target):
            place = quarter_at(base + step, quarter, side)
            mixer = (mixer_keep_ref[place].astype(F32) + mixer_recv_ref[place].astype(F32)).astype(BF16)
            block = mixer.shape[0] // 2
            for other in range(4):
                piece = mixer[:, other * high : (other + 1) * high]
                target[step, flip(other ^ me_n), high:, :] = jnp.concatenate(
                    [piece[0:block, :], piece[block : 2 * block, :]], axis=1
                )
            return carry

        lax.fori_loop(0, 2, one_slot, 0)


def expand_grads(place, normed_own, normed_other, grad_hidden, mixer_keep, mixer_recv):
    rows, width = normed_own.shape
    out = shape((2, 4, width // 4 + width // 16, grad_hidden.shape[1] // 4), BF16)
    return call(
        expand_grads_kernel,
        [out, out],
        place, normed_own, normed_other, grad_hidden, mixer_keep, mixer_recv,
        scratch=[pltpu.VMEM((width, 2 * rows), BF16), pltpu.VMEM((width, 2 * rows), BF16)],
        name="expand_grads",
    )


def triple_grads_kernel(
    place_ref, x0_ref, x1_ref, x2_ref, x3_ref, near_ref, far_ref, normed_ref, grad_triple_ref, sums_in_ref,
    t0_ref, t1_ref, t2_ref, t3_ref, packet_ref, sums_ref,
    weight_ref,
):
    me, corner = place_ref[0], place_ref[7]
    rows, width = normed_ref.shape
    part = grad_triple_ref.shape[2]
    def sum_block(step, sums):
        here = rows_at(step, 64)
        gain_sum, shift_sum = sums
        for slot, x_ref in enumerate((x0_ref, x1_ref, x2_ref, x3_ref)):
            unit, _ = unit_rows(x_ref[here, :].astype(F32))
            grad = (near_ref if slot < 2 else far_ref)[slot % 2, here, :].astype(F32)
            gain_sum += (grad * unit).reshape(8, 8, width).sum(axis=0)
            shift_sum += grad.reshape(8, 8, width).sum(axis=0)
        return gain_sum, shift_sum

    gain_sum, shift_sum = lax.fori_loop(
        0, rows // 256, sum_block, (jnp.zeros((8, width), F32), jnp.zeros((8, width), F32))
    )
    gain_sum, shift_sum = column_sum(gain_sum), column_sum(shift_sum)
    sums_ref[0:16, :] = sums_in_ref[...]
    sums_ref[16:24, :] = jnp.zeros((8, width), F32)
    sums_ref[SUM_FRONT_GAIN : SUM_FRONT_GAIN + 1, :] = gain_sum
    sums_ref[SUM_FRONT_SHIFT : SUM_FRONT_SHIFT + 1, :] = shift_sum
    group = lax.broadcasted_iota(jnp.int32, (1, width), 1) // part
    for row, index in ((0, 0), (1, 2)):
        bias = column_sum(grad_triple_ref[index].astype(F32))
        sums_ref[SUM_TRIPLE + row : SUM_TRIPLE + row + 1, :] = jnp.where(
            group == me, jnp.concatenate([bias] * (width // part), axis=1), 0.0
        )
    for index in range(3):
        weight_ref[index * part : (index + 1) * part, :] = dot(grad_triple_ref[index], normed_ref[...], TN).astype(BF16)
    piece = 3 * part // 4
    for slot, target in enumerate((t0_ref, t1_ref, t2_ref, t3_ref)):
        target[...] = weight_ref[rows_at(corner ^ slot, piece), :]
    local = far_ref.shape[1]
    packet_ref[0:local, :] = far_ref[0]
    packet_ref[local : 2 * local, :] = far_ref[1]
    put_sums(packet_ref, 2 * local, sums_ref[...])


def triple_grads(place, shards, near, far, normed, grad_triple, sums):
    rows, width = normed.shape
    part = grad_triple.shape[2]
    return call(
        triple_grads_kernel,
        [shape((3 * part // 4, width), BF16)] * 4
        + [shape((rows // 2 + 2 * SUMS, width), BF16), shape((SUMS, width), F32)],
        place, *shards, near, far, normed, grad_triple, sums,
        scratch=[pltpu.VMEM((3 * part, width), BF16)],
        vmem=16,
        name="triple_grads",
    )


def pair_kernel(place_ref, near_ref, sent_ref, recv_ref, packet_ref, own_ref):
    local = near_ref.shape[1]
    own_ref[...] = near_ref[0].astype(F32) + recv_ref[0:local, :].astype(F32)
    packet_ref[0:local, :] = (near_ref[1].astype(F32) + recv_ref[local : 2 * local, :].astype(F32)).astype(BF16)
    put_sums(packet_ref, local, get_sums(sent_ref, 2 * local) + get_sums(recv_ref, 2 * local))


def pair_part(place, near, sent, recv):
    _, local, width = near.shape
    return call(
        pair_kernel,
        [shape((local + 2 * SUMS, width), BF16), shape((local, width), F32)],
        place, near, sent, recv,
        name="pair_part",
    )


def home_kernel(place_ref, t0_ref, t1_ref, t2_ref, t3_ref, sent_ref, recv_ref, packet_ref):
    piece = t0_ref.shape[0]
    local = sent_ref.shape[0] - 2 * SUMS
    total = t0_ref[...].astype(F32) + t1_ref[...].astype(F32) + t2_ref[...].astype(F32) + t3_ref[...].astype(F32)
    packet_ref[0:piece, :] = total.astype(BF16)
    put_sums(packet_ref, piece, get_sums(sent_ref, local) + get_sums(recv_ref, local))


def home_part(place, pieces, sent, recv):
    piece, width = pieces[0].shape
    return call(
        home_kernel, [shape((piece + 2 * SUMS, width), BF16)], place, *pieces, sent, recv, name="home_part"
    )[0]


def front_kernel(place_ref, x_ref, own_ref, recv_ref, grad_middle_ref, vectors_ref, out_ref):
    unit, scale = unit_rows(x_ref[...].astype(F32))
    grad = own_ref[...] + recv_ref[0 : own_ref.shape[0], :].astype(F32)
    back = norm_pullback(grad, unit, scale, vector(vectors_ref, FRONT_GAIN))
    out_ref[...] = (grad_middle_ref[...] + back).astype(BF16)


def front_part(place, x, *arrays):
    return call(front_kernel, [shape(x.shape, BF16)], place, x, *arrays, name="front_part")[0]


def spread_kernel(place_ref, sent_ref, recv_ref, packet_ref):
    piece = sent_ref.shape[0] - 2 * SUMS
    packet_ref[0:piece, :] = (sent_ref[0:piece, :].astype(F32) + recv_ref[0:piece, :].astype(F32)).astype(BF16)
    put_sums(packet_ref, piece, get_sums(sent_ref, piece) + get_sums(recv_ref, piece))


def spread_part(place, sent, recv):
    return call(spread_kernel, [shape(sent.shape, BF16)], place, sent, recv, name="spread_part")[0]


def last_kernel(place_ref, s0_ref, s1_ref, s2_ref, s3_ref, a_ref, b_ref, c_ref, packet_ref, total_ref):
    side, corner = place_ref[1], place_ref[7]
    piece = s0_ref.shape[0] - 2 * SUMS
    for slot, ref in enumerate((s0_ref, s1_ref, s2_ref, s3_ref)):
        packet_ref[rows_at(corner ^ slot, piece), :] = ref[0:piece, :]
    put_sums(
        packet_ref,
        4 * piece,
        (get_sums(s0_ref, piece) + get_sums(s1_ref, piece)) + (get_sums(s2_ref, piece) + get_sums(s3_ref, piece)),
    )
    total_ref[...] = a_ref[0].astype(F32) + b_ref[0].astype(F32) + c_ref[...].astype(F32)
    half = (packet_ref.shape[0] - 4 * piece - 2 * SUMS)
    chunk = total_ref.shape[1]
    start = 4 * piece + 2 * SUMS
    packet_ref[start:, 0:chunk] = total_ref[rows_at(2 * (1 - side), half), :].astype(BF16)
    packet_ref[start:, chunk : 2 * chunk] = total_ref[rows_at(2 * (1 - side) + 1, half), :].astype(BF16)


def last_part(place, packets, a, b, c):
    rows, width = packets[0].shape
    piece = rows - 2 * SUMS
    block = width // 8
    return call(
        last_kernel,
        [shape((4 * piece + 2 * SUMS + block // 2, width), BF16), shape(c.shape, F32)],
        place, *packets, a, b, c,
        name="last_part",
    )


def results_kernel(
    place_ref, sent_ref, recv_ref, total_ref, ra_ref, rb_ref, rc_ref, layer_ref, rows_ref,
    triple_ref, expand_ref, mixer_ref, reduce_ref, layer_out_ref, rows_out_ref, triple_bias_ref, table_ref,
    front_gain_ref, front_shift_ref, mixer_bias_ref, back_gain_ref, back_shift_ref, expand_bias_ref, reduce_bias_ref,
    sums_ref,
):
    side, me_n, stay = place_ref[1], place_ref[3], place_ref[5]
    layer_out_ref[...] = layer_ref[...]
    rows_out_ref[...] = rows_ref[...]
    weights, width = triple_ref.shape
    part = mixer_ref.shape[1]

    @pl.when(stay == 1)
    def _():
        triple_ref[...] = sent_ref[0:weights, :].astype(F32)
        sums_ref[...] = get_sums(sent_ref, weights)

    @pl.when(stay == 0)
    def _():
        triple_ref[...] = recv_ref[0:weights, :].astype(F32)
        sums_ref[...] = get_sums(recv_ref, weights)

    block, double = expand_ref.shape
    chunk, half = double // 2, block // 2
    start = weights + 2 * SUMS
    for index in range(2):
        mine = total_ref[rows_at(2 * side + index, half), :]
        other = recv_ref[start:, index * chunk : (index + 1) * chunk].astype(F32)
        first = jnp.full(mine.shape, side, jnp.int32) == 0
        here = slice(index * half, (index + 1) * half)
        expand_ref[here, 0:chunk] = jnp.where(first, mine, other)
        expand_ref[here, chunk:double] = jnp.where(first, other, mine)
        mixer_ref[here, :] = total_ref[2 * block :, index * part : (index + 1) * part]
    reduce_ref[...] = ra_ref[0].astype(F32) + rb_ref[0].astype(F32) + rc_ref[...].astype(F32)
    pair = sums_ref[SUM_TRIPLE : SUM_TRIPLE + 2, :]
    bias = jnp.zeros((2, part), F32)
    for group in range(width // part):
        mine = jnp.full(bias.shape, me_n, jnp.int32) == group
        bias = jnp.where(mine, pair[:, group * part : (group + 1) * part], bias)
    triple_bias_ref[...] = bias
    table_ref[...] = sums_ref[SUM_TABLE : SUM_TABLE + table_ref.shape[0], :]
    for index, ref in (
        (SUM_FRONT_GAIN, front_gain_ref), (SUM_FRONT_SHIFT, front_shift_ref), (SUM_MIXER, mixer_bias_ref),
        (SUM_GAIN, back_gain_ref), (SUM_SHIFT, back_shift_ref), (SUM_COT, reduce_bias_ref),
    ):
        ref[...] = sums_ref[index : index + 1, :].reshape(width)
    for index in range(4):
        expand_bias_ref[index * width : (index + 1) * width] = (
            sums_ref[SUM_EXPAND + index : SUM_EXPAND + index + 1, :].reshape(width)
        )


def results(place, sent, recv, total, ra, rb, rc, layer, rows, passes):
    width = sent.shape[1]
    block = width // 8
    piece = (sent.shape[0] - 2 * SUMS - block // 2) // 4
    row = shape((width,), F32)
    return call(
        results_kernel,
        [
            shape((4 * piece, width), F32), shape((block, width), F32), shape((block, width // 4), F32),
            shape(rc.shape, F32), shape(layer.shape, BF16), shape(rows.shape, BF16),
            shape((2, width // 4), F32), shape((passes, width), F32),
            row, row, row, row, row, shape((4 * width,), F32), row,
        ],
        place, sent, recv, total, ra, rb, rc, layer, rows,
        scratch=[pltpu.VMEM((SUMS, width), F32)],
        name="results",
    )


def after(value, *earlier):
    return lax.optimization_barrier((value, earlier))[0]


def body(
    inputs,
    pass_ids,
    front_gain,
    front_shift,
    triple_weight,
    triple_bias,
    mixer_weight,
    mixer_bias,
    back_gain,
    back_shift,
    expand_weight,
    expand_bias,
    reduce_weight,
    reduce_bias,
    pass_table,
    cotangent,
):
    width = inputs.shape[1]
    part = triple_weight.shape[2]
    wide_size, narrow_size = lax.axis_size("wide"), lax.axis_size("narrow")
    low_bits = wide_size.bit_length() - 4
    side_bit, x_bit, y_bit = 1 << low_bits, 2 << low_bits, 4 << low_bits

    wide, narrow = lax.axis_index("wide"), lax.axis_index("narrow")
    c, h, l = wide & 1, narrow >> 1, narrow & 1
    me = 2 * c + l
    top = wide >> low_bits
    side, quarter = top & 1, top >> 1
    x1, y1 = (wide >> 1) & 1, (wide >> 2) & 1
    stay = (c == h).astype(jnp.int32)
    corner = 2 * y1 + x1
    place = jnp.stack(
        [
            me, side, quarter, narrow,
            jnp.where(c == 0, 2 * x1 + y1, corner),
            stay,
            jnp.where(h == 0, 2 * x1 + y1, corner),
            corner,
        ]
    ).astype(jnp.int32)

    def send(name, value, target):
        pairs = []
        for w in range(wide_size):
            for n in range(narrow_size):
                to = target(w, n)
                if to is not None:
                    pairs.append((w * narrow_size + n, to[0] * narrow_size + to[1]))
        with jax.named_scope(name):
            return lax.ppermute(value, AXES, pairs)

    def stays(w, n):
        return (w & 1) == (n >> 1)

    def moved(w, n):
        return (w, n) if stays(w, n) else (w ^ 1, n ^ 2)

    def home(w, n):
        return None if stays(w, n) else (w, n ^ 2)

    def lend(w, n):
        return (w, n ^ 2) if stays(w, n) else None

    def core(w, n):
        return (w ^ 1, n)

    def pair(w, n):
        return (w, n ^ 1)

    def diagonal(w, n):
        return (w ^ 1, n ^ 1)

    def across(w, n):
        return (w, n ^ 2)

    def sided(w, n):
        return (w ^ side_bit, n)

    def first(w, n):
        return (w ^ (y_bit if w & side_bit else x_bit), n)

    def second(w, n):
        return (w ^ (x_bit if w & side_bit else y_bit), n)

    def step_x(w, n):
        return (w ^ 2, n)

    def step_y(w, n):
        return (w ^ 4, n)

    def step_xy(w, n):
        return (w ^ 6, n)

    def of_stay(target):
        return lambda w, n: target(w, n) if stays(w, n) else None

    def of_moved(target):
        return lambda w, n: None if stays(w, n) else target(w, n)

    def add(*terms):
        return sum(t.astype(F32) for t in terms).astype(BF16)

    together = lax.optimization_barrier

    weight_t = jnp.swapaxes(triple_weight, 1, 2).reshape(3 * part, width)
    piece = 3 * part // 4
    lent = lax.dynamic_slice_in_dim(weight_t, corner * piece, piece)
    place, lent = together((place, lent))
    p0 = send("lend_weight", lent, lend)
    x0 = send("rows_move", after(inputs, lent), moved)
    x1_stay = send("rows_pair", inputs, of_stay(pair))
    vectors, tail = gather_vectors(
        place, triple_bias, pass_ids,
        front_gain, front_shift, mixer_bias, back_gain, back_shift, reduce_bias, expand_bias, pass_table,
    )
    tail = send("tail_move", tail, moved)
    x0, p0, x1_stay, vectors, tail = together((x0, p0, x1_stay, vectors, tail))
    x1_moved = send("rows_pair", x0, of_moved(pair))
    p1, p2, p3 = (send("lent", p0, of_moved(step)) for step in (step_x, step_y, step_xy))
    x1_moved, p1, p2, p3 = together((x1_moved, p1, p2, p3))
    x1_rows = jnp.where(stay == 1, x1_stay, x1_moved)
    x2 = send("rows_core", x0, core)
    x3 = send("pair_core", x1_rows, core)
    cot_own = send("cot_move", after(cotangent, x1_rows), moved)

    shards = (x0, x1_rows, x2, x3)
    m0, m1, m2, m3, mixed_t, normed, triple, weight = attend_forward(
        place, shards, tail, vectors, weight_t, (p0, p1, p2, p3)
    )
    m1, m2, m3, cot_own = together(
        (send("m_pair", m1, pair), send("m_core", m2, core), send("m_diagonal", m3, diagonal), cot_own)
    )
    cot_other = send("cot_core", cot_own, sided)
    normed_two, middle, mixed_rows = mixer_part(place, (m0, m1, m2, m3), x0, mixer_weight, vectors, reduce_weight)
    normed_other, cot_other = together((send("normed_core", normed_two, sided), cot_other))
    second_own, grad_own, feed_send, active, grad_hidden, bias_sums = feed_part(
        place, normed_two, normed_other, cot_own, cot_other, expand_weight, reduce_weight, vectors
    )
    feed_recv = send("feed_core", feed_send, sided)
    reduce_send, reduce_keep = reduce_grads(place, cot_own, cot_other, active)
    grad_own, feed_recv, reduce_send = together((grad_own, feed_recv, reduce_send))
    reduce_first = send("reduce_first", reduce_send, first)
    grad_middle, grad_low, g0, g1, g2, g3 = joint_part(
        place, grad_own, feed_recv, middle, cot_own, mixer_weight, vectors
    )
    g1, g2, g3 = send("g_pair", g1, pair), send("g_core", g2, core), send("g_diagonal", g3, diagonal)
    out_rows, sums, mixer_send, mixer_keep = outer_part(
        place, second_own, grad_own, feed_recv, middle, cot_own, grad_low, mixed_rows, tail, vectors, bias_sums,
        seq_rows=pass_ids.shape[1],
    )
    mixer_recv = send("mixer_core", mixer_send, sided)
    expand_send, expand_keep = expand_grads(
        place, normed_two, normed_other, grad_hidden, mixer_keep, mixer_recv
    )
    g1, g2, g3, expand_send, expand_keep, out_rows, reduce_first = together(
        (g1, g2, g3, expand_send, expand_keep, out_rows, reduce_first)
    )
    reduce_second = send("reduce_second", add(reduce_keep[1], reduce_first[1]), second)
    expand_first = send("expand_first", expand_send, first)
    layer_out = send("out_move", out_rows, moved)
    near, far, grad_triple_rows = attend_backward(
        place, (g0, g1, g2, g3), triple, mixed_t, tail, weight
    )

    def halved(keep, first_recv, second_recv):
        return (
            add(keep[0, 0:2], first_recv[0, 0:2], second_recv[0:2]),
            add(keep[0, 2:4], first_recv[0, 2:4], second_recv[2:4]),
        )

    far, near, grad_triple_rows, reduce_second, layer_out = together(
        (far, near, grad_triple_rows, reduce_second, layer_out)
    )
    reduce_a, reduce_b = halved(reduce_keep, reduce_first, reduce_second)
    reduce_pair = send("reduce_pair", reduce_b, pair)
    t0, t1, t2, t3, core_packet, all_sums = triple_grads(place, shards, near, far, normed, grad_triple_rows, sums)
    core_packet = after(core_packet, reduce_pair)
    core_recv, expand_first = together((send("far_core", core_packet, core), expand_first))

    pair_packet, own_rows = pair_part(place, near, core_packet, core_recv)
    pair_recv = send("near_pair", pair_packet, pair)
    t1, t2, t3 = send("triple_x", t1, step_x), send("triple_y", t2, step_y), send("triple_xy", t3, step_xy)
    expand_second = send("expand_second", add(expand_keep[1], expand_first[1]), second)
    reduce_across = send("reduce_across", add(reduce_a[1], reduce_pair[1]), across)
    t1, t2, t3, pair_recv, expand_second, reduce_across = together(
        (t1, t2, t3, pair_recv, expand_second, reduce_across)
    )

    home_packet = home_part(place, (t0, t1, t2, t3), pair_packet, pair_recv)
    home_recv = send("triple_home", home_packet, home)
    grad_rows = front_part(place, x0, own_rows, pair_recv, grad_middle, vectors)
    grad_inputs = send("rows_home", grad_rows, moved)
    expand_a, expand_b = halved(expand_keep, expand_first, expand_second)
    expand_pair = send("expand_pair", expand_b, pair)
    home_recv, expand_pair, grad_rows = together((home_recv, expand_pair, grad_rows))

    spread = spread_part(place, home_packet, home_recv)
    s1, s2, s3 = (send("triple_spread", spread, of_stay(step)) for step in (step_x, step_y, step_xy))
    expand_across = send("expand_across", add(expand_a[1], expand_pair[1]), across)
    s1, s2, s3, expand_across, grad_inputs = together((s1, s2, s3, expand_across, grad_inputs))

    last_packet, total = last_part(place, (spread, s1, s2, s3), expand_a, expand_pair, expand_across)
    last_recv = send("last_core", last_packet, core)
    (
        grad_triple, total_expand, total_mixer, total_reduce, layer_out, grad_inputs, grad_triple_bias, grad_table,
        grad_front_gain, grad_front_shift, grad_mixer_bias, grad_back_gain, grad_back_shift, grad_expand_bias,
        grad_reduce_bias,
    ) = results(
        place, last_packet, last_recv, total, reduce_a, reduce_pair, reduce_across, layer_out, grad_inputs,
        pass_table.shape[0],
    )
    grad_triple = jnp.swapaxes(grad_triple.reshape(3, part, width), 1, 2)
    if low_bits:
        size = 1 << low_bits
        peers = [[size * i + j for j in range(size)] for i in range(wide_size // size)]
        total_expand, total_reduce, total_mixer = (
            lax.psum_scatter(t, "wide", scatter_dimension=d, axis_index_groups=peers, tiled=True)
            for t, d in ((total_expand, 0), (total_reduce, 1), (total_mixer, 0))
        )
        peers = [[i + 8 * j for j in range(wide_size // 8)] for i in range(8)]
        (
            grad_triple, grad_triple_bias, grad_table, grad_front_gain, grad_front_shift, grad_mixer_bias,
            grad_back_gain, grad_back_shift, grad_expand_bias, grad_reduce_bias,
        ) = lax.psum(
            (
                grad_triple, grad_triple_bias, grad_table, grad_front_gain, grad_front_shift, grad_mixer_bias,
                grad_back_gain, grad_back_shift, grad_expand_bias, grad_reduce_bias,
            ),
            "wide", axis_index_groups=peers,
        )
    return (
        layer_out,
        grad_inputs,
        grad_front_gain,
        grad_front_shift,
        grad_triple,
        grad_triple_bias,
        total_mixer,
        grad_mixer_bias,
        grad_back_gain,
        grad_back_shift,
        total_expand,
        grad_expand_bias,
        total_reduce.T,
        grad_reduce_bias,
        grad_table,
    )


def solution(mesh):
    rows = P(AXES, None)
    block = P("wide", "narrow")
    return jax.shard_map(
        body,
        mesh=mesh,
        in_specs=(
            rows, P("wide", None), P(), P(), P(None, None, "narrow"), P(None, "narrow"),
            P(), P(), P(), P(), P(), P(), P(), P(), P(), rows,
        ),
        out_specs=(
            rows, rows, P(), P(), P(None, None, "narrow"), P(None, "narrow"), block,
            P(), P(), P(), block, P(), block, P(), P(),
        ),
        check_vma=False,
    )
```

```python
import math

import jax
import jax.numpy as jnp
from jax import lax
from jax.experimental import pallas as pl
from jax.experimental.pallas import tpu as pltpu
from jax.sharding import PartitionSpec as P


HEAD_DIM = 64
EPSILON = 1e-05
BLOCK = 256
LONG_FORWARD, LONG_BACKWARD = 768, 1280
HIDDEN = -1e30
F32 = jnp.float32
BF16 = jnp.bfloat16
MIB = 1024 * 1024
AXES = ("wide", "narrow")
NN = (((1,), (0,)), ((), ()))
NT = (((1,), (1,)), ((), ()))
TN = (((0,), (0,)), ((), ()))
GELU_A = math.sqrt(2.0 / math.pi)
GELU_B = 0.044715
shape = jax.ShapeDtypeStruct

FRONT_GAIN, FRONT_SHIFT, MIXER_BIAS, BACK_GAIN, BACK_SHIFT, REDUCE_BIAS, EXPAND_BIAS, TABLE = 0, 1, 2, 3, 4, 5, 6, 10
SUM_TABLE, SUM_COT, SUM_MIXER, SUM_GAIN, SUM_SHIFT, SUM_EXPAND = 0, 5, 6, 7, 8, 9
SUM_FRONT_GAIN, SUM_FRONT_SHIFT, SUM_TRIPLE = 16, 17, 18
SUMS = 24


def dot(left, right, dims=NN):
    return lax.dot_general(left, right, dims, preferred_element_type=F32)


def whole():
    return pl.BlockSpec(memory_space=pltpu.VMEM)


def call(kernel, outs, *arrays, scratch=(), vmem=12, name=None):
    return pl.pallas_call(
        kernel,
        out_shape=tuple(outs),
        in_specs=[pl.BlockSpec(memory_space=pltpu.SMEM)] + [whole()] * (len(arrays) - 1),
        out_specs=(whole(),) * len(outs),
        scratch_shapes=list(scratch),
        compiler_params=pltpu.CompilerParams(vmem_limit_bytes=vmem * MIB),
        name=name,
    )(*arrays)


def unit_rows(values):
    centred = values - jnp.mean(values, axis=-1, keepdims=True)
    scale = lax.rsqrt(jnp.mean(centred * centred, axis=-1, keepdims=True) + EPSILON)
    return centred * scale, scale


def norm_pullback(grad_out, unit, scale, gain):
    grad_unit = grad_out * gain
    inner = (
        grad_unit
        - jnp.mean(grad_unit, axis=-1, keepdims=True)
        - unit * jnp.mean(grad_unit * unit, axis=-1, keepdims=True)
    )
    return inner * scale


def column_sum(values):
    return jnp.sum(values, axis=0, keepdims=True)


def put_sums(packet_ref, start, sums):
    high = sums.astype(BF16).astype(F32)
    packet_ref[start : start + 2 * SUMS, :] = jnp.concatenate([high, sums - high], axis=0).astype(BF16)


def get_sums(packet_ref, start):
    both = packet_ref[start : start + 2 * SUMS, :].astype(F32)
    return both[0:SUMS, :] + both[SUMS : 2 * SUMS, :]


def keep_head(block, head, axis):
    place = lax.broadcasted_iota(jnp.int32, block.shape, axis) // HEAD_DIM
    return jnp.where(place == head, block, jnp.zeros_like(block))


def rows_at(index, count):
    if isinstance(index, int):
        return slice(index * count, (index + 1) * count)
    return pl.ds(pl.multiple_of(index * count, math.gcd(count, 64)), count)


def each_head(heads, one_head, looped):
    if looped:
        lax.fori_loop(0, heads, lambda head, carry: one_head(head) or carry, 0)
    else:
        for head in range(heads):
            one_head(head)


def vector(vectors_ref, index):
    return vectors_ref[index : index + 1, :]


def pass_ids_of(tail_ref, row_ref, col_ref):
    width = tail_ref.shape[1]
    rows = row_ref.shape[1]
    tail = tail_ref[...].astype(F32)
    row_ref[:, 0:width] = tail[1:2, :]
    row_ref[:, width:rows] = tail[2:3, 0 : rows - width]
    for start in range(0, rows, BLOCK):
        col_ref[start : start + BLOCK, :] = jnp.broadcast_to(row_ref[:, start : start + BLOCK], (128, BLOCK)).T


def visibility(ids_col_ref, ids_row_ref, start, keys):
    seen = ids_col_ref[0:keys, 0:1] <= ids_row_ref[:, start : start + BLOCK]
    key_place = lax.broadcasted_iota(jnp.int32, (keys, BLOCK), 0)
    query_place = lax.broadcasted_iota(jnp.int32, (keys, BLOCK), 1) + start
    return jnp.where(seen & (key_place <= query_place), 0.0, HIDDEN).astype(F32)


def vectors_kernel(place_ref, bias_ref, ids_ref, *refs):
    tail_ref, out_ref, table_ref, long_ref = refs[-1], refs[-2], refs[-3], refs[-4]
    width = out_ref.shape[1]
    out_ref[...] = jnp.zeros_like(out_ref)
    for index, ref in enumerate(refs[:-4]):
        out_ref[index : index + 1, :] = ref[...].astype(F32).reshape(1, width)
    long = long_ref[...].astype(F32).reshape(1, long_ref.shape[0])
    for index in range(long_ref.shape[0] // width):
        out_ref[EXPAND_BIAS + index : EXPAND_BIAS + index + 1, :] = long[:, index * width : (index + 1) * width]
    out_ref[TABLE : TABLE + table_ref.shape[0], :] = table_ref[...].astype(F32)
    ids = ids_ref[...].astype(F32)
    bias = bias_ref[...].astype(F32)
    rest, double = ids.shape[1] - width, 2 * bias.shape[1]
    tail = [
        jnp.concatenate([bias[0:1, :], bias[1:2, :], jnp.zeros((1, width - double), F32)], axis=1),
        ids[:, 0:width],
        jnp.concatenate([ids[:, width:], jnp.zeros((1, width - rest), F32)], axis=1),
        jnp.zeros((13, width), F32),
    ]
    tail_ref[...] = jnp.concatenate(tail, axis=0).astype(BF16)


def gather_vectors(place, bias, ids, *arrays):
    width = arrays[0].shape[0]
    return call(
        vectors_kernel,
        [shape((16, width), F32), shape((16, width), BF16)],
        place, bias, ids, *arrays,
        vmem=4,
        name="gather_vectors",
    )


def attend_forward_kernel(
    place_ref, x0_ref, x1_ref, x2_ref, x3_ref, tail_ref, vectors_ref, weight_own_ref, p0_ref, p1_ref, p2_ref, p3_ref,
    m0_ref, m1_ref, m2_ref, m3_ref, mixed_t_ref, normed_ref, triple_ref, weight_ref,
    ids_row_ref, ids_col_ref, q_t_ref, v_t_ref, bias_t_ref, mixed_ref, straight_ref,
):
    me, stay, corner = place_ref[0], place_ref[5], place_ref[7]
    _, rows, part = triple_ref.shape
    local = x0_ref.shape[0]
    piece = p0_ref.shape[0]
    heads = part // HEAD_DIM
    gain = vector(vectors_ref, FRONT_GAIN)
    shift = vector(vectors_ref, FRONT_SHIFT)
    pass_ids_of(tail_ref, ids_row_ref, ids_col_ref)

    @pl.when(stay == 1)
    def _():
        weight_ref[...] = weight_own_ref[...]

    @pl.when(stay == 0)
    def _():
        for slot, value in enumerate((p0_ref, p1_ref, p2_ref, p3_ref)):
            weight_ref[rows_at(corner ^ slot, piece), :] = value[...]

    straight_ref[...] = weight_ref[...].T
    bias = tail_ref[...].astype(F32)[0:1, 0 : 2 * part]
    for slot, x_ref in enumerate((x0_ref, x1_ref, x2_ref, x3_ref)):
        here = rows_at(me ^ slot, local)
        unit, _ = unit_rows(x_ref[...].astype(F32))
        normed = (unit * gain + shift).astype(BF16)
        normed_ref[here, :] = normed
        q = (dot(normed, straight_ref[:, 0:part]) + bias[:, 0:part]).astype(BF16)
        triple_ref[0, here, :] = q * jnp.asarray(HEAD_DIM**-0.5, BF16)
        triple_ref[1, here, :] = dot(normed, straight_ref[:, part : 2 * part]).astype(BF16)
        triple_ref[2, here, :] = (dot(normed, straight_ref[:, 2 * part : 3 * part]) + bias[:, part : 2 * part]).astype(BF16)

    for start in range(0, rows, BLOCK):
        cols = slice(start, start + BLOCK)
        q_t_ref[:, cols] = triple_ref[0, cols, :].T
        v_t_ref[:, cols] = triple_ref[2, cols, :].T

    mixed_t_ref[part : part + 8, :] = jnp.zeros((8, rows), F32)
    for start in range(0, rows, BLOCK):
        keys = start + BLOCK
        cols = slice(start, keys)
        bias_t_ref[0:keys, :] = visibility(ids_col_ref, ids_row_ref, start, keys)

        def one_head(head, keys=keys, cols=cols):
            here = rows_at(head, HEAD_DIM)
            scores = dot(triple_ref[1, 0:keys, :], keep_head(q_t_ref[:, cols], head, 0)) + bias_t_ref[0:keys, :]
            top = jnp.max(scores, axis=0, keepdims=True)
            weights = jnp.exp(scores - top)
            total = jnp.sum(weights, axis=0, keepdims=True)
            mixed_t_ref[here, cols] = dot(v_t_ref[here, 0:keys], weights.astype(BF16)) / total
            mixed_t_ref[pl.ds(part + head, 1), cols] = top + jnp.log(total)

        each_head(heads, one_head, keys > LONG_FORWARD)
        mixed_ref[cols, :] = mixed_t_ref[0:part, cols].T.astype(BF16)
    for slot, out_ref in enumerate((m0_ref, m1_ref, m2_ref, m3_ref)):
        pack_rows(out_ref, mixed_ref, me ^ slot)


def pack_rows(out_ref, rows_ref, index):
    half, part = out_ref.shape[0], out_ref.shape[1] // 2
    out_ref[:, 0:part] = rows_ref[rows_at(2 * index, half), :]
    out_ref[:, part : 2 * part] = rows_ref[rows_at(2 * index + 1, half), :]


def unpack_rows(rows_ref, packed_ref, index):
    half, part = packed_ref.shape[0], packed_ref.shape[1] // 2
    rows_ref[rows_at(2 * index, half), :] = packed_ref[:, 0:part]
    rows_ref[rows_at(2 * index + 1, half), :] = packed_ref[:, part : 2 * part]


def attend_forward(place, shards, tail, vectors, weight, pieces):
    local, width = shards[0].shape
    rows = 4 * local
    part = weight.shape[0] // 3
    return call(
        attend_forward_kernel,
        [shape((local // 2, 2 * part), BF16)] * 4
        + [
            shape((part + 8, rows), F32),
            shape((rows, width), BF16),
            shape((3, rows, part), BF16),
            shape(weight.shape, BF16),
        ],
        place, *shards, tail, vectors, weight, *pieces,
        scratch=[
            pltpu.VMEM((1, rows), F32),
            pltpu.VMEM((rows, 128), F32),
            pltpu.VMEM((part, rows), BF16),
            pltpu.VMEM((part, rows), BF16),
            pltpu.VMEM((rows, BLOCK), F32),
            pltpu.VMEM((rows, part), BF16),
            pltpu.VMEM((width, 3 * part), BF16),
        ],
        vmem=16,
        name="attend_forward",
    )


def attend_backward_kernel(
    place_ref, g0_ref, g1_ref, g2_ref, g3_ref, triple_ref, mixed_t_ref, tail_ref, weight_ref,
    near_ref, far_ref, grad_triple_ref,
    grad_ref, grad_t_ref, delta_ref, grad_q_t_ref, grad_k_ref, grad_v_ref, bias_t_ref,
    ids_row_ref, ids_col_ref, q_t_ref, k_t_ref,
):
    me = place_ref[0]
    _, rows, part = triple_ref.shape
    local = near_ref.shape[1]
    heads = part // HEAD_DIM
    for slot, packed_ref in enumerate((g0_ref, g1_ref, g2_ref, g3_ref)):
        unpack_rows(grad_ref, packed_ref, me ^ slot)
    pass_ids_of(tail_ref, ids_row_ref, ids_col_ref)
    for start in range(0, rows, BLOCK):
        cols = slice(start, start + BLOCK)
        q_t_ref[:, cols] = triple_ref[0, cols, :].T
        k_t_ref[:, cols] = triple_ref[1, cols, :].T
        grad_t = grad_ref[cols, :].T
        grad_t_ref[:, cols] = grad_t
        product = grad_t.astype(F32) * mixed_t_ref[0:part, cols]
        for head in range(heads):
            delta_ref[head : head + 1, cols] = column_sum(product[head * HEAD_DIM : (head + 1) * HEAD_DIM, :])
    grad_k_ref[...] = jnp.zeros_like(grad_k_ref)
    grad_v_ref[...] = jnp.zeros_like(grad_v_ref)
    for start in range(0, rows, BLOCK):
        keys = start + BLOCK
        cols = slice(start, keys)
        bias_t_ref[0:keys, :] = visibility(ids_col_ref, ids_row_ref, start, keys)

        def one_head(head, keys=keys, cols=cols):
            here = rows_at(head, HEAD_DIM)
            scores = dot(triple_ref[1, 0:keys, :], keep_head(q_t_ref[:, cols], head, 0))
            probs = jnp.exp(scores + bias_t_ref[0:keys, :] - mixed_t_ref[pl.ds(part + head, 1), cols])
            grad_probs = dot(triple_ref[2, 0:keys, :], keep_head(grad_t_ref[:, cols], head, 0))
            grad_scores = (probs * (grad_probs - delta_ref[pl.ds(head, 1), cols])).astype(BF16)
            grad_v_ref[0:keys, :] += dot(probs.astype(BF16), keep_head(grad_ref[cols, :], head, 1))
            grad_k_ref[0:keys, :] += dot(grad_scores, keep_head(triple_ref[0, cols, :], head, 1))
            grad_q_t_ref[here, cols] = dot(k_t_ref[here, 0:keys], grad_scores)

        each_head(heads, one_head, keys > LONG_BACKWARD)
    factor = HEAD_DIM**-0.5
    for start in range(0, rows, BLOCK):
        cols = slice(start, start + BLOCK)
        grad_triple_ref[0, cols, :] = (grad_q_t_ref[:, cols].T * factor).astype(BF16)
    grad_triple_ref[1] = grad_k_ref[...].astype(BF16)
    grad_triple_ref[2] = grad_v_ref[...].astype(BF16)
    for slot in range(4):
        here = rows_at(me ^ slot, local)
        target = near_ref if slot < 2 else far_ref
        target[slot % 2] = (
            dot(grad_triple_ref[0, here, :], weight_ref[0:part, :])
            + dot(grad_triple_ref[1, here, :], weight_ref[part : 2 * part, :])
            + dot(grad_triple_ref[2, here, :], weight_ref[2 * part : 3 * part, :])
        ).astype(BF16)


def attend_backward(place, grads, triple, mixed_t, tail, weight):
    _, rows, part = triple.shape
    width = weight.shape[1]
    heads = part // HEAD_DIM
    pair = shape((2, rows // 4, width), BF16)
    return call(
        attend_backward_kernel,
        [pair, pair, shape((3, rows, part), BF16)],
        place, *grads, triple, mixed_t, tail, weight,
        scratch=[
            pltpu.VMEM((rows, part), BF16),
            pltpu.VMEM((part, rows), BF16),
            pltpu.VMEM((heads, rows), F32),
            pltpu.VMEM((part, rows), F32),
            pltpu.VMEM((rows, part), F32),
            pltpu.VMEM((rows, part), F32),
            pltpu.VMEM((rows, BLOCK), F32),
            pltpu.VMEM((1, rows), F32),
            pltpu.VMEM((rows, 128), F32),
            pltpu.VMEM((part, rows), BF16),
            pltpu.VMEM((part, rows), BF16),
        ],
        vmem=16,
        name="attend_backward",
    )


def mixer_kernel(
    place_ref, m0_ref, m1_ref, m2_ref, m3_ref, x_ref, mixer_ref, vectors_ref, _later_ref,
    normed_ref, middle_ref, mixed_ref,
):
    me = place_ref[0]
    half, double = m0_ref.shape
    part = double // 2
    middle = x_ref[...].astype(F32) + vector(vectors_ref, MIXER_BIAS)
    for slot, packed_ref in enumerate((m0_ref, m1_ref, m2_ref, m3_ref)):
        cols = slice(slot * part, (slot + 1) * part)
        mixed_ref[0:half, cols] = packed_ref[:, 0:part]
        mixed_ref[half : 2 * half, cols] = packed_ref[:, part:double]
        middle += dot(mixed_ref[:, cols], mixer_ref[rows_at(me ^ slot, part), :])
    middle_ref[...] = middle
    unit, _ = unit_rows(middle)
    normed_ref[...] = (unit * vector(vectors_ref, BACK_GAIN) + vector(vectors_ref, BACK_SHIFT)).astype(BF16)


def mixer_part(place, packed, x, mixer, vectors, later):
    rows, width = x.shape
    return call(
        mixer_kernel,
        [shape((rows, width), BF16), shape((rows, width), F32), shape((rows, width), BF16)],
        place, *packed, x, mixer, vectors, later,
        name="mixer_part",
    )


def feed_kernel(
    place_ref, normed_own_ref, normed_other_ref, cot_own_ref, cot_other_ref, expand_ref, reduce_ref, vectors_ref,
    second_ref, grad_ref, send_ref, active_ref, grad_hidden_ref, bias_sum_ref,
    total_ref, back_ref,
):
    side = place_ref[1]
    rows = normed_own_ref.shape[0]
    chunk = active_ref.shape[1] // 4
    lane = lax.broadcasted_iota(jnp.int32, (1, 2 * chunk), 1) // chunk
    total_ref[...] = jnp.zeros_like(total_ref)
    back_ref[...] = jnp.zeros_like(back_ref)

    def one_chunk(index, carry):
        block = pl.ds(pl.multiple_of((2 * index + side) * chunk, 128), chunk)
        expand = expand_ref[:, block]
        reduce = reduce_ref[block, :]
        bias = vectors_ref[pl.ds(EXPAND_BIAS + index, 1), pl.ds(pl.multiple_of(side * chunk, 128), chunk)]
        sums = jnp.zeros((1, chunk), F32)
        for part, (normed_ref, cot_ref) in enumerate(((normed_own_ref, cot_own_ref), (normed_other_ref, cot_other_ref))):
            here = slice(part * rows, (part + 1) * rows)
            cols = pl.ds(pl.multiple_of(index * chunk, 128), chunk)
            hidden = dot(normed_ref[...], expand) + bias
            square = hidden * hidden
            bend = jnp.tanh(GELU_A * hidden * (1.0 + GELU_B * square))
            half = 0.5 * (1.0 + bend)
            active = (hidden * half).astype(BF16)
            active_ref[here, cols] = active
            total_ref[here, :] += dot(active, reduce)
            slope = half + (0.5 * GELU_A) * hidden * (1.0 - bend * bend) * (1.0 + (3.0 * GELU_B) * square)
            grad_hidden = (dot(cot_ref[...], reduce, NT) * slope).astype(BF16)
            grad_hidden_ref[here, cols] = grad_hidden
            sums += column_sum(grad_hidden.astype(F32))
            back_ref[here, :] += dot(grad_hidden, expand, NT)
        bias_sum_ref[pl.ds(index, 1), :] = jnp.where(lane == side, jnp.concatenate([sums, sums], axis=1), 0.0)
        return carry

    lax.fori_loop(0, 4, one_chunk, 0)
    second_ref[...] = total_ref[0:rows, :]
    grad_ref[...] = back_ref[0:rows, :]
    send_ref[0] = back_ref[rows : 2 * rows, :].astype(BF16)
    send_ref[1] = total_ref[rows : 2 * rows, :].astype(BF16)


def feed_part(place, normed_own, normed_other, cot_own, cot_other, expand, reduce, vectors):
    rows, width = normed_own.shape
    hidden = expand.shape[1]
    return call(
        feed_kernel,
        [
            shape((rows, width), F32),
            shape((rows, width), F32),
            shape((2, rows, width), BF16),
            shape((2 * rows, hidden // 2), BF16),
            shape((2 * rows, hidden // 2), BF16),
            shape((4, width), F32),
        ],
        place, normed_own, normed_other, cot_own, cot_other, expand, reduce, vectors,
        scratch=[
            pltpu.VMEM((2 * rows, width), F32),
            pltpu.VMEM((2 * rows, width), F32),
        ],
        vmem=16,
        name="feed_part",
    )


def joint_kernel(
    place_ref, grad_own_ref, recv_ref, middle_ref, cot_ref, mixer_ref, vectors_ref,
    grad_middle_ref, grad_low_ref, g0_ref, g1_ref, g2_ref, g3_ref,
):
    me = place_ref[0]
    half, double = g0_ref.shape
    part = double // 2
    grad_normed = grad_own_ref[...] + recv_ref[0].astype(F32)
    unit, scale = unit_rows(middle_ref[...])
    back = norm_pullback(grad_normed, unit, scale, vector(vectors_ref, BACK_GAIN))
    grad_middle = cot_ref[...].astype(F32) + back
    grad_middle_ref[...] = grad_middle
    grad_low = grad_middle.astype(BF16)
    grad_low_ref[...] = grad_low
    for slot, packed_ref in enumerate((g0_ref, g1_ref, g2_ref, g3_ref)):
        grad = dot(grad_low, mixer_ref[rows_at(me ^ slot, part), :], NT).astype(BF16)
        packed_ref[:, 0:part] = grad[0:half, :]
        packed_ref[:, part:double] = grad[half : 2 * half, :]


def joint_part(place, *arrays):
    rows, width = arrays[0].shape
    part = width // 4
    return call(
        joint_kernel,
        [shape((rows, width), F32), shape((rows, width), BF16)] + [shape((rows // 2, 2 * part), BF16)] * 4,
        place, *arrays,
        name="joint_part",
    )


def outer_kernel(
    place_ref, second_ref, grad_own_ref, recv_ref, middle_ref, cot_ref, grad_low_ref, mixed_ref,
    tail_ref, vectors_ref, bias_sum_ref,
    out_ref, sums_ref, mixer_send_ref, mixer_keep_ref,
    total_ref, ids_row_ref, ids_ref,
):
    me, side = place_ref[0], place_ref[1]
    rows = cot_ref.shape[0]
    cot = cot_ref[...].astype(F32)
    unit, _ = unit_rows(middle_ref[...])
    pass_ids_of(tail_ref, ids_row_ref, ids_ref)
    grad_normed = grad_own_ref[...] + recv_ref[0].astype(F32)
    sums_ref[...] = jnp.zeros_like(sums_ref)
    passes = lax.broadcasted_iota(jnp.int32, (rows, 128), 1).astype(F32)
    chosen = (ids_ref[rows_at(me, rows), :] == passes).astype(BF16)
    table = vectors_ref[TABLE : TABLE + 5, :]
    embedded = dot(chosen, jnp.concatenate([table, jnp.zeros((123, table.shape[1]), F32)], axis=0).astype(BF16))
    sums_ref[SUM_TABLE : SUM_TABLE + 5, :] = dot(chosen, cot_ref[...], TN)[0:5, :]
    second = second_ref[...] + recv_ref[1].astype(F32) + vector(vectors_ref, REDUCE_BIAS)
    out_ref[...] = (middle_ref[...] + second + embedded).astype(BF16)
    sums_ref[SUM_COT : SUM_COT + 1, :] = column_sum(cot)
    sums_ref[SUM_MIXER : SUM_MIXER + 1, :] = column_sum(grad_low_ref[...].astype(F32))
    sums_ref[SUM_GAIN : SUM_GAIN + 1, :] = column_sum(grad_normed * unit)
    sums_ref[SUM_SHIFT : SUM_SHIFT + 1, :] = column_sum(grad_normed)
    sums_ref[SUM_EXPAND : SUM_EXPAND + 4, :] = bias_sum_ref[...]
    block = mixer_send_ref.shape[1]
    total_ref[...] = dot(mixed_ref[...], grad_low_ref[...], TN).astype(BF16)
    for slot in range(4):
        mixer_keep_ref[me ^ slot] = total_ref[rows_at(2 * slot + side, block), :]
        mixer_send_ref[me ^ slot] = total_ref[rows_at(2 * slot + (1 - side), block), :]


def outer_part(place, *arrays, seq_rows):
    rows, width = arrays[0].shape
    part = shape((4, width // 8, width), BF16)
    return call(
        outer_kernel,
        [shape((rows, width), BF16), shape((16, width), F32), part, part],
        place, *arrays,
        scratch=[pltpu.VMEM((width, width), BF16), pltpu.VMEM((1, seq_rows), F32), pltpu.VMEM((seq_rows, 128), F32)],
        name="outer_part",
    )


def flip(index):
    return ((index & 1) << 1) | (index >> 1)


def quarter_at(slot, quarter, side):
    return quarter ^ jnp.where(side == 0, flip(slot), slot)


def transposed_rows(out_ref, own_ref, other_ref, spare_ref, places):
    rows, width = own_ref.shape
    part = width // 4
    spare_ref[:, 0:rows] = own_ref[...].T
    spare_ref[:, rows : 2 * rows] = other_ref[...].T
    for index, place in enumerate(places):
        out_ref[index * part : (index + 1) * part, :] = spare_ref[rows_at(place, part), :]


def reduce_grads_kernel(place_ref, cot_own_ref, cot_other_ref, active_ref, send_ref, keep_ref, cot_t_ref, spare_ref):
    side, quarter, me_n = place_ref[1], place_ref[2], place_ref[3]
    chunk = active_ref.shape[1] // 4
    part = send_ref.shape[2]
    transposed_rows(cot_t_ref, cot_own_ref, cot_other_ref, spare_ref, [me_n ^ flip(index) for index in range(4)])
    for base, target in ((0, keep_ref), (2, send_ref)):

        def one_slot(step, carry, base=base, target=target):
            cols = pl.ds(pl.multiple_of(quarter_at(base + step, quarter, side) * chunk, 128), chunk)
            reduce = dot(cot_t_ref[...], active_ref[:, cols]).astype(BF16)
            for index in range(4):
                target[step, index] = reduce[index * part : (index + 1) * part, :]
            return carry

        lax.fori_loop(0, 2, one_slot, 0)


def reduce_grads(place, cot_own, cot_other, active):
    rows, width = cot_own.shape
    out = shape((2, 4, width // 4, active.shape[1] // 4), BF16)
    return call(
        reduce_grads_kernel,
        [out, out],
        place, cot_own, cot_other, active,
        scratch=[pltpu.VMEM((width, 2 * rows), BF16), pltpu.VMEM((width, 2 * rows), BF16)],
        name="reduce_grads",
    )


def expand_grads_kernel(
    place_ref, normed_own_ref, normed_other_ref, grad_hidden_ref, mixer_keep_ref, mixer_recv_ref,
    send_ref, keep_ref,
    normed_t_ref, spare_ref,
):
    side, quarter, me_n = place_ref[1], place_ref[2], place_ref[3]
    width = normed_own_ref.shape[1]
    chunk = grad_hidden_ref.shape[1] // 4
    high = width // 4
    quarters = [quarter_at(slot, quarter, side) for slot in range(4)]
    transposed_rows(normed_t_ref, normed_own_ref, normed_other_ref, spare_ref, quarters)

    def one_chunk(index, carry):
        cols = pl.ds(pl.multiple_of((me_n ^ flip(index)) * chunk, 128), chunk)
        expand = dot(normed_t_ref[...], grad_hidden_ref[:, cols]).astype(BF16)
        for slot in range(4):
            target = keep_ref if slot < 2 else send_ref
            target[slot % 2, index, 0:high, :] = expand[slot * high : (slot + 1) * high, :]
        return carry

    lax.fori_loop(0, 4, one_chunk, 0)
    for base, target in ((0, keep_ref), (2, send_ref)):

        def one_slot(step, carry, base=base, target=target):
            place = quarter_at(base + step, quarter, side)
            mixer = (mixer_keep_ref[place].astype(F32) + mixer_recv_ref[place].astype(F32)).astype(BF16)
            block = mixer.shape[0] // 2
            for other in range(4):
                piece = mixer[:, other * high : (other + 1) * high]
                target[step, flip(other ^ me_n), high:, :] = jnp.concatenate(
                    [piece[0:block, :], piece[block : 2 * block, :]], axis=1
                )
            return carry

        lax.fori_loop(0, 2, one_slot, 0)


def expand_grads(place, normed_own, normed_other, grad_hidden, mixer_keep, mixer_recv):
    rows, width = normed_own.shape
    out = shape((2, 4, width // 4 + width // 16, grad_hidden.shape[1] // 4), BF16)
    return call(
        expand_grads_kernel,
        [out, out],
        place, normed_own, normed_other, grad_hidden, mixer_keep, mixer_recv,
        scratch=[pltpu.VMEM((width, 2 * rows), BF16), pltpu.VMEM((width, 2 * rows), BF16)],
        name="expand_grads",
    )


def triple_grads_kernel(
    place_ref, x0_ref, x1_ref, x2_ref, x3_ref, near_ref, far_ref, normed_ref, grad_triple_ref, sums_in_ref,
    t0_ref, t1_ref, t2_ref, t3_ref, packet_ref, sums_ref,
    weight_ref,
):
    me, corner = place_ref[0], place_ref[7]
    rows, width = normed_ref.shape
    part = grad_triple_ref.shape[2]
    def sum_block(step, sums):
        here = rows_at(step, 64)
        gain_sum, shift_sum = sums
        for slot, x_ref in enumerate((x0_ref, x1_ref, x2_ref, x3_ref)):
            unit, _ = unit_rows(x_ref[here, :].astype(F32))
            grad = (near_ref if slot < 2 else far_ref)[slot % 2, here, :].astype(F32)
            gain_sum += (grad * unit).reshape(8, 8, width).sum(axis=0)
            shift_sum += grad.reshape(8, 8, width).sum(axis=0)
        return gain_sum, shift_sum

    gain_sum, shift_sum = lax.fori_loop(
        0, rows // 256, sum_block, (jnp.zeros((8, width), F32), jnp.zeros((8, width), F32))
    )
    gain_sum, shift_sum = column_sum(gain_sum), column_sum(shift_sum)
    sums_ref[0:16, :] = sums_in_ref[...]
    sums_ref[16:24, :] = jnp.zeros((8, width), F32)
    sums_ref[SUM_FRONT_GAIN : SUM_FRONT_GAIN + 1, :] = gain_sum
    sums_ref[SUM_FRONT_SHIFT : SUM_FRONT_SHIFT + 1, :] = shift_sum
    group = lax.broadcasted_iota(jnp.int32, (1, width), 1) // part
    for row, index in ((0, 0), (1, 2)):
        bias = column_sum(grad_triple_ref[index].astype(F32))
        sums_ref[SUM_TRIPLE + row : SUM_TRIPLE + row + 1, :] = jnp.where(
            group == me, jnp.concatenate([bias] * (width // part), axis=1), 0.0
        )
    for index in range(3):
        weight_ref[index * part : (index + 1) * part, :] = dot(grad_triple_ref[index], normed_ref[...], TN).astype(BF16)
    piece = 3 * part // 4
    for slot, target in enumerate((t0_ref, t1_ref, t2_ref, t3_ref)):
        target[...] = weight_ref[rows_at(corner ^ slot, piece), :]
    local = far_ref.shape[1]
    packet_ref[0:local, :] = far_ref[0]
    packet_ref[local : 2 * local, :] = far_ref[1]
    put_sums(packet_ref, 2 * local, sums_ref[...])


def triple_grads(place, shards, near, far, normed, grad_triple, sums):
    rows, width = normed.shape
    part = grad_triple.shape[2]
    return call(
        triple_grads_kernel,
        [shape((3 * part // 4, width), BF16)] * 4
        + [shape((rows // 2 + 2 * SUMS, width), BF16), shape((SUMS, width), F32)],
        place, *shards, near, far, normed, grad_triple, sums,
        scratch=[pltpu.VMEM((3 * part, width), BF16)],
        vmem=16,
        name="triple_grads",
    )


def pair_kernel(place_ref, near_ref, sent_ref, recv_ref, packet_ref, own_ref):
    local = near_ref.shape[1]
    own_ref[...] = near_ref[0].astype(F32) + recv_ref[0:local, :].astype(F32)
    packet_ref[0:local, :] = (near_ref[1].astype(F32) + recv_ref[local : 2 * local, :].astype(F32)).astype(BF16)
    put_sums(packet_ref, local, get_sums(sent_ref, 2 * local) + get_sums(recv_ref, 2 * local))


def pair_part(place, near, sent, recv):
    _, local, width = near.shape
    return call(
        pair_kernel,
        [shape((local + 2 * SUMS, width), BF16), shape((local, width), F32)],
        place, near, sent, recv,
        name="pair_part",
    )


def home_kernel(place_ref, t0_ref, t1_ref, t2_ref, t3_ref, sent_ref, recv_ref, packet_ref):
    piece = t0_ref.shape[0]
    local = sent_ref.shape[0] - 2 * SUMS
    total = t0_ref[...].astype(F32) + t1_ref[...].astype(F32) + t2_ref[...].astype(F32) + t3_ref[...].astype(F32)
    packet_ref[0:piece, :] = total.astype(BF16)
    put_sums(packet_ref, piece, get_sums(sent_ref, local) + get_sums(recv_ref, local))


def home_part(place, pieces, sent, recv):
    piece, width = pieces[0].shape
    return call(
        home_kernel, [shape((piece + 2 * SUMS, width), BF16)], place, *pieces, sent, recv, name="home_part"
    )[0]


def front_kernel(place_ref, x_ref, own_ref, recv_ref, grad_middle_ref, vectors_ref, out_ref):
    unit, scale = unit_rows(x_ref[...].astype(F32))
    grad = own_ref[...] + recv_ref[0 : own_ref.shape[0], :].astype(F32)
    back = norm_pullback(grad, unit, scale, vector(vectors_ref, FRONT_GAIN))
    out_ref[...] = (grad_middle_ref[...] + back).astype(BF16)


def front_part(place, x, *arrays):
    return call(front_kernel, [shape(x.shape, BF16)], place, x, *arrays, name="front_part")[0]


def spread_kernel(place_ref, sent_ref, recv_ref, packet_ref):
    piece = sent_ref.shape[0] - 2 * SUMS
    packet_ref[0:piece, :] = (sent_ref[0:piece, :].astype(F32) + recv_ref[0:piece, :].astype(F32)).astype(BF16)
    put_sums(packet_ref, piece, get_sums(sent_ref, piece) + get_sums(recv_ref, piece))


def spread_part(place, sent, recv):
    return call(spread_kernel, [shape(sent.shape, BF16)], place, sent, recv, name="spread_part")[0]


def last_kernel(place_ref, s0_ref, s1_ref, s2_ref, s3_ref, a_ref, b_ref, c_ref, packet_ref, total_ref):
    side, corner = place_ref[1], place_ref[7]
    piece = s0_ref.shape[0] - 2 * SUMS
    for slot, ref in enumerate((s0_ref, s1_ref, s2_ref, s3_ref)):
        packet_ref[rows_at(corner ^ slot, piece), :] = ref[0:piece, :]
    put_sums(
        packet_ref,
        4 * piece,
        (get_sums(s0_ref, piece) + get_sums(s1_ref, piece)) + (get_sums(s2_ref, piece) + get_sums(s3_ref, piece)),
    )
    total_ref[...] = a_ref[0].astype(F32) + b_ref[0].astype(F32) + c_ref[...].astype(F32)
    half = (packet_ref.shape[0] - 4 * piece - 2 * SUMS)
    chunk = total_ref.shape[1]
    start = 4 * piece + 2 * SUMS
    packet_ref[start:, 0:chunk] = total_ref[rows_at(2 * (1 - side), half), :].astype(BF16)
    packet_ref[start:, chunk : 2 * chunk] = total_ref[rows_at(2 * (1 - side) + 1, half), :].astype(BF16)


def last_part(place, packets, a, b, c):
    rows, width = packets[0].shape
    piece = rows - 2 * SUMS
    block = width // 8
    return call(
        last_kernel,
        [shape((4 * piece + 2 * SUMS + block // 2, width), BF16), shape(c.shape, F32)],
        place, *packets, a, b, c,
        name="last_part",
    )


def results_kernel(
    place_ref, sent_ref, recv_ref, total_ref,
    triple_ref, expand_ref, mixer_ref, triple_bias_ref, table_ref,
    front_gain_ref, front_shift_ref, mixer_bias_ref, back_gain_ref, back_shift_ref, expand_bias_ref, reduce_bias_ref,
    sums_ref,
):
    side, me_n, stay = place_ref[1], place_ref[3], place_ref[5]
    weights, width = triple_ref.shape
    part = mixer_ref.shape[1]

    @pl.when(stay == 1)
    def _():
        triple_ref[...] = sent_ref[0:weights, :].astype(F32)
        sums_ref[...] = get_sums(sent_ref, weights)

    @pl.when(stay == 0)
    def _():
        triple_ref[...] = recv_ref[0:weights, :].astype(F32)
        sums_ref[...] = get_sums(recv_ref, weights)

    block, double = expand_ref.shape
    chunk, half = double // 2, block // 2
    start = weights + 2 * SUMS
    for index in range(2):
        mine = total_ref[rows_at(2 * side + index, half), :]
        other = recv_ref[start:, index * chunk : (index + 1) * chunk].astype(F32)
        first = jnp.full(mine.shape, side, jnp.int32) == 0
        here = slice(index * half, (index + 1) * half)
        expand_ref[here, 0:chunk] = jnp.where(first, mine, other)
        expand_ref[here, chunk:double] = jnp.where(first, other, mine)
        mixer_ref[here, :] = total_ref[2 * block :, index * part : (index + 1) * part]
    pair = sums_ref[SUM_TRIPLE : SUM_TRIPLE + 2, :]
    bias = jnp.zeros((2, part), F32)
    for group in range(width // part):
        mine = jnp.full(bias.shape, me_n, jnp.int32) == group
        bias = jnp.where(mine, pair[:, group * part : (group + 1) * part], bias)
    triple_bias_ref[...] = bias
    table_ref[...] = sums_ref[SUM_TABLE : SUM_TABLE + table_ref.shape[0], :]
    for index, ref in (
        (SUM_FRONT_GAIN, front_gain_ref), (SUM_FRONT_SHIFT, front_shift_ref), (SUM_MIXER, mixer_bias_ref),
        (SUM_GAIN, back_gain_ref), (SUM_SHIFT, back_shift_ref), (SUM_COT, reduce_bias_ref),
    ):
        ref[...] = sums_ref[index : index + 1, :].reshape(width)
    for index in range(4):
        expand_bias_ref[index * width : (index + 1) * width] = (
            sums_ref[SUM_EXPAND + index : SUM_EXPAND + index + 1, :].reshape(width)
        )


def early_results_kernel(place_ref, ra_ref, rb_ref, rc_ref, layer_ref, rows_ref, reduce_ref, layer_out_ref, rows_out_ref):
    reduce_ref[...] = ra_ref[0].astype(F32) + rb_ref[0].astype(F32) + rc_ref[...].astype(F32)
    layer_out_ref[...] = layer_ref[...]
    rows_out_ref[...] = rows_ref[...]


def early_results(place, ra, rb, rc, layer, rows):
    return call(
        early_results_kernel,
        [shape(rc.shape, F32), shape(layer.shape, BF16), shape(rows.shape, BF16)],
        place, ra, rb, rc, layer, rows,
        name="early_results",
    )


def results(place, sent, recv, total, passes):
    width = sent.shape[1]
    block = width // 8
    piece = (sent.shape[0] - 2 * SUMS - block // 2) // 4
    row = shape((width,), F32)
    return call(
        results_kernel,
        [
            shape((4 * piece, width), F32), shape((block, width), F32), shape((block, width // 4), F32),
            shape((2, width // 4), F32), shape((passes, width), F32),
            row, row, row, row, row, shape((4 * width,), F32), row,
        ],
        place, sent, recv, total,
        scratch=[pltpu.VMEM((SUMS, width), F32)],
        name="results",
    )


def after(value, *earlier):
    return lax.optimization_barrier((value, earlier))[0]


def body(
    inputs,
    pass_ids,
    front_gain,
    front_shift,
    triple_weight,
    triple_bias,
    mixer_weight,
    mixer_bias,
    back_gain,
    back_shift,
    expand_weight,
    expand_bias,
    reduce_weight,
    reduce_bias,
    pass_table,
    cotangent,
):
    width = inputs.shape[1]
    part = triple_weight.shape[2]
    wide_size, narrow_size = lax.axis_size("wide"), lax.axis_size("narrow")
    low_bits = wide_size.bit_length() - 4
    side_bit, x_bit, y_bit = 1 << low_bits, 2 << low_bits, 4 << low_bits

    wide, narrow = lax.axis_index("wide"), lax.axis_index("narrow")
    c, h, l = wide & 1, narrow >> 1, narrow & 1
    me = 2 * c + l
    top = wide >> low_bits
    side, quarter = top & 1, top >> 1
    x1, y1 = (wide >> 1) & 1, (wide >> 2) & 1
    stay = (c == h).astype(jnp.int32)
    corner = 2 * y1 + x1
    place = jnp.stack(
        [
            me, side, quarter, narrow,
            jnp.where(c == 0, 2 * x1 + y1, corner),
            stay,
            jnp.where(h == 0, 2 * x1 + y1, corner),
            corner,
        ]
    ).astype(jnp.int32)

    def send(name, value, target):
        pairs = []
        for w in range(wide_size):
            for n in range(narrow_size):
                to = target(w, n)
                if to is not None:
                    pairs.append((w * narrow_size + n, to[0] * narrow_size + to[1]))
        with jax.named_scope(name):
            return lax.ppermute(value, AXES, pairs)

    def stays(w, n):
        return (w & 1) == (n >> 1)

    def moved(w, n):
        return (w, n) if stays(w, n) else (w ^ 1, n ^ 2)

    def home(w, n):
        return None if stays(w, n) else (w, n ^ 2)

    def lend(w, n):
        return (w, n ^ 2) if stays(w, n) else None

    def core(w, n):
        return (w ^ 1, n)

    def pair(w, n):
        return (w, n ^ 1)

    def diagonal(w, n):
        return (w ^ 1, n ^ 1)

    def across(w, n):
        return (w, n ^ 2)

    def sided(w, n):
        return (w ^ side_bit, n)

    def first(w, n):
        return (w ^ (y_bit if w & side_bit else x_bit), n)

    def second(w, n):
        return (w ^ (x_bit if w & side_bit else y_bit), n)

    def step_x(w, n):
        return (w ^ 2, n)

    def step_y(w, n):
        return (w ^ 4, n)

    def step_xy(w, n):
        return (w ^ 6, n)

    def of_stay(target):
        return lambda w, n: target(w, n) if stays(w, n) else None

    def of_moved(target):
        return lambda w, n: None if stays(w, n) else target(w, n)

    def add(*terms):
        return sum(t.astype(F32) for t in terms).astype(BF16)

    together = lax.optimization_barrier

    weight_t = jnp.swapaxes(triple_weight, 1, 2).reshape(3 * part, width)
    piece = 3 * part // 4
    lent = lax.dynamic_slice_in_dim(weight_t, corner * piece, piece)
    place, lent = together((place, lent))
    p0 = send("lend_weight", lent, lend)
    x0 = send("rows_move", after(inputs, lent), moved)
    x1_stay = send("rows_pair", inputs, of_stay(pair))
    vectors, tail = gather_vectors(
        place, triple_bias, pass_ids,
        front_gain, front_shift, mixer_bias, back_gain, back_shift, reduce_bias, expand_bias, pass_table,
    )
    tail = send("tail_move", tail, moved)
    x0, p0, x1_stay, vectors, tail = together((x0, p0, x1_stay, vectors, tail))
    x1_moved = send("rows_pair", x0, of_moved(pair))
    p1, p2, p3 = (send("lent", p0, of_moved(step)) for step in (step_x, step_y, step_xy))
    x1_moved, p1, p2, p3 = together((x1_moved, p1, p2, p3))
    x1_rows = jnp.where(stay == 1, x1_stay, x1_moved)
    x2 = send("rows_core", x0, core)
    x3 = send("pair_core", x1_rows, core)
    cot_own = send("cot_move", after(cotangent, x1_rows), moved)

    shards = (x0, x1_rows, x2, x3)
    m0, m1, m2, m3, mixed_t, normed, triple, weight = attend_forward(
        place, shards, tail, vectors, weight_t, (p0, p1, p2, p3)
    )
    m1, m2, m3, cot_own = together(
        (send("m_pair", m1, pair), send("m_core", m2, core), send("m_diagonal", m3, diagonal), cot_own)
    )
    cot_other = send("cot_core", cot_own, sided)
    normed_two, middle, mixed_rows = mixer_part(place, (m0, m1, m2, m3), x0, mixer_weight, vectors, reduce_weight)
    normed_other, cot_other = together((send("normed_core", normed_two, sided), cot_other))
    second_own, grad_own, feed_send, active, grad_hidden, bias_sums = feed_part(
        place, normed_two, normed_other, cot_own, cot_other, expand_weight, reduce_weight, vectors
    )
    feed_recv = send("feed_core", feed_send, sided)
    reduce_send, reduce_keep = reduce_grads(place, cot_own, cot_other, active)
    grad_own, feed_recv, reduce_send = together((grad_own, feed_recv, reduce_send))
    reduce_first = send("reduce_first", reduce_send, first)
    grad_middle, grad_low, g0, g1, g2, g3 = joint_part(
        place, grad_own, feed_recv, middle, cot_own, mixer_weight, vectors
    )
    g1, g2, g3 = send("g_pair", g1, pair), send("g_core", g2, core), send("g_diagonal", g3, diagonal)
    out_rows, sums, mixer_send, mixer_keep = outer_part(
        place, second_own, grad_own, feed_recv, middle, cot_own, grad_low, mixed_rows, tail, vectors, bias_sums,
        seq_rows=pass_ids.shape[1],
    )
    mixer_recv = send("mixer_core", mixer_send, sided)
    expand_send, expand_keep = expand_grads(
        place, normed_two, normed_other, grad_hidden, mixer_keep, mixer_recv
    )
    g1, g2, g3, expand_send, expand_keep, out_rows, reduce_first = together(
        (g1, g2, g3, expand_send, expand_keep, out_rows, reduce_first)
    )
    reduce_second = send("reduce_second", add(reduce_keep[1], reduce_first[1]), second)
    expand_first = send("expand_first", expand_send, first)
    layer_out = send("out_move", out_rows, moved)
    near, far, grad_triple_rows = attend_backward(
        place, (g0, g1, g2, g3), triple, mixed_t, tail, weight
    )

    def halved(keep, first_recv, second_recv):
        return (
            add(keep[0, 0:2], first_recv[0, 0:2], second_recv[0:2]),
            add(keep[0, 2:4], first_recv[0, 2:4], second_recv[2:4]),
        )

    far, near, grad_triple_rows, reduce_second, layer_out = together(
        (far, near, grad_triple_rows, reduce_second, layer_out)
    )
    reduce_a, reduce_b = halved(reduce_keep, reduce_first, reduce_second)
    reduce_pair = send("reduce_pair", reduce_b, pair)
    t0, t1, t2, t3, core_packet, all_sums = triple_grads(place, shards, near, far, normed, grad_triple_rows, sums)
    core_packet = after(core_packet, reduce_pair)
    core_recv, expand_first = together((send("far_core", core_packet, core), expand_first))

    pair_packet, own_rows = pair_part(place, near, core_packet, core_recv)
    pair_recv = send("near_pair", pair_packet, pair)
    t1, t2, t3 = send("triple_x", t1, step_x), send("triple_y", t2, step_y), send("triple_xy", t3, step_xy)
    expand_second = send("expand_second", add(expand_keep[1], expand_first[1]), second)
    reduce_across = send("reduce_across", add(reduce_a[1], reduce_pair[1]), across)
    t1, t2, t3, pair_recv, expand_second, reduce_across = together(
        (t1, t2, t3, pair_recv, expand_second, reduce_across)
    )

    home_packet = home_part(place, (t0, t1, t2, t3), pair_packet, pair_recv)
    home_recv = send("triple_home", home_packet, home)
    grad_rows = front_part(place, x0, own_rows, pair_recv, grad_middle, vectors)
    grad_inputs = send("rows_home", grad_rows, moved)
    expand_a, expand_b = halved(expand_keep, expand_first, expand_second)
    expand_pair = send("expand_pair", expand_b, pair)
    home_recv, expand_pair, grad_rows = together((home_recv, expand_pair, grad_rows))

    spread = spread_part(place, home_packet, home_recv)
    s1, s2, s3 = (send("triple_spread", spread, of_stay(step)) for step in (step_x, step_y, step_xy))
    expand_across = send("expand_across", add(expand_a[1], expand_pair[1]), across)
    s1, s2, s3, expand_across, grad_inputs = together((s1, s2, s3, expand_across, grad_inputs))

    last_packet, total = last_part(place, (spread, s1, s2, s3), expand_a, expand_pair, expand_across)
    last_recv = send("last_core", last_packet, core)
    total_reduce, layer_out, grad_inputs = early_results(
        place, reduce_a, reduce_pair, after(reduce_across, last_packet), layer_out, grad_inputs
    )
    last_recv, total_reduce, layer_out, grad_inputs = together((last_recv, total_reduce, layer_out, grad_inputs))
    (
        grad_triple, total_expand, total_mixer, grad_triple_bias, grad_table,
        grad_front_gain, grad_front_shift, grad_mixer_bias, grad_back_gain, grad_back_shift, grad_expand_bias,
        grad_reduce_bias,
    ) = results(place, last_packet, last_recv, total, pass_table.shape[0])
    grad_triple = jnp.swapaxes(grad_triple.reshape(3, part, width), 1, 2)
    if low_bits:
        size = 1 << low_bits
        peers = [[size * i + j for j in range(size)] for i in range(wide_size // size)]
        total_expand, total_reduce, total_mixer = (
            lax.psum_scatter(t, "wide", scatter_dimension=d, axis_index_groups=peers, tiled=True)
            for t, d in ((total_expand, 0), (total_reduce, 1), (total_mixer, 0))
        )
        peers = [[i + 8 * j for j in range(wide_size // 8)] for i in range(8)]
        (
            grad_triple, grad_triple_bias, grad_table, grad_front_gain, grad_front_shift, grad_mixer_bias,
            grad_back_gain, grad_back_shift, grad_expand_bias, grad_reduce_bias,
        ) = lax.psum(
            (
                grad_triple, grad_triple_bias, grad_table, grad_front_gain, grad_front_shift, grad_mixer_bias,
                grad_back_gain, grad_back_shift, grad_expand_bias, grad_reduce_bias,
            ),
            "wide", axis_index_groups=peers,
        )
    return (
        layer_out,
        grad_inputs,
        grad_front_gain,
        grad_front_shift,
        grad_triple,
        grad_triple_bias,
        total_mixer,
        grad_mixer_bias,
        grad_back_gain,
        grad_back_shift,
        total_expand,
        grad_expand_bias,
        total_reduce.T,
        grad_reduce_bias,
        grad_table,
    )


def solution(mesh):
    rows = P(AXES, None)
    block = P("wide", "narrow")
    return jax.shard_map(
        body,
        mesh=mesh,
        in_specs=(
            rows, P("wide", None), P(), P(), P(None, None, "narrow"), P(None, "narrow"),
            P(), P(), P(), P(), P(), P(), P(), P(), P(), rows,
        ),
        out_specs=(
            rows, rows, P(), P(), P(None, None, "narrow"), P(None, "narrow"), block,
            P(), P(), P(), block, P(), block, P(), P(),
        ),
        check_vma=False,
    )
```

```python
import math

import jax
import jax.numpy as jnp
from jax import lax
from jax.experimental import pallas as pl
from jax.experimental.pallas import tpu as pltpu
from jax.sharding import PartitionSpec as P


HEAD_DIM = 64
EPSILON = 1e-05
BLOCK = 256
LONG_FORWARD, LONG_BACKWARD = 768, 1280
HIDDEN = -1e30
F32 = jnp.float32
BF16 = jnp.bfloat16
MIB = 1024 * 1024
AXES = ("wide", "narrow")
NN = (((1,), (0,)), ((), ()))
NT = (((1,), (1,)), ((), ()))
TN = (((0,), (0,)), ((), ()))
GELU_A = math.sqrt(2.0 / math.pi)
GELU_B = 0.044715
shape = jax.ShapeDtypeStruct

FRONT_GAIN, FRONT_SHIFT, MIXER_BIAS, BACK_GAIN, BACK_SHIFT, REDUCE_BIAS, EXPAND_BIAS, TABLE = 0, 1, 2, 3, 4, 5, 6, 10
SUM_TABLE, SUM_COT, SUM_MIXER, SUM_GAIN, SUM_SHIFT, SUM_EXPAND = 0, 5, 6, 7, 8, 9
SUM_FRONT_GAIN, SUM_FRONT_SHIFT, SUM_TRIPLE = 16, 17, 18
SUMS = 24


def dot(left, right, dims=NN):
    return lax.dot_general(left, right, dims, preferred_element_type=F32)


def whole():
    return pl.BlockSpec(memory_space=pltpu.VMEM)


def call(kernel, outs, *arrays, scratch=(), vmem=12, name=None):
    return pl.pallas_call(
        kernel,
        out_shape=tuple(outs),
        in_specs=[pl.BlockSpec(memory_space=pltpu.SMEM)] + [whole()] * (len(arrays) - 1),
        out_specs=(whole(),) * len(outs),
        scratch_shapes=list(scratch),
        compiler_params=pltpu.CompilerParams(vmem_limit_bytes=vmem * MIB),
        name=name,
    )(*arrays)


def unit_rows(values):
    centred = values - jnp.mean(values, axis=-1, keepdims=True)
    scale = lax.rsqrt(jnp.mean(centred * centred, axis=-1, keepdims=True) + EPSILON)
    return centred * scale, scale


def norm_pullback(grad_out, unit, scale, gain):
    grad_unit = grad_out * gain
    inner = (
        grad_unit
        - jnp.mean(grad_unit, axis=-1, keepdims=True)
        - unit * jnp.mean(grad_unit * unit, axis=-1, keepdims=True)
    )
    return inner * scale


def column_sum(values):
    return jnp.sum(values, axis=0, keepdims=True)


def put_sums(packet_ref, start, sums):
    high = sums.astype(BF16).astype(F32)
    packet_ref[start : start + 2 * SUMS, :] = jnp.concatenate([high, sums - high], axis=0).astype(BF16)


def get_sums(packet_ref, start):
    both = packet_ref[start : start + 2 * SUMS, :].astype(F32)
    return both[0:SUMS, :] + both[SUMS : 2 * SUMS, :]


def keep_head(block, head, axis):
    place = lax.broadcasted_iota(jnp.int32, block.shape, axis) // HEAD_DIM
    return jnp.where(place == head, block, jnp.zeros_like(block))


def rows_at(index, count):
    if isinstance(index, int):
        return slice(index * count, (index + 1) * count)
    return pl.ds(pl.multiple_of(index * count, math.gcd(count, 64)), count)


def each_head(heads, one_head, looped):
    if looped:
        lax.fori_loop(0, heads, lambda head, carry: one_head(head) or carry, 0)
    else:
        for head in range(heads):
            one_head(head)


def vector(vectors_ref, index):
    return vectors_ref[index : index + 1, :]


def pass_ids_of(tail_ref, row_ref, col_ref):
    width = tail_ref.shape[1]
    rows = row_ref.shape[1]
    tail = tail_ref[...].astype(F32)
    row_ref[:, 0:width] = tail[1:2, :]
    row_ref[:, width:rows] = tail[2:3, 0 : rows - width]
    for start in range(0, rows, BLOCK):
        col_ref[start : start + BLOCK, :] = jnp.broadcast_to(row_ref[:, start : start + BLOCK], (128, BLOCK)).T


def visibility(ids_col_ref, ids_row_ref, start, keys):
    seen = ids_col_ref[0:keys, 0:1] <= ids_row_ref[:, start : start + BLOCK]
    key_place = lax.broadcasted_iota(jnp.int32, (keys, BLOCK), 0)
    query_place = lax.broadcasted_iota(jnp.int32, (keys, BLOCK), 1) + start
    return jnp.where(seen & (key_place <= query_place), 0.0, HIDDEN).astype(F32)


def vectors_kernel(place_ref, bias_ref, ids_ref, *refs):
    tail_ref, out_ref, table_ref, long_ref = refs[-1], refs[-2], refs[-3], refs[-4]
    width = out_ref.shape[1]
    out_ref[...] = jnp.zeros_like(out_ref)
    for index, ref in enumerate(refs[:-4]):
        out_ref[index : index + 1, :] = ref[...].astype(F32).reshape(1, width)
    long = long_ref[...].astype(F32).reshape(1, long_ref.shape[0])
    for index in range(long_ref.shape[0] // width):
        out_ref[EXPAND_BIAS + index : EXPAND_BIAS + index + 1, :] = long[:, index * width : (index + 1) * width]
    out_ref[TABLE : TABLE + table_ref.shape[0], :] = table_ref[...].astype(F32)
    ids = ids_ref[...].astype(F32)
    bias = bias_ref[...].astype(F32)
    rest, double = ids.shape[1] - width, 2 * bias.shape[1]
    tail = [
        jnp.concatenate([bias[0:1, :], bias[1:2, :], jnp.zeros((1, width - double), F32)], axis=1),
        ids[:, 0:width],
        jnp.concatenate([ids[:, width:], jnp.zeros((1, width - rest), F32)], axis=1),
        jnp.zeros((13, width), F32),
    ]
    tail_ref[...] = jnp.concatenate(tail, axis=0).astype(BF16)


def gather_vectors(place, bias, ids, *arrays):
    width = arrays[0].shape[0]
    return call(
        vectors_kernel,
        [shape((16, width), F32), shape((16, width), BF16)],
        place, bias, ids, *arrays,
        vmem=4,
        name="gather_vectors",
    )


def attend_forward_kernel(
    place_ref, x0_ref, x1_ref, x2_ref, x3_ref, tail_ref, vectors_ref, weight_own_ref, p0_ref, p1_ref, p2_ref, p3_ref,
    m0_ref, m1_ref, m2_ref, m3_ref, mixed_t_ref, normed_ref, triple_ref, weight_ref,
    ids_row_ref, ids_col_ref, q_t_ref, v_t_ref, bias_t_ref, mixed_ref, straight_ref,
):
    me, stay, corner = place_ref[0], place_ref[5], place_ref[7]
    _, rows, part = triple_ref.shape
    local = x0_ref.shape[0]
    piece = p0_ref.shape[0]
    heads = part // HEAD_DIM
    gain = vector(vectors_ref, FRONT_GAIN)
    shift = vector(vectors_ref, FRONT_SHIFT)
    pass_ids_of(tail_ref, ids_row_ref, ids_col_ref)

    @pl.when(stay == 1)
    def _():
        weight_ref[...] = weight_own_ref[...]

    @pl.when(stay == 0)
    def _():
        for slot, value in enumerate((p0_ref, p1_ref, p2_ref, p3_ref)):
            weight_ref[rows_at(corner ^ slot, piece), :] = value[...]

    straight_ref[...] = weight_ref[...].T
    bias = tail_ref[...].astype(F32)[0:1, 0 : 2 * part]
    for slot, x_ref in enumerate((x0_ref, x1_ref, x2_ref, x3_ref)):
        here = rows_at(me ^ slot, local)
        unit, _ = unit_rows(x_ref[...].astype(F32))
        normed = (unit * gain + shift).astype(BF16)
        normed_ref[here, :] = normed
        q = (dot(normed, straight_ref[:, 0:part]) + bias[:, 0:part]).astype(BF16)
        triple_ref[0, here, :] = q * jnp.asarray(HEAD_DIM**-0.5, BF16)
        triple_ref[1, here, :] = dot(normed, straight_ref[:, part : 2 * part]).astype(BF16)
        triple_ref[2, here, :] = (dot(normed, straight_ref[:, 2 * part : 3 * part]) + bias[:, part : 2 * part]).astype(BF16)

    for start in range(0, rows, BLOCK):
        cols = slice(start, start + BLOCK)
        q_t_ref[:, cols] = triple_ref[0, cols, :].T
        v_t_ref[:, cols] = triple_ref[2, cols, :].T

    mixed_t_ref[part : part + 8, :] = jnp.zeros((8, rows), F32)
    for start in range(0, rows, BLOCK):
        keys = start + BLOCK
        cols = slice(start, keys)
        bias_t_ref[0:keys, :] = visibility(ids_col_ref, ids_row_ref, start, keys)

        def one_head(head, keys=keys, cols=cols):
            here = rows_at(head, HEAD_DIM)
            scores = dot(triple_ref[1, 0:keys, :], keep_head(q_t_ref[:, cols], head, 0)) + bias_t_ref[0:keys, :]
            top = jnp.max(scores, axis=0, keepdims=True)
            weights = jnp.exp(scores - top)
            total = jnp.sum(weights, axis=0, keepdims=True)
            mixed_t_ref[here, cols] = dot(v_t_ref[here, 0:keys], weights.astype(BF16)) / total
            mixed_t_ref[pl.ds(part + head, 1), cols] = top + jnp.log(total)

        each_head(heads, one_head, keys > LONG_FORWARD)
        mixed_ref[cols, :] = mixed_t_ref[0:part, cols].T.astype(BF16)
    for slot, out_ref in enumerate((m0_ref, m1_ref, m2_ref, m3_ref)):
        pack_rows(out_ref, mixed_ref, me ^ slot)


def pack_rows(out_ref, rows_ref, index):
    half, part = out_ref.shape[0], out_ref.shape[1] // 2
    out_ref[:, 0:part] = rows_ref[rows_at(2 * index, half), :]
    out_ref[:, part : 2 * part] = rows_ref[rows_at(2 * index + 1, half), :]


def unpack_rows(rows_ref, packed_ref, index):
    half, part = packed_ref.shape[0], packed_ref.shape[1] // 2
    rows_ref[rows_at(2 * index, half), :] = packed_ref[:, 0:part]
    rows_ref[rows_at(2 * index + 1, half), :] = packed_ref[:, part : 2 * part]


def attend_forward(place, shards, tail, vectors, weight, pieces):
    local, width = shards[0].shape
    rows = 4 * local
    part = weight.shape[0] // 3
    return call(
        attend_forward_kernel,
        [shape((local // 2, 2 * part), BF16)] * 4
        + [
            shape((part + 8, rows), F32),
            shape((rows, width), BF16),
            shape((3, rows, part), BF16),
            shape(weight.shape, BF16),
        ],
        place, *shards, tail, vectors, weight, *pieces,
        scratch=[
            pltpu.VMEM((1, rows), F32),
            pltpu.VMEM((rows, 128), F32),
            pltpu.VMEM((part, rows), BF16),
            pltpu.VMEM((part, rows), BF16),
            pltpu.VMEM((rows, BLOCK), F32),
            pltpu.VMEM((rows, part), BF16),
            pltpu.VMEM((width, 3 * part), BF16),
        ],
        vmem=16,
        name="attend_forward",
    )


def attend_backward_kernel(
    place_ref, g0_ref, g1_ref, g2_ref, g3_ref, triple_ref, mixed_t_ref, tail_ref, weight_ref,
    near_ref, far_ref, grad_triple_ref,
    grad_ref, grad_t_ref, delta_ref, grad_q_t_ref, grad_k_ref, grad_v_ref, bias_t_ref,
    ids_row_ref, ids_col_ref, q_t_ref, k_t_ref,
):
    me = place_ref[0]
    _, rows, part = triple_ref.shape
    local = near_ref.shape[1]
    heads = part // HEAD_DIM
    for slot, packed_ref in enumerate((g0_ref, g1_ref, g2_ref, g3_ref)):
        unpack_rows(grad_ref, packed_ref, me ^ slot)
    pass_ids_of(tail_ref, ids_row_ref, ids_col_ref)
    for start in range(0, rows, BLOCK):
        cols = slice(start, start + BLOCK)
        q_t_ref[:, cols] = triple_ref[0, cols, :].T
        k_t_ref[:, cols] = triple_ref[1, cols, :].T
        grad_t = grad_ref[cols, :].T
        grad_t_ref[:, cols] = grad_t
        product = grad_t.astype(F32) * mixed_t_ref[0:part, cols]
        for head in range(heads):
            delta_ref[head : head + 1, cols] = column_sum(product[head * HEAD_DIM : (head + 1) * HEAD_DIM, :])
    grad_k_ref[...] = jnp.zeros_like(grad_k_ref)
    grad_v_ref[...] = jnp.zeros_like(grad_v_ref)
    for start in range(0, rows, BLOCK):
        keys = start + BLOCK
        cols = slice(start, keys)
        bias_t_ref[0:keys, :] = visibility(ids_col_ref, ids_row_ref, start, keys)

        def one_head(head, keys=keys, cols=cols):
            here = rows_at(head, HEAD_DIM)
            scores = dot(triple_ref[1, 0:keys, :], keep_head(q_t_ref[:, cols], head, 0))
            probs = jnp.exp(scores + bias_t_ref[0:keys, :] - mixed_t_ref[pl.ds(part + head, 1), cols])
            grad_probs = dot(triple_ref[2, 0:keys, :], keep_head(grad_t_ref[:, cols], head, 0))
            grad_scores = (probs * (grad_probs - delta_ref[pl.ds(head, 1), cols])).astype(BF16)
            grad_v_ref[0:keys, :] += dot(probs.astype(BF16), keep_head(grad_ref[cols, :], head, 1))
            grad_k_ref[0:keys, :] += dot(grad_scores, keep_head(triple_ref[0, cols, :], head, 1))
            grad_q_t_ref[here, cols] = dot(k_t_ref[here, 0:keys], grad_scores)

        each_head(heads, one_head, keys > LONG_BACKWARD)
    factor = HEAD_DIM**-0.5
    for start in range(0, rows, BLOCK):
        cols = slice(start, start + BLOCK)
        grad_triple_ref[0, cols, :] = (grad_q_t_ref[:, cols].T * factor).astype(BF16)
    grad_triple_ref[1] = grad_k_ref[...].astype(BF16)
    grad_triple_ref[2] = grad_v_ref[...].astype(BF16)
    for slot in range(4):
        here = rows_at(me ^ slot, local)
        target = near_ref if slot < 2 else far_ref
        target[slot % 2] = (
            dot(grad_triple_ref[0, here, :], weight_ref[0:part, :])
            + dot(grad_triple_ref[1, here, :], weight_ref[part : 2 * part, :])
            + dot(grad_triple_ref[2, here, :], weight_ref[2 * part : 3 * part, :])
        ).astype(BF16)


def attend_backward(place, grads, triple, mixed_t, tail, weight):
    _, rows, part = triple.shape
    width = weight.shape[1]
    heads = part // HEAD_DIM
    pair = shape((2, rows // 4, width), BF16)
    return call(
        attend_backward_kernel,
        [pair, pair, shape((3, rows, part), BF16)],
        place, *grads, triple, mixed_t, tail, weight,
        scratch=[
            pltpu.VMEM((rows, part), BF16),
            pltpu.VMEM((part, rows), BF16),
            pltpu.VMEM((heads, rows), F32),
            pltpu.VMEM((part, rows), F32),
            pltpu.VMEM((rows, part), F32),
            pltpu.VMEM((rows, part), F32),
            pltpu.VMEM((rows, BLOCK), F32),
            pltpu.VMEM((1, rows), F32),
            pltpu.VMEM((rows, 128), F32),
            pltpu.VMEM((part, rows), BF16),
            pltpu.VMEM((part, rows), BF16),
        ],
        vmem=16,
        name="attend_backward",
    )


def mixer_kernel(
    place_ref, m0_ref, m1_ref, m2_ref, m3_ref, x_ref, mixer_ref, vectors_ref, _later_ref,
    normed_ref, middle_ref, mixed_ref,
):
    me = place_ref[0]
    half, double = m0_ref.shape
    part = double // 2
    middle = x_ref[...].astype(F32) + vector(vectors_ref, MIXER_BIAS)
    for slot, packed_ref in enumerate((m0_ref, m1_ref, m2_ref, m3_ref)):
        cols = slice(slot * part, (slot + 1) * part)
        mixed_ref[0:half, cols] = packed_ref[:, 0:part]
        mixed_ref[half : 2 * half, cols] = packed_ref[:, part:double]
        middle += dot(mixed_ref[:, cols], mixer_ref[rows_at(me ^ slot, part), :])
    middle_ref[...] = middle
    unit, _ = unit_rows(middle)
    normed_ref[...] = (unit * vector(vectors_ref, BACK_GAIN) + vector(vectors_ref, BACK_SHIFT)).astype(BF16)


def mixer_part(place, packed, x, mixer, vectors, later):
    rows, width = x.shape
    return call(
        mixer_kernel,
        [shape((rows, width), BF16), shape((rows, width), F32), shape((rows, width), BF16)],
        place, *packed, x, mixer, vectors, later,
        name="mixer_part",
    )


def feed_kernel(
    place_ref, normed_own_ref, normed_other_ref, cot_own_ref, cot_other_ref, expand_ref, reduce_ref, vectors_ref,
    second_ref, grad_ref, send_ref, active_ref, grad_hidden_ref, bias_sum_ref,
    total_ref, back_ref,
):
    side = place_ref[1]
    rows = normed_own_ref.shape[0]
    chunk = active_ref.shape[1] // 4
    lane = lax.broadcasted_iota(jnp.int32, (1, 2 * chunk), 1) // chunk
    total_ref[...] = jnp.zeros_like(total_ref)
    back_ref[...] = jnp.zeros_like(back_ref)

    def one_chunk(index, carry):
        block = pl.ds(pl.multiple_of((2 * index + side) * chunk, 128), chunk)
        expand = expand_ref[:, block]
        reduce = reduce_ref[block, :]
        bias = vectors_ref[pl.ds(EXPAND_BIAS + index, 1), pl.ds(pl.multiple_of(side * chunk, 128), chunk)]
        sums = jnp.zeros((1, chunk), F32)
        for part, (normed_ref, cot_ref) in enumerate(((normed_own_ref, cot_own_ref), (normed_other_ref, cot_other_ref))):
            here = slice(part * rows, (part + 1) * rows)
            cols = pl.ds(pl.multiple_of(index * chunk, 128), chunk)
            hidden = dot(normed_ref[...], expand) + bias
            square = hidden * hidden
            bend = jnp.tanh(GELU_A * hidden * (1.0 + GELU_B * square))
            half = 0.5 * (1.0 + bend)
            active = (hidden * half).astype(BF16)
            active_ref[here, cols] = active
            total_ref[here, :] += dot(active, reduce)
            slope = half + (0.5 * GELU_A) * hidden * (1.0 - bend * bend) * (1.0 + (3.0 * GELU_B) * square)
            grad_hidden = (dot(cot_ref[...], reduce, NT) * slope).astype(BF16)
            grad_hidden_ref[here, cols] = grad_hidden
            sums += column_sum(grad_hidden.astype(F32))
            back_ref[here, :] += dot(grad_hidden, expand, NT)
        bias_sum_ref[pl.ds(index, 1), :] = jnp.where(lane == side, jnp.concatenate([sums, sums], axis=1), 0.0)
        return carry

    lax.fori_loop(0, 4, one_chunk, 0)
    second_ref[...] = total_ref[0:rows, :]
    grad_ref[...] = back_ref[0:rows, :]
    send_ref[0] = back_ref[rows : 2 * rows, :].astype(BF16)
    send_ref[1] = total_ref[rows : 2 * rows, :].astype(BF16)


def feed_part(place, normed_own, normed_other, cot_own, cot_other, expand, reduce, vectors):
    rows, width = normed_own.shape
    hidden = expand.shape[1]
    return call(
        feed_kernel,
        [
            shape((rows, width), F32),
            shape((rows, width), F32),
            shape((2, rows, width), BF16),
            shape((2 * rows, hidden // 2), BF16),
            shape((2 * rows, hidden // 2), BF16),
            shape((4, width), F32),
        ],
        place, normed_own, normed_other, cot_own, cot_other, expand, reduce, vectors,
        scratch=[
            pltpu.VMEM((2 * rows, width), F32),
            pltpu.VMEM((2 * rows, width), F32),
        ],
        vmem=16,
        name="feed_part",
    )


def joint_kernel(
    place_ref, grad_own_ref, recv_ref, middle_ref, cot_ref, mixer_ref, vectors_ref,
    grad_middle_ref, grad_low_ref, g0_ref, g1_ref, g2_ref, g3_ref,
):
    me = place_ref[0]
    half, double = g0_ref.shape
    part = double // 2
    grad_normed = grad_own_ref[...] + recv_ref[0].astype(F32)
    unit, scale = unit_rows(middle_ref[...])
    back = norm_pullback(grad_normed, unit, scale, vector(vectors_ref, BACK_GAIN))
    grad_middle = cot_ref[...].astype(F32) + back
    grad_middle_ref[...] = grad_middle
    grad_low = grad_middle.astype(BF16)
    grad_low_ref[...] = grad_low
    for slot, packed_ref in enumerate((g0_ref, g1_ref, g2_ref, g3_ref)):
        grad = dot(grad_low, mixer_ref[rows_at(me ^ slot, part), :], NT).astype(BF16)
        packed_ref[:, 0:part] = grad[0:half, :]
        packed_ref[:, part:double] = grad[half : 2 * half, :]


def joint_part(place, *arrays):
    rows, width = arrays[0].shape
    part = width // 4
    return call(
        joint_kernel,
        [shape((rows, width), F32), shape((rows, width), BF16)] + [shape((rows // 2, 2 * part), BF16)] * 4,
        place, *arrays,
        name="joint_part",
    )


def outer_kernel(
    place_ref, second_ref, grad_own_ref, recv_ref, middle_ref, cot_ref, grad_low_ref, mixed_ref,
    tail_ref, vectors_ref, bias_sum_ref,
    out_ref, sums_ref, mixer_send_ref, mixer_keep_ref,
    total_ref, ids_row_ref, ids_ref,
):
    me, side = place_ref[0], place_ref[1]
    rows = cot_ref.shape[0]
    cot = cot_ref[...].astype(F32)
    unit, _ = unit_rows(middle_ref[...])
    pass_ids_of(tail_ref, ids_row_ref, ids_ref)
    grad_normed = grad_own_ref[...] + recv_ref[0].astype(F32)
    sums_ref[...] = jnp.zeros_like(sums_ref)
    passes = lax.broadcasted_iota(jnp.int32, (rows, 128), 1).astype(F32)
    chosen = (ids_ref[rows_at(me, rows), :] == passes).astype(BF16)
    table = vectors_ref[TABLE : TABLE + 5, :]
    embedded = dot(chosen, jnp.concatenate([table, jnp.zeros((123, table.shape[1]), F32)], axis=0).astype(BF16))
    sums_ref[SUM_TABLE : SUM_TABLE + 5, :] = dot(chosen, cot_ref[...], TN)[0:5, :]
    second = second_ref[...] + recv_ref[1].astype(F32) + vector(vectors_ref, REDUCE_BIAS)
    out_ref[...] = (middle_ref[...] + second + embedded).astype(BF16)
    sums_ref[SUM_COT : SUM_COT + 1, :] = column_sum(cot)
    sums_ref[SUM_MIXER : SUM_MIXER + 1, :] = column_sum(grad_low_ref[...].astype(F32))
    sums_ref[SUM_GAIN : SUM_GAIN + 1, :] = column_sum(grad_normed * unit)
    sums_ref[SUM_SHIFT : SUM_SHIFT + 1, :] = column_sum(grad_normed)
    sums_ref[SUM_EXPAND : SUM_EXPAND + 4, :] = bias_sum_ref[...]
    block = mixer_send_ref.shape[1]
    total_ref[...] = dot(mixed_ref[...], grad_low_ref[...], TN).astype(BF16)
    for slot in range(4):
        mixer_keep_ref[me ^ slot] = total_ref[rows_at(2 * slot + side, block), :]
        mixer_send_ref[me ^ slot] = total_ref[rows_at(2 * slot + (1 - side), block), :]


def outer_part(place, *arrays, seq_rows):
    rows, width = arrays[0].shape
    part = shape((4, width // 8, width), BF16)
    return call(
        outer_kernel,
        [shape((rows, width), BF16), shape((16, width), F32), part, part],
        place, *arrays,
        scratch=[pltpu.VMEM((width, width), BF16), pltpu.VMEM((1, seq_rows), F32), pltpu.VMEM((seq_rows, 128), F32)],
        name="outer_part",
    )


def flip(index):
    return ((index & 1) << 1) | (index >> 1)


def quarter_at(slot, quarter, side):
    return quarter ^ jnp.where(side == 0, flip(slot), slot)


def transposed_rows(out_ref, own_ref, other_ref, spare_ref, places):
    rows, width = own_ref.shape
    part = width // 4
    spare_ref[:, 0:rows] = own_ref[...].T
    spare_ref[:, rows : 2 * rows] = other_ref[...].T
    for index, place in enumerate(places):
        out_ref[index * part : (index + 1) * part, :] = spare_ref[rows_at(place, part), :]


def reduce_grads_kernel(place_ref, cot_own_ref, cot_other_ref, active_ref, send_ref, keep_ref, cot_t_ref, spare_ref):
    side, quarter, me_n = place_ref[1], place_ref[2], place_ref[3]
    chunk = active_ref.shape[1] // 4
    part = send_ref.shape[2]
    transposed_rows(cot_t_ref, cot_own_ref, cot_other_ref, spare_ref, [me_n ^ flip(index) for index in range(4)])
    for base, target in ((0, keep_ref), (2, send_ref)):

        def one_slot(step, carry, base=base, target=target):
            cols = pl.ds(pl.multiple_of(quarter_at(base + step, quarter, side) * chunk, 128), chunk)
            reduce = dot(cot_t_ref[...], active_ref[:, cols]).astype(BF16)
            for index in range(4):
                target[step, index] = reduce[index * part : (index + 1) * part, :]
            return carry

        lax.fori_loop(0, 2, one_slot, 0)


def reduce_grads(place, cot_own, cot_other, active):
    rows, width = cot_own.shape
    out = shape((2, 4, width // 4, active.shape[1] // 4), BF16)
    return call(
        reduce_grads_kernel,
        [out, out],
        place, cot_own, cot_other, active,
        scratch=[pltpu.VMEM((width, 2 * rows), BF16), pltpu.VMEM((width, 2 * rows), BF16)],
        name="reduce_grads",
    )


def expand_grads_kernel(
    place_ref, normed_own_ref, normed_other_ref, grad_hidden_ref, mixer_keep_ref, mixer_recv_ref,
    send_ref, keep_ref,
    normed_t_ref, spare_ref,
):
    side, quarter, me_n = place_ref[1], place_ref[2], place_ref[3]
    width = normed_own_ref.shape[1]
    chunk = grad_hidden_ref.shape[1] // 4
    high = width // 4
    quarters = [quarter_at(slot, quarter, side) for slot in range(4)]
    transposed_rows(normed_t_ref, normed_own_ref, normed_other_ref, spare_ref, quarters)

    def one_chunk(index, carry):
        cols = pl.ds(pl.multiple_of((me_n ^ flip(index)) * chunk, 128), chunk)
        expand = dot(normed_t_ref[...], grad_hidden_ref[:, cols]).astype(BF16)
        for slot in range(4):
            target = keep_ref if slot < 2 else send_ref
            target[slot % 2, index, 0:high, :] = expand[slot * high : (slot + 1) * high, :]
        return carry

    lax.fori_loop(0, 4, one_chunk, 0)
    for base, target in ((0, keep_ref), (2, send_ref)):

        def one_slot(step, carry, base=base, target=target):
            place = quarter_at(base + step, quarter, side)
            mixer = (mixer_keep_ref[place].astype(F32) + mixer_recv_ref[place].astype(F32)).astype(BF16)
            block = mixer.shape[0] // 2
            for other in range(4):
                piece = mixer[:, other * high : (other + 1) * high]
                target[step, flip(other ^ me_n), high:, :] = jnp.concatenate(
                    [piece[0:block, :], piece[block : 2 * block, :]], axis=1
                )
            return carry

        lax.fori_loop(0, 2, one_slot, 0)


def expand_grads(place, normed_own, normed_other, grad_hidden, mixer_keep, mixer_recv):
    rows, width = normed_own.shape
    out = shape((2, 4, width // 4 + width // 16, grad_hidden.shape[1] // 4), BF16)
    return call(
        expand_grads_kernel,
        [out, out],
        place, normed_own, normed_other, grad_hidden, mixer_keep, mixer_recv,
        scratch=[pltpu.VMEM((width, 2 * rows), BF16), pltpu.VMEM((width, 2 * rows), BF16)],
        name="expand_grads",
    )


def triple_grads_kernel(
    place_ref, x0_ref, x1_ref, x2_ref, x3_ref, near_ref, far_ref, normed_ref, grad_triple_ref, sums_in_ref,
    t0_ref, t1_ref, t2_ref, t3_ref, packet_ref, sums_ref,
    weight_ref,
):
    me, corner = place_ref[0], place_ref[7]
    rows, width = normed_ref.shape
    part = grad_triple_ref.shape[2]
    def sum_block(step, sums):
        here = rows_at(step, 64)
        gain_sum, shift_sum = sums
        for slot, x_ref in enumerate((x0_ref, x1_ref, x2_ref, x3_ref)):
            unit, _ = unit_rows(x_ref[here, :].astype(F32))
            grad = (near_ref if slot < 2 else far_ref)[slot % 2, here, :].astype(F32)
            gain_sum += (grad * unit).reshape(8, 8, width).sum(axis=0)
            shift_sum += grad.reshape(8, 8, width).sum(axis=0)
        return gain_sum, shift_sum

    gain_sum, shift_sum = lax.fori_loop(
        0, rows // 256, sum_block, (jnp.zeros((8, width), F32), jnp.zeros((8, width), F32))
    )
    gain_sum, shift_sum = column_sum(gain_sum), column_sum(shift_sum)
    sums_ref[0:16, :] = sums_in_ref[...]
    sums_ref[16:24, :] = jnp.zeros((8, width), F32)
    sums_ref[SUM_FRONT_GAIN : SUM_FRONT_GAIN + 1, :] = gain_sum
    sums_ref[SUM_FRONT_SHIFT : SUM_FRONT_SHIFT + 1, :] = shift_sum
    group = lax.broadcasted_iota(jnp.int32, (1, width), 1) // part
    for row, index in ((0, 0), (1, 2)):
        bias = column_sum(grad_triple_ref[index].astype(F32))
        sums_ref[SUM_TRIPLE + row : SUM_TRIPLE + row + 1, :] = jnp.where(
            group == me, jnp.concatenate([bias] * (width // part), axis=1), 0.0
        )
    for index in range(3):
        weight_ref[index * part : (index + 1) * part, :] = dot(grad_triple_ref[index], normed_ref[...], TN).astype(BF16)
    piece = 3 * part // 4
    for slot, target in enumerate((t0_ref, t1_ref, t2_ref, t3_ref)):
        target[...] = weight_ref[rows_at(corner ^ slot, piece), :]
    local = far_ref.shape[1]
    packet_ref[0:local, :] = far_ref[0]
    packet_ref[local : 2 * local, :] = far_ref[1]
    put_sums(packet_ref, 2 * local, sums_ref[...])


def triple_grads(place, shards, near, far, normed, grad_triple, sums):
    rows, width = normed.shape
    part = grad_triple.shape[2]
    return call(
        triple_grads_kernel,
        [shape((3 * part // 4, width), BF16)] * 4
        + [shape((rows // 2 + 2 * SUMS, width), BF16), shape((SUMS, width), F32)],
        place, *shards, near, far, normed, grad_triple, sums,
        scratch=[pltpu.VMEM((3 * part, width), BF16)],
        vmem=16,
        name="triple_grads",
    )


def pair_kernel(place_ref, near_ref, sent_ref, recv_ref, packet_ref, own_ref):
    local = near_ref.shape[1]
    own_ref[...] = near_ref[0].astype(F32) + recv_ref[0:local, :].astype(F32)
    packet_ref[0:local, :] = (near_ref[1].astype(F32) + recv_ref[local : 2 * local, :].astype(F32)).astype(BF16)
    put_sums(packet_ref, local, get_sums(sent_ref, 2 * local) + get_sums(recv_ref, 2 * local))


def pair_part(place, near, sent, recv):
    _, local, width = near.shape
    return call(
        pair_kernel,
        [shape((local + 2 * SUMS, width), BF16), shape((local, width), F32)],
        place, near, sent, recv,
        name="pair_part",
    )


def home_kernel(place_ref, t0_ref, t1_ref, t2_ref, t3_ref, sent_ref, recv_ref, packet_ref):
    piece = t0_ref.shape[0]
    local = sent_ref.shape[0] - 2 * SUMS
    total = t0_ref[...].astype(F32) + t1_ref[...].astype(F32) + t2_ref[...].astype(F32) + t3_ref[...].astype(F32)
    packet_ref[0:piece, :] = total.astype(BF16)
    put_sums(packet_ref, piece, get_sums(sent_ref, local) + get_sums(recv_ref, local))


def home_part(place, pieces, sent, recv):
    piece, width = pieces[0].shape
    return call(
        home_kernel, [shape((piece + 2 * SUMS, width), BF16)], place, *pieces, sent, recv, name="home_part"
    )[0]


def front_kernel(place_ref, x_ref, own_ref, recv_ref, grad_middle_ref, vectors_ref, out_ref):
    unit, scale = unit_rows(x_ref[...].astype(F32))
    grad = own_ref[...] + recv_ref[0 : own_ref.shape[0], :].astype(F32)
    back = norm_pullback(grad, unit, scale, vector(vectors_ref, FRONT_GAIN))
    out_ref[...] = (grad_middle_ref[...] + back).astype(BF16)


def front_part(place, x, *arrays):
    return call(front_kernel, [shape(x.shape, BF16)], place, x, *arrays, name="front_part")[0]


def spread_kernel(place_ref, sent_ref, recv_ref, packet_ref):
    piece = sent_ref.shape[0] - 2 * SUMS
    packet_ref[0:piece, :] = (sent_ref[0:piece, :].astype(F32) + recv_ref[0:piece, :].astype(F32)).astype(BF16)
    put_sums(packet_ref, piece, get_sums(sent_ref, piece) + get_sums(recv_ref, piece))


def spread_part(place, sent, recv):
    return call(spread_kernel, [shape(sent.shape, BF16)], place, sent, recv, name="spread_part")[0]


def last_kernel(place_ref, s0_ref, s1_ref, s2_ref, s3_ref, a_ref, b_ref, c_ref, packet_ref, total_ref):
    side, corner = place_ref[1], place_ref[7]
    piece = s0_ref.shape[0] - 2 * SUMS
    for slot, ref in enumerate((s0_ref, s1_ref, s2_ref, s3_ref)):
        packet_ref[rows_at(corner ^ slot, piece), :] = ref[0:piece, :]
    put_sums(
        packet_ref,
        4 * piece,
        (get_sums(s0_ref, piece) + get_sums(s1_ref, piece)) + (get_sums(s2_ref, piece) + get_sums(s3_ref, piece)),
    )
    total_ref[...] = a_ref[0].astype(F32) + b_ref[0].astype(F32) + c_ref[...].astype(F32)
    half = (packet_ref.shape[0] - 4 * piece - 2 * SUMS)
    chunk = total_ref.shape[1]
    start = 4 * piece + 2 * SUMS
    packet_ref[start:, 0:chunk] = total_ref[rows_at(2 * (1 - side), half), :].astype(BF16)
    packet_ref[start:, chunk : 2 * chunk] = total_ref[rows_at(2 * (1 - side) + 1, half), :].astype(BF16)


def last_part(place, packets, a, b, c):
    rows, width = packets[0].shape
    piece = rows - 2 * SUMS
    block = width // 8
    return call(
        last_kernel,
        [shape((4 * piece + 2 * SUMS + block // 2, width), BF16), shape(c.shape, F32)],
        place, *packets, a, b, c,
        name="last_part",
    )


def results_kernel(
    place_ref, sent_ref, recv_ref, total_ref,
    triple_ref, expand_ref, mixer_ref, triple_bias_ref, table_ref,
    front_gain_ref, front_shift_ref, mixer_bias_ref, back_gain_ref, back_shift_ref, expand_bias_ref, reduce_bias_ref,
    sums_ref,
):
    side, me_n, stay = place_ref[1], place_ref[3], place_ref[5]
    weights, width = triple_ref.shape
    part = mixer_ref.shape[1]

    @pl.when(stay == 1)
    def _():
        triple_ref[...] = sent_ref[0:weights, :].astype(F32)
        sums_ref[...] = get_sums(sent_ref, weights)

    @pl.when(stay == 0)
    def _():
        triple_ref[...] = recv_ref[0:weights, :].astype(F32)
        sums_ref[...] = get_sums(recv_ref, weights)

    block, double = expand_ref.shape
    chunk, half = double // 2, block // 2
    start = weights + 2 * SUMS
    for index in range(2):
        mine = total_ref[rows_at(2 * side + index, half), :]
        other = recv_ref[start:, index * chunk : (index + 1) * chunk].astype(F32)
        first = jnp.full(mine.shape, side, jnp.int32) == 0
        here = slice(index * half, (index + 1) * half)
        expand_ref[here, 0:chunk] = jnp.where(first, mine, other)
        expand_ref[here, chunk:double] = jnp.where(first, other, mine)
        mixer_ref[here, :] = total_ref[2 * block :, index * part : (index + 1) * part]
    pair = sums_ref[SUM_TRIPLE : SUM_TRIPLE + 2, :]
    bias = jnp.zeros((2, part), F32)
    for group in range(width // part):
        mine = jnp.full(bias.shape, me_n, jnp.int32) == group
        bias = jnp.where(mine, pair[:, group * part : (group + 1) * part], bias)
    triple_bias_ref[...] = bias
    table_ref[...] = sums_ref[SUM_TABLE : SUM_TABLE + table_ref.shape[0], :]
    for index, ref in (
        (SUM_FRONT_GAIN, front_gain_ref), (SUM_FRONT_SHIFT, front_shift_ref), (SUM_MIXER, mixer_bias_ref),
        (SUM_GAIN, back_gain_ref), (SUM_SHIFT, back_shift_ref), (SUM_COT, reduce_bias_ref),
    ):
        ref[...] = sums_ref[index : index + 1, :].reshape(width)
    for index in range(4):
        expand_bias_ref[index * width : (index + 1) * width] = (
            sums_ref[SUM_EXPAND + index : SUM_EXPAND + index + 1, :].reshape(width)
        )


def early_results_kernel(place_ref, ra_ref, rb_ref, rc_ref, layer_ref, rows_ref, reduce_ref, layer_out_ref, rows_out_ref):
    reduce_ref[...] = ra_ref[0].astype(F32) + rb_ref[0].astype(F32) + rc_ref[...].astype(F32)
    layer_out_ref[...] = layer_ref[...]
    rows_out_ref[...] = rows_ref[...]


def early_results(place, ra, rb, rc, layer, rows):
    return call(
        early_results_kernel,
        [shape(rc.shape, F32), shape(layer.shape, BF16), shape(rows.shape, BF16)],
        place, ra, rb, rc, layer, rows,
        name="early_results",
    )


def results(place, sent, recv, total, passes):
    width = sent.shape[1]
    block = width // 8
    piece = (sent.shape[0] - 2 * SUMS - block // 2) // 4
    row = shape((width,), F32)
    return call(
        results_kernel,
        [
            shape((4 * piece, width), F32), shape((block, width), F32), shape((block, width // 4), F32),
            shape((2, width // 4), F32), shape((passes, width), F32),
            row, row, row, row, row, shape((4 * width,), F32), row,
        ],
        place, sent, recv, total,
        scratch=[pltpu.VMEM((SUMS, width), F32)],
        name="results",
    )


def after(value, *earlier):
    return lax.optimization_barrier((value, earlier))[0]


def body(
    inputs,
    pass_ids,
    front_gain,
    front_shift,
    triple_weight,
    triple_bias,
    mixer_weight,
    mixer_bias,
    back_gain,
    back_shift,
    expand_weight,
    expand_bias,
    reduce_weight,
    reduce_bias,
    pass_table,
    cotangent,
):
    width = inputs.shape[1]
    part = triple_weight.shape[2]
    wide_size, narrow_size = lax.axis_size("wide"), lax.axis_size("narrow")
    low_bits = wide_size.bit_length() - 4
    side_bit, x_bit, y_bit = 1 << low_bits, 2 << low_bits, 4 << low_bits

    wide, narrow = lax.axis_index("wide"), lax.axis_index("narrow")
    c, h, l = wide & 1, narrow >> 1, narrow & 1
    me = 2 * c + l
    top = wide >> low_bits
    side, quarter = top & 1, top >> 1
    x1, y1 = (wide >> 1) & 1, (wide >> 2) & 1
    stay = (c == h).astype(jnp.int32)
    corner = 2 * y1 + x1
    place = jnp.stack(
        [
            me, side, quarter, narrow,
            jnp.where(c == 0, 2 * x1 + y1, corner),
            stay,
            jnp.where(h == 0, 2 * x1 + y1, corner),
            corner,
        ]
    ).astype(jnp.int32)

    def send(name, value, target):
        pairs = []
        for w in range(wide_size):
            for n in range(narrow_size):
                to = target(w, n)
                if to is not None:
                    pairs.append((w * narrow_size + n, to[0] * narrow_size + to[1]))
        with jax.named_scope(name):
            return lax.ppermute(value, AXES, pairs)

    def stays(w, n):
        return (w & 1) == (n >> 1)

    def moved(w, n):
        return (w, n) if stays(w, n) else (w ^ 1, n ^ 2)

    def home(w, n):
        return None if stays(w, n) else (w, n ^ 2)

    def lend(w, n):
        return (w, n ^ 2) if stays(w, n) else None

    def core(w, n):
        return (w ^ 1, n)

    def pair(w, n):
        return (w, n ^ 1)

    def diagonal(w, n):
        return (w ^ 1, n ^ 1)

    def across(w, n):
        return (w, n ^ 2)

    def sided(w, n):
        return (w ^ side_bit, n)

    def first(w, n):
        return (w ^ (y_bit if w & side_bit else x_bit), n)

    def second(w, n):
        return (w ^ (x_bit if w & side_bit else y_bit), n)

    def step_x(w, n):
        return (w ^ 2, n)

    def step_y(w, n):
        return (w ^ 4, n)

    def step_xy(w, n):
        return (w ^ 6, n)

    def of_stay(target):
        return lambda w, n: target(w, n) if stays(w, n) else None

    def of_moved(target):
        return lambda w, n: None if stays(w, n) else target(w, n)

    def add(*terms):
        return sum(t.astype(F32) for t in terms).astype(BF16)

    together = lax.optimization_barrier

    weight_t = jnp.swapaxes(triple_weight, 1, 2).reshape(3 * part, width)
    piece = 3 * part // 4
    lent = lax.dynamic_slice_in_dim(weight_t, corner * piece, piece)
    place, lent = together((place, lent))
    p0 = send("lend_weight", lent, lend)
    x0 = send("rows_move", inputs, moved)
    x1_stay = send("rows_pair", inputs, of_stay(pair))
    vectors, tail = gather_vectors(
        place, triple_bias, pass_ids,
        front_gain, front_shift, mixer_bias, back_gain, back_shift, reduce_bias, expand_bias, pass_table,
    )
    tail = send("tail_move", tail, moved)
    x0, p0, x1_stay, vectors, tail = together((x0, p0, x1_stay, vectors, tail))
    x1_moved = send("rows_pair", x0, of_moved(pair))
    p1, p2, p3 = (send("lent", p0, of_moved(step)) for step in (step_x, step_y, step_xy))
    x1_moved, p1, p2, p3 = together((x1_moved, p1, p2, p3))
    x1_rows = jnp.where(stay == 1, x1_stay, x1_moved)
    x2 = send("rows_core", x0, core)
    x3 = send("pair_core", x1_rows, core)
    cot_own = send("cot_move", after(cotangent, x1_rows), moved)

    shards = (x0, x1_rows, x2, x3)
    m0, m1, m2, m3, mixed_t, normed, triple, weight = attend_forward(
        place, shards, tail, vectors, weight_t, (p0, p1, p2, p3)
    )
    m1, m2, m3, cot_own = together(
        (send("m_pair", m1, pair), send("m_core", m2, core), send("m_diagonal", m3, diagonal), cot_own)
    )
    cot_other = send("cot_core", cot_own, sided)
    normed_two, middle, mixed_rows = mixer_part(place, (m0, m1, m2, m3), x0, mixer_weight, vectors, reduce_weight)
    normed_other, cot_other = together((send("normed_core", normed_two, sided), cot_other))
    second_own, grad_own, feed_send, active, grad_hidden, bias_sums = feed_part(
        place, normed_two, normed_other, cot_own, cot_other, expand_weight, reduce_weight, vectors
    )
    feed_recv = send("feed_core", feed_send, sided)
    reduce_send, reduce_keep = reduce_grads(place, cot_own, cot_other, active)
    grad_own, feed_recv, reduce_send = together((grad_own, feed_recv, reduce_send))
    reduce_first = send("reduce_first", reduce_send, first)
    grad_middle, grad_low, g0, g1, g2, g3 = joint_part(
        place, grad_own, feed_recv, middle, cot_own, mixer_weight, vectors
    )
    g1, g2, g3 = send("g_pair", g1, pair), send("g_core", g2, core), send("g_diagonal", g3, diagonal)
    out_rows, sums, mixer_send, mixer_keep = outer_part(
        place, second_own, grad_own, feed_recv, middle, cot_own, grad_low, mixed_rows, tail, vectors, bias_sums,
        seq_rows=pass_ids.shape[1],
    )
    mixer_recv = send("mixer_core", mixer_send, sided)
    expand_send, expand_keep = expand_grads(
        place, normed_two, normed_other, grad_hidden, mixer_keep, mixer_recv
    )
    g1, g2, g3, expand_send, expand_keep, out_rows, reduce_first = together(
        (g1, g2, g3, expand_send, expand_keep, out_rows, reduce_first)
    )
    reduce_second = send("reduce_second", add(reduce_keep[1], reduce_first[1]), second)
    expand_first = send("expand_first", expand_send, first)
    layer_out = send("out_move", out_rows, moved)
    near, far, grad_triple_rows = attend_backward(
        place, (g0, g1, g2, g3), triple, mixed_t, tail, weight
    )

    def halved(keep, first_recv, second_recv):
        return (
            add(keep[0, 0:2], first_recv[0, 0:2], second_recv[0:2]),
            add(keep[0, 2:4], first_recv[0, 2:4], second_recv[2:4]),
        )

    far, near, grad_triple_rows, reduce_second, layer_out = together(
        (far, near, grad_triple_rows, reduce_second, layer_out)
    )
    reduce_a, reduce_b = halved(reduce_keep, reduce_first, reduce_second)
    reduce_pair = send("reduce_pair", reduce_b, pair)
    t0, t1, t2, t3, core_packet, all_sums = triple_grads(place, shards, near, far, normed, grad_triple_rows, sums)
    core_packet = after(core_packet, reduce_pair)
    core_recv, expand_first = together((send("far_core", core_packet, core), expand_first))

    pair_packet, own_rows = pair_part(place, near, core_packet, core_recv)
    pair_recv = send("near_pair", pair_packet, pair)
    t1, t2, t3 = send("triple_x", t1, step_x), send("triple_y", t2, step_y), send("triple_xy", t3, step_xy)
    expand_second = send("expand_second", add(expand_keep[1], expand_first[1]), second)
    reduce_across = send("reduce_across", add(reduce_a[1], reduce_pair[1]), across)
    t1, t2, t3, pair_recv, expand_second, reduce_across = together(
        (t1, t2, t3, pair_recv, expand_second, reduce_across)
    )

    home_packet = home_part(place, (t0, t1, t2, t3), pair_packet, pair_recv)
    home_recv = send("triple_home", home_packet, home)
    grad_rows = front_part(place, x0, own_rows, pair_recv, grad_middle, vectors)
    grad_inputs = send("rows_home", grad_rows, moved)
    expand_a, expand_b = halved(expand_keep, expand_first, expand_second)
    expand_pair = send("expand_pair", expand_b, pair)
    home_recv, expand_pair, grad_rows = together((home_recv, expand_pair, grad_rows))

    spread = spread_part(place, home_packet, home_recv)
    s1, s2, s3 = (send("triple_spread", spread, of_stay(step)) for step in (step_x, step_y, step_xy))
    expand_across = send("expand_across", add(expand_a[1], expand_pair[1]), across)
    s1, s2, s3, expand_across, grad_inputs = together((s1, s2, s3, expand_across, grad_inputs))

    last_packet, total = last_part(place, (spread, s1, s2, s3), expand_a, expand_pair, expand_across)
    last_recv = send("last_core", last_packet, core)
    total_reduce, layer_out, grad_inputs = early_results(
        place, reduce_a, reduce_pair, after(reduce_across, last_packet), layer_out, grad_inputs
    )
    last_recv, total_reduce, layer_out, grad_inputs = together((last_recv, total_reduce, layer_out, grad_inputs))
    (
        grad_triple, total_expand, total_mixer, grad_triple_bias, grad_table,
        grad_front_gain, grad_front_shift, grad_mixer_bias, grad_back_gain, grad_back_shift, grad_expand_bias,
        grad_reduce_bias,
    ) = results(place, last_packet, last_recv, total, pass_table.shape[0])
    grad_triple = jnp.swapaxes(grad_triple.reshape(3, part, width), 1, 2)
    if low_bits:
        size = 1 << low_bits
        peers = [[size * i + j for j in range(size)] for i in range(wide_size // size)]
        total_expand, total_reduce, total_mixer = (
            lax.psum_scatter(t, "wide", scatter_dimension=d, axis_index_groups=peers, tiled=True)
            for t, d in ((total_expand, 0), (total_reduce, 1), (total_mixer, 0))
        )
        peers = [[i + 8 * j for j in range(wide_size // 8)] for i in range(8)]
        (
            grad_triple, grad_triple_bias, grad_table, grad_front_gain, grad_front_shift, grad_mixer_bias,
            grad_back_gain, grad_back_shift, grad_expand_bias, grad_reduce_bias,
        ) = lax.psum(
            (
                grad_triple, grad_triple_bias, grad_table, grad_front_gain, grad_front_shift, grad_mixer_bias,
                grad_back_gain, grad_back_shift, grad_expand_bias, grad_reduce_bias,
            ),
            "wide", axis_index_groups=peers,
        )
    return (
        layer_out,
        grad_inputs,
        grad_front_gain,
        grad_front_shift,
        grad_triple,
        grad_triple_bias,
        total_mixer,
        grad_mixer_bias,
        grad_back_gain,
        grad_back_shift,
        total_expand,
        grad_expand_bias,
        total_reduce.T,
        grad_reduce_bias,
        grad_table,
    )


def solution(mesh):
    rows = P(AXES, None)
    block = P("wide", "narrow")
    return jax.shard_map(
        body,
        mesh=mesh,
        in_specs=(
            rows, P("wide", None), P(), P(), P(None, None, "narrow"), P(None, "narrow"),
            P(), P(), P(), P(), P(), P(), P(), P(), P(), rows,
        ),
        out_specs=(
            rows, rows, P(), P(), P(None, None, "narrow"), P(None, "narrow"), block,
            P(), P(), P(), block, P(), block, P(), P(),
        ),
        check_vma=False,
    )
```
